32 devices in a mesh: groups: 2 (over y), band: 4 (over z), wt: 4 (over x, core).
Axes of the slice: x: 2, y: 2, z: 4, core: 2. Of those that a mesh axis runs over, the one named last changes fastest.
Arguments:
- prior_state: float32 [128, 16, 1024], P('groups', 'band', 'wt'), parts along dimension 0, may hold values from -6 to 6
- langevin_noise: float32 [4, 128, 16, 1024], P(None, 'groups', 'band', 'wt'), parts along dimension 1, may hold values from -6 to 6
- station_values: float32 [8192], P(('groups', 'band', 'wt')), parts along dimension 0, may hold values from -6 to 6
- entry_cell: int32 [8192], P(('groups', 'band', 'wt')), parts along dimension 0, may hold values from 0 to 65535
- entry_owner: int32 [8192], P(('groups', 'band', 'wt')), parts along dimension 0, may hold values from 0 to 3, as said below
- entry_slot: int32 [8192], P(('groups', 'band', 'wt')), parts along dimension 0, may hold values from 0 to 255
- entry_weight: float32 [8192], P(('groups', 'band', 'wt')), parts along dimension 0, may hold values from 0.25 to 1
- live_counts: int32 [32], P(('groups', 'band', 'wt')), parts along dimension 0, may hold values from 64 to 256, as said below
- lift_weight: bfloat16 [64, 256], replicated, may hold values from -0.75 to 0.75
- conv_weight: bfloat16 [9, 256, 256], replicated, may hold values from -0.125 to 0.125
- head_weight: bfloat16 [256, 64], replicated, may hold values from -0.375 to 0.375
- first_gain: float32 [256], replicated, may hold values from 0.1 to 1.9
- second_gain: float32 [256], replicated, may hold values from 0.1 to 1.9
Outputs:
- analysis_state: float32 [128, 16, 1024], P('groups', 'band', 'wt'), parts along dimension 0
- innovation: float32 [8192], P(('groups', 'band', 'wt')), parts along dimension 0
The draws below stay inside these ranges and needn't reach their ends.
There are 2 independent parts, one for each index of `groups`. The reference program is written for one: setup_inputs(seed, part) draws one part's arguments, and reference() takes and returns one part's arrays. A program takes and returns all parts, laid end to end along the dimension named above; an argument that names none is the same for every part. Nothing has to cross between parts.
Inputs may be any that keep to these rules, and one draw needn't show every extreme that they name: `entry_owner`: an entry's owner band lies within 2 bands of the entry's own band; every list holds an entry at offset +2 and one at -2, clipped to the existing bands. `live_counts`: some list is full in every draw.
All inputs are finite; a program needn't handle non-finite values.
Results may differ from the reference program's by a relative error of at most 0.0014.
Values may be sent and summed in bfloat16 or wider, within the bound.
No kernel may reach another device: no remote copies, remote signals or barrier semaphores. Data moves between devices by JAX's collectives and lax.ppermute only.
A program may use at most 64 MiB of HBM per device.

```python
import math
import jax
import jax.numpy as jnp
from jax import lax

VARS = 64
CHAN = 256
LATB = 4
LOND = 256
S_DEV = 256
ENT = 256
REACH = 2
NLAT = 16
NLON = 1024
NSTAT = 4096
ENTRIES = 4096
N_BAND = 4
N_WT = 4


def draw_entry_owner(key, part):
    total = ENT * N_BAND * N_WT
    position = jnp.arange(total, dtype=jnp.int32)
    band_of = position // ENT // N_WT
    offset = jax.random.randint(jax.random.fold_in(key, 11), (total,), -REACH, REACH + 1)
    within = position % ENT
    offset = jnp.where(within == 0, REACH, jnp.where(within == 1, -REACH, offset))
    return jnp.clip(band_of + offset, 0, N_BAND - 1).astype(jnp.int32)


def draw_live_counts(key, part):
    lists = N_BAND * N_WT
    counts = jax.random.randint(jax.random.fold_in(key, 21), (lists,), ENT // 4, ENT + 1)
    fullest = jax.random.randint(jax.random.fold_in(key, 22), (), 0, lists)
    return jnp.where(jnp.arange(lists, dtype=jnp.int32) == fullest, ENT, counts).astype(jnp.int32)


def place_ends(values, own_key, low, top_value):
    dims = values.shape
    index_at = [jax.random.randint(jax.random.fold_in(own_key, axis), (), 0, dims[axis]) for axis in range(len(dims))]
    values = values.at[tuple(index_at)].set(low)
    longest = dims.index(max(dims))
    index_at[longest] = (index_at[longest] + 1) % dims[longest]
    return values.at[tuple(index_at)].set(top_value)


def levels(key, extent, shards, low, high):
    level = 1.0
    for dim, blocks in shards:
        heights = jax.random.uniform(jax.random.fold_in(jax.random.fold_in(key, 6), dim), (blocks,), jnp.float32, low / len(shards), high / len(shards))
        level = level * jnp.repeat(jnp.exp(heights), extent[dim] // blocks).reshape((-1,) + (1,) * (len(extent) - 1 - dim))
    return level


def noise(own_key, extent, width, bound, split=(), kind=jnp.bfloat16):
    drawn = width * jax.random.normal(own_key, extent, jnp.float32)
    if split:
        drawn = drawn * levels(own_key, extent, split, -0.22, 0.18)
    return jnp.clip(drawn, -bound, bound).astype(kind)


def setup_inputs(seed: int = 0, part: int = 0) -> dict:
    streams_of = jax.random.split(jax.random.key(seed), 14)
    own_keys = jax.random.split(jax.random.fold_in(streams_of[13], part), 14)
    return {
        "prior_state": noise(own_keys[0], (VARS, NLAT, NLON), 1.0, 6.0, ((1, 4), (2, 4)), jnp.float32),
        "langevin_noise": noise(own_keys[1], (4, VARS, NLAT, NLON), 1.0, 6.0, ((2, 4), (3, 4)), jnp.float32),
        "station_values": noise(own_keys[2], (NSTAT,), 1.0, 6.0, ((0, 16),), jnp.float32),
        "entry_cell": place_ends(jax.random.randint(own_keys[3], (ENTRIES,), 0, VARS * LATB * LOND), jax.random.fold_in(own_keys[3], 1), 0, (VARS * LATB * LOND) - 1).astype(jnp.int32),
        "entry_owner": draw_entry_owner(jax.random.fold_in(jax.random.fold_in(streams_of[13], part), 71), part),
        "entry_slot": place_ends(jax.random.randint(own_keys[5], (ENTRIES,), 0, S_DEV), jax.random.fold_in(own_keys[5], 1), 0, S_DEV - 1).astype(jnp.int32),
        "entry_weight": jnp.clip(0.25 + 0.75 * jax.random.uniform(own_keys[6], (ENTRIES,), jnp.float32) ** levels(own_keys[6], (ENTRIES,), ((0, 16),), -0.2, 0.2), 0.25, 1.0),
        "live_counts": draw_live_counts(jax.random.fold_in(jax.random.fold_in(streams_of[13], part), 71), part),
        "lift_weight": noise(streams_of[8], (VARS, CHAN), VARS ** -0.5, 0.75),
        "conv_weight": noise(streams_of[9], (9, CHAN, CHAN), (9 * CHAN) ** -0.5, 0.125),
        "head_weight": noise(streams_of[10], (CHAN, VARS), CHAN ** -0.5, 0.375),
        "first_gain": jnp.clip(1.0 + 0.18 * jax.random.normal(streams_of[11], (CHAN,), jnp.float32), 0.1, 1.9),
        "second_gain": jnp.clip(1.0 + 0.18 * jax.random.normal(streams_of[12], (CHAN,), jnp.float32), 0.1, 1.9),
    }


noise_levels = (1.0, 0.6, 0.3)
obs_precision = 4.0
step_factor = 0.1

def rms_scale(values, gain):
    power = lax.optimization_barrier(jnp.mean(values * values, axis=0, keepdims=True))
    return values * lax.rsqrt(power + 1e-06) * gain[:, None, None]

def conv_global(hidden, conv_weight):
    padded = jnp.pad(hidden, ((0, 0), (1, 1), (0, 0)))
    padded = jnp.concatenate([padded[:, :, -1:], padded, padded[:, :, :1]], axis=2)
    total = jnp.zeros((conv_weight.shape[2], NLAT, NLON), jnp.float32)
    for tap_index in range(9):
        row_shift, col_shift = divmod(tap_index, 3)
        window = padded[:, row_shift:row_shift + NLAT, col_shift:col_shift + NLON].astype(jnp.float32)
        total = total + jnp.einsum('co,chw->ohw', conv_weight[tap_index].astype(jnp.float32), window)
    return total

def reference(prior_state, langevin_noise, station_values, entry_cell, entry_owner, entry_slot, entry_weight, live_counts, lift_weight, conv_weight, head_weight, first_gain, second_gain):
    position = jnp.arange(ENTRIES, dtype=jnp.int32)
    listed = position // ENT
    band_of = listed // N_WT
    sector = listed % N_WT
    alive = position % ENT < live_counts[listed]
    weights = jnp.where(alive, entry_weight, jnp.float32(0.0))
    variable = entry_cell // (LATB * LOND)
    remain = entry_cell % (LATB * LOND)
    rowpos = band_of * LATB + remain // LOND
    colpos = sector * LOND + remain % LOND
    flat_cell = (variable * NLAT * NLON + rowpos * NLON + colpos).astype(jnp.int32)
    station = ((entry_owner * N_WT + sector) * S_DEV + entry_slot).astype(jnp.int32)

    def evaluate(current, level):
        scaled = (current / math.sqrt(1.0 + level * level)).astype(jnp.bfloat16)
        lifted = jnp.einsum('vo,vhw->ohw', lift_weight.astype(jnp.float32), scaled.astype(jnp.float32))
        first = jax.nn.silu(rms_scale(lifted, first_gain)).astype(jnp.bfloat16)
        mixed = lifted + conv_global(first, conv_weight)
        second = jax.nn.silu(rms_scale(mixed, second_gain)).astype(jnp.bfloat16)
        score = jnp.einsum('co,chw->ohw', head_weight.astype(jnp.float32), second.astype(jnp.float32)) / level
        values = weights * current.reshape(-1)[flat_cell]
        interp = jnp.zeros((NSTAT,), jnp.float32).at[station].add(values)
        innov = station_values - interp
        adjoint = jnp.zeros((VARS * NLAT * NLON,), jnp.float32).at[flat_cell].add(weights * innov[station])
        return (score + obs_precision * adjoint.reshape(current.shape), innov)
    current = prior_state
    innov = station_values
    for section in range(2):
        upper = noise_levels[section]
        lower = noise_levels[section + 1]
        spread = upper * upper - lower * lower
        drift, innov = evaluate(current, upper)
        current = current + spread * drift + math.sqrt(spread) * langevin_noise[2 * section]
        factor = step_factor * lower * lower
        drift, innov = evaluate(current, lower)
        current = current + factor * drift + math.sqrt(2.0 * factor) * langevin_noise[2 * section + 1]
    return (current, innov)
```

```python
import functools
import math

import jax
import jax.numpy as jnp
from jax import lax
from jax.experimental import pallas as pl
from jax.experimental.pallas import tpu as pltpu
from jax.sharding import PartitionSpec as P

F32 = jnp.float32
BF16 = jnp.bfloat16
REACH = 2
HALO = 4
LANES = 128
HALF = 64

noise_levels = (1.0, 0.6, 0.3)
obs_precision = 4.0
step_factor = 0.1


def sub_steps():
    steps = []
    for section in range(2):
        upper, lower = noise_levels[section], noise_levels[section + 1]
        spread = upper * upper - lower * lower
        steps.append((upper, spread, math.sqrt(spread)))
        factor = step_factor * lower * lower
        steps.append((lower, factor, math.sqrt(2.0 * factor)))
    return steps


STEPS = sub_steps()


def shrink(level):
    return 1.0 / math.sqrt(1.0 + level * level)


def vmem_call(kernel, outs, *args, scratch=()):
    args = [pltpu.with_memory_space_constraint(a, pltpu.VMEM) for a in args]
    spec = pl.BlockSpec(memory_space=pltpu.VMEM)
    return pl.pallas_call(
        kernel,
        out_shape=[pltpu.VMEM(shape, dtype) for shape, dtype in outs],
        in_specs=[spec] * len(args),
        out_specs=[spec] * len(outs),
        scratch_shapes=list(scratch),
        compiler_params=pltpu.CompilerParams(vmem_limit_bytes=48 * 2**20),
    )(*args)


def dot(a, b, ca=1, cb=0):
    return lax.dot_general(a, b, (((ca,), (cb,)), ((), ())), preferred_element_type=F32)


def pieces(x, count):
    out = []
    for _ in range(count):
        part = x.astype(BF16)
        out.append(part)
        x = x - part.astype(F32)
    return out


def iota(shape, dim):
    return lax.broadcasted_iota(jnp.int32, shape, dim).astype(F32)


def silu_norm(values, gain):
    power = jnp.mean(values * values, axis=1, keepdims=True)
    half = values * (0.5 * lax.rsqrt(power + 1e-06)) * gain
    return half + half * jnp.tanh(half)


def is_even(axis):
    return lax.rem(lax.axis_index(axis), 2) == 0


def setup_kernel(
    prior, noise, cell, owner, slot, weight, live, station,
    state_msg, entry_msg, noise_a, noise_b,
    *, lond, latb, slots, n_wt,
):
    count = cell.shape[1]
    cells = cell[...]
    lon = cells % lond
    row = (cells // lond) % latb
    variable = cells // (lond * latb)
    rv = row * prior.shape[0] + variable
    key = owner[...] * slots + slot[...]
    alive = lax.broadcasted_iota(jnp.int32, (1, count), 1) < live[...]
    weights = jnp.where(alive, weight[...], 0.0)
    mine = lax.axis_index("band") * slots + lax.broadcasted_iota(jnp.int32, (1, count), 1)
    rows = [key.astype(F32), rv.astype(F32), lon.astype(F32), weights, station[...], mine.astype(F32)]
    entry_msg[0:1] = rows[0]
    entry_msg[1:2] = rows[1]
    entry_msg[2:3] = rows[2]
    entry_msg[3:4] = rows[3]
    entry_msg[4:5] = rows[4]
    entry_msg[5:6] = rows[5]
    entry_msg[6:8] = jnp.zeros((2, count), F32)
    columns = jnp.transpose(entry_msg[...])
    rv_col, lon_col = columns[:, 1:2], columns[:, 2:3]
    one_hot = jnp.where(rv_col == iota((count, latb * prior.shape[0]), 1), 1.0, 0.0).astype(BF16)
    current = jnp.concatenate([prior[:, r, :] for r in range(latb)], axis=0)
    picked = sum(dot(one_hot, part) for part in pieces(current, 3))
    at = jnp.sum(jnp.where(lon_col == iota((count, lond), 1), picked, 0.0), axis=1, keepdims=True)
    eye = iota((count, count), 0) == iota((count, count), 1)
    entry_msg[6:7] = weights * jnp.sum(jnp.where(eye, at, 0.0), axis=0, keepdims=True)
    for r in range(latb):
        state_msg[r] = (prior[:, r, :] * shrink(STEPS[0][0])).astype(BF16)
    up = [(k, r) for k in range(3) for r in range(1 + k, latb)]
    down = [(k, r) for k in range(3) for r in range(0, latb - 1 - k)]

    @pl.when(is_even("band"))
    def _():
        for i in range(len(up)):
            noise_a[i] = noise[up[i][0], :, up[i][1], :].astype(BF16)
            noise_b[i] = noise[down[i][0], :, down[i][1], :].astype(BF16)

    @pl.when(jnp.logical_not(is_even("band")))
    def _():
        for i in range(len(up)):
            noise_a[i] = noise[down[i][0], :, down[i][1], :].astype(BF16)
            noise_b[i] = noise[up[i][0], :, up[i][1], :].astype(BF16)


def edges_into(edge_ref, state, rows, level):
    lane = lax.broadcasted_iota(jnp.int32, (1, LANES), 1)
    width = state.shape[2]
    edge = jnp.zeros(edge_ref.shape, F32)
    for r in range(rows):
        slab = state[r]
        edge = jnp.where(lane == r, slab[:, 0:1], edge)
        edge = jnp.where(lane == HALF + r, slab[:, width - 1 : width], edge)
    edge_ref[...] = (edge * shrink(level)).astype(BF16)


def extend_kernel(prior, halo_a, halo_b, state, edge, *, latb):
    grow = 1.0 / shrink(STEPS[0][0])
    for r in range(latb):
        state[HALO + r] = prior[:, r, :]

    @pl.when(is_even("band"))
    def _():
        for r in range(latb):
            state[r] = halo_b[r].astype(F32) * grow
            state[HALO + latb + r] = halo_a[r].astype(F32) * grow

    @pl.when(jnp.logical_not(is_even("band")))
    def _():
        for r in range(latb):
            state[r] = halo_a[r].astype(F32) * grow
            state[HALO + latb + r] = halo_b[r].astype(F32) * grow

    edges_into(edge, state, 2 * HALO + latb, STEPS[0][0])


def tables_kernel(*refs, n_msgs, variables, latb, lond):
    msgs = refs[:n_msgs]
    keys, cols, pick, spread = refs[n_msgs:]
    count = msgs[0].shape[1]
    high = latb * variables
    even = is_even("band")
    own = msgs[0][...]
    low = jnp.where(even, msgs[2][...], msgs[1][...])
    up = jnp.where(even, msgs[1][...], msgs[2][...])
    for i in range(n_msgs):
        keys[:, i * count : (i + 1) * count] = msgs[i][...]
    for j, msg in enumerate((own, low, up)):
        col = jnp.transpose(msg)
        block = slice(j * count, (j + 1) * count)
        key = jnp.broadcast_to(col[:, 0:1], (count, LANES))
        acc = jnp.zeros((count, LANES), F32)
        for i in range(n_msgs):
            for part in range(count // LANES):
                at = slice(part * LANES, (part + 1) * LANES)
                acc = acc + jnp.where(key == msgs[i][5:6, at], msgs[i][4:5, at], 0.0)
        cols[0, block] = key
        cols[1, block] = jnp.broadcast_to(jnp.sum(acc, axis=1, keepdims=True), (count, LANES))
        cols[2, block] = jnp.broadcast_to(col[:, 3:4], (count, LANES))
        cols[3, block] = jnp.broadcast_to(col[:, 2:3], (count, LANES))
        cols[4, block] = jnp.broadcast_to(col[:, 1:2] * lond + col[:, 2:3], (count, LANES))
        cols[5, block] = jnp.broadcast_to(col[:, 5:6], (count, LANES))
        spread[j] = jnp.where(iota((high, count), 0) == msg[1:2], 1.0, 0.0).astype(BF16)
        if j == 0:
            pick[...] = jnp.where(col[:, 1:2] == iota((count, high), 1), 1.0, 0.0).astype(BF16)


def network_kernel(*refs, step, rows, latb, gather):
    state, edge_a, edge_b, noise, halo_a, halo_b, lift, conv, head, gain_1, gain_2 = refs[:11]
    if gather:
        pick, cols, target, at_entries, firsts, lifteds, halos = refs[11:]
    else:
        target, firsts, lifteds = refs[11:]
    level, drift, kick = STEPS[step]
    scale = shrink(level)
    wide = rows + 2
    out_halo = (rows - latb) // 2
    width = state.shape[2]
    channels = lift.shape[1]
    band = lax.axis_index("band")
    north = band == 0
    south = band == lax.axis_size("band") - 1

    lane = lax.broadcasted_iota(jnp.int32, (1, LANES), 1)
    even = is_even("wt")
    from_a, from_b = edge_a[...].astype(F32), edge_b[...].astype(F32)
    right = jnp.where(even, from_a, from_b)
    left = jnp.where(even, from_b, from_a)
    edge = pltpu.roll(jnp.where(lane < HALF, right, left), HALF, 1).astype(BF16)
    edge = silu_norm(dot(edge, lift[...], 0, 0), gain_1[...])

    sub = lax.broadcasted_iota(jnp.int32, (width, 1), 0)
    for r in range(wide):
        lifted = dot((state[r] * scale).astype(BF16), lift[...], 0, 0)
        if 1 <= r <= rows:
            lifteds[(r - 1) * width : r * width] = lifted
        first = silu_norm(lifted, gain_1[...])
        before, after = edge[r : r + 1], edge[HALF + r : HALF + r + 1]
        outside = None
        if r < out_halo + 1:
            outside = north
        elif r >= out_halo + 1 + latb:
            outside = south
        if outside is not None:
            first = jnp.where(outside, 0.0, first)
            before = jnp.where(outside, 0.0, before)
            after = jnp.where(outside, 0.0, after)
        here = slice(r * width, (r + 1) * width)
        firsts[here, 0:channels] = jnp.where(sub == 0, before, pltpu.roll(first, 1, 0)).astype(BF16)
        firsts[here, channels : 2 * channels] = first.astype(BF16)
        firsts[here, 2 * channels : 3 * channels] = jnp.where(
            sub == width - 1, after, pltpu.roll(first, width - 1, 0)
        ).astype(BF16)

    mixed = lifteds[0 : rows * width]
    for p in range(3):
        mixed = mixed + dot(
            firsts[p * width : (p + rows) * width], conv[3 * channels * p : 3 * channels * (p + 1)]
        )
    second = silu_norm(mixed, gain_2[...]).astype(BF16)
    base = sum(3 - k for k in range(step))
    if out_halo:
        even_band = is_even("band")
    for i in range(rows):
        score = dot(head[...], second[i * width : (i + 1) * width], 0, 1)
        r = i - out_halo
        if 0 <= r < latb:
            draw = noise[step, :, r, :]
        else:
            a, b = halo_a[base + i % (out_halo + latb)], halo_b[base + i % (out_halo + latb)]
            draw = (jnp.where(even_band, b, a) if r < 0 else jnp.where(even_band, a, b)).astype(F32)
        target[i] = state[i + 1] + (drift / level) * score + kick * draw
    if gather:
        variables = state.shape[1]
        for r in range(latb):
            for j, part in enumerate(pieces(target[out_halo + r], 3)):
                halos[r * variables : (r + 1) * variables, j * width : (j + 1) * width] = part
        picked = dot(pick[...], halos[...])
        picked = picked[:, 0:width] + picked[:, width : 2 * width] + picked[:, 2 * width :]
        count = pick.shape[0]
        lon = jnp.concatenate([cols[3, 0:count]] * (width // LANES), axis=1)
        at = jnp.sum(jnp.where(lon == iota((count, width), 1), picked, 0.0), axis=1, keepdims=True)
        at_entries[...] = jnp.broadcast_to(at, (count, LANES))


def matching(key, keys, values):
    count = values[0].shape[1]
    acc = jnp.zeros(key.shape, F32)
    for i, row in enumerate(values):
        for part in range(count // LANES):
            at = slice(part * LANES, (part + 1) * LANES)
            known = keys[0:1, i * count + part * LANES : i * count + (part + 1) * LANES]
            acc = acc + jnp.where(key == known, row[:, at], 0.0)
    return jnp.sum(acc, axis=1, keepdims=True)


def update_kernel(*refs, step, n_msgs, rows, latb, value_row):
    target, keys, cols, spread = refs[:4]
    values = [ref[value_row : value_row + 1] for ref in refs[4 : 4 + n_msgs]]
    rest = refs[4 + n_msgs :]
    last = step == len(STEPS) - 1
    count = values[0].shape[1]
    variables, width = target.shape[1], target.shape[2]
    out_halo = (rows - latb) // 2
    strength = obs_precision * STEPS[step][1]

    def column(j):
        block = slice(j * count, (j + 1) * count)
        found = matching(cols[0, block], keys, values)
        return strength * cols[2, block] * (cols[1, block] - found)

    def spread_rows(j, column_j, rows_from, rows_to):
        block = slice(j * count, (j + 1) * count)
        lon = jnp.concatenate([cols[3, block]] * (width // LANES), axis=1)
        tall = jnp.concatenate([column_j] * (width // LANES), axis=1)
        value = jnp.where(lon == iota((count, width), 1), tall, 0.0)
        parts = jnp.concatenate(pieces(value, 2), axis=1)
        both = dot(spread[j, rows_from * variables : rows_to * variables], parts)
        return both[:, 0:width] + both[:, width:]

    mine = column(0)
    own = spread_rows(0, mine, 0, latb)
    if last:
        state, innov = rest
        for r in range(latb):
            state[:, r, :] = target[out_halo + r] + own[r * variables : (r + 1) * variables]
        found = matching(cols[5, 0:count], keys, values)
        eye = iota((count, count), 0) == iota((count, count), 1)
        innov[...] = keys[4:5, 0:count] - jnp.sum(jnp.where(eye, found, 0.0), axis=0, keepdims=True)
        return
    at_entries, state, edge, value = rest
    row_cell = keys[1:2, 0:count] * width + keys[2:3, 0:count]
    cell = jnp.concatenate([cols[4, 0:count]] * (count // LANES), axis=1)
    tall = jnp.concatenate([mine] * (count // LANES), axis=1)
    before = jnp.concatenate([at_entries[...]] * (count // LANES), axis=1)
    eye = iota((count, count), 0) == iota((count, count), 1)
    total = jnp.where(cell == row_cell, tall, 0.0) + jnp.where(eye, before, 0.0)
    value[...] = jnp.broadcast_to(
        keys[3:4, 0:count] * jnp.sum(total, axis=0, keepdims=True), value.shape
    )
    for r in range(latb):
        state[out_halo + r] = target[out_halo + r] + own[r * variables : (r + 1) * variables]
    if out_halo:
        low = spread_rows(1, column(1), latb - out_halo, latb)
        up = spread_rows(2, column(2), 0, out_halo)
        for r in range(out_halo):
            here = slice(r * variables, (r + 1) * variables)
            state[r] = target[r] + low[here]
            state[out_halo + latb + r] = target[out_halo + latb + r] + up[here]
    edges_into(edge, state, rows, STEPS[step + 1][0])


def swaps(count):
    first = [(i, i ^ 1) for i in range(count)]
    other = [(i, (i - 1) % count if i % 2 == 0 else (i + 1) % count) for i in range(count)]
    return first, other


def from_neighbours(block, axis):
    return [lax.ppermute(block, axis, route) for route in swaps(lax.axis_size(axis))]


def from_bands(block):
    count = lax.axis_size("band")
    found = [block] + from_neighbours(block, "band")
    reach = min(2 * REACH + 1, count)
    far = sorted({d % count for d in range(-reach, reach + 1)} - {0, 1, count - 1})
    for distance in far:
        route = [(i, (i + distance) % count) for i in range(count)]
        found.append(lax.ppermute(block, "band", route))
    return found


def per_device(
    prior_state, langevin_noise, station_values, entry_cell, entry_owner, entry_slot,
    entry_weight, live_counts, lift_weight, conv_weight, head_weight, first_gain, second_gain,
):
    variables, latb, lond = prior_state.shape
    count = entry_cell.shape[0]
    slots = station_values.shape[0]
    channels = lift_weight.shape[1]
    taps = conv_weight.reshape(-1, channels)
    gain_1, gain_2 = first_gain.reshape(1, -1), second_gain.reshape(1, -1)

    def row(a):
        return a.reshape(1, -1)

    noise_slabs = sum(latb - 1 - k for k in range(3))
    state_msg, entry_msg, noise_a, noise_b = vmem_call(
        functools.partial(
            setup_kernel, lond=lond, latb=latb, slots=slots, n_wt=lax.axis_size("wt")
        ),
        [
            ((latb, variables, lond), BF16),
            ((8, count), F32),
            ((noise_slabs, variables, lond), BF16),
            ((noise_slabs, variables, lond), BF16),
        ],
        prior_state, langevin_noise, row(entry_cell), row(entry_owner), row(entry_slot),
        row(entry_weight), jnp.broadcast_to(live_counts, (1, count)), row(station_values),
    )
    halos = from_neighbours(state_msg, "band")
    msgs = from_bands(entry_msg)
    route_a, route_b = swaps(lax.axis_size("band"))
    noise_halo_a = lax.ppermute(noise_a, "band", route_a)
    noise_halo_b = lax.ppermute(noise_b, "band", route_b)
    n_msgs = len(msgs)
    state, edge = vmem_call(
        functools.partial(extend_kernel, latb=latb),
        [((2 * HALO + latb, variables, lond), F32), ((variables, LANES), BF16)],
        prior_state, *halos,
    )
    edges = from_neighbours(edge, "wt")
    keys, cols, pick, spread = vmem_call(
        functools.partial(tables_kernel, n_msgs=n_msgs, variables=variables, latb=latb, lond=lond),
        [
            ((8, n_msgs * count), F32),
            ((6, 3 * count, LANES), F32),
            ((count, latb * variables), BF16),
            ((3, latb * variables, count), BF16),
        ],
        *msgs,
    )
    values, value_row = msgs, 6
    for step in range(len(STEPS)):
        last = step == len(STEPS) - 1
        rows = latb + 2 * (HALO - 1 - step)
        network_out = [((rows, variables, lond), F32)]
        network_in = [
            state, *edges, langevin_noise, noise_halo_a, noise_halo_b,
            lift_weight, taps, head_weight, gain_1, gain_2,
        ]
        scratch = [
            pltpu.VMEM(((rows + 2) * lond, 3 * channels), BF16),
            pltpu.VMEM((rows * lond, channels), F32),
        ]
        if not last:
            network_out.append(((count, LANES), F32))
            network_in += [pick, cols]
            scratch.append(pltpu.VMEM((latb * variables, 3 * lond), BF16))
        found = vmem_call(
            functools.partial(network_kernel, step=step, rows=rows, latb=latb, gather=not last),
            network_out,
            *network_in,
            scratch=scratch,
        )
        update = functools.partial(
            update_kernel, step=step, n_msgs=n_msgs, rows=rows, latb=latb, value_row=value_row
        )
        if last:
            state, innov = vmem_call(
                update,
                [((variables, latb, lond), F32), ((1, count), F32)],
                found[0], keys, cols, spread, *values,
            )
            return state, innov.reshape(-1)
        state, edge, value = vmem_call(
            update,
            [((rows, variables, lond), F32), ((variables, LANES), BF16), ((8, count), F32)],
            found[0], keys, cols, spread, *values, found[1],
        )
        values, value_row = from_bands(value), 0
        edges = from_neighbours(edge, "wt")


def solution(mesh):
    split = P(("groups", "band", "wt"))
    in_specs = (
        P("groups", "band", "wt"),
        P(None, "groups", "band", "wt"),
        split, split, split, split, split, split,
        P(), P(), P(), P(), P(),
    )
    out_specs = (P("groups", "band", "wt"), split)
    return jax.shard_map(
        per_device, mesh=mesh, in_specs=in_specs, out_specs=out_specs, check_vma=False
    )
```

```python
import functools
import math

import jax
import jax.numpy as jnp
from jax import lax
from jax.experimental import pallas as pl
from jax.experimental.pallas import tpu as pltpu
from jax.sharding import PartitionSpec as P

F32 = jnp.float32
BF16 = jnp.bfloat16
REACH = 2
HALO = 4
LANES = 128
HALF = 64
CHUNK = 4

noise_levels = (1.0, 0.6, 0.3)
obs_precision = 4.0
step_factor = 0.1


def sub_steps():
    steps = []
    for section in range(2):
        upper, lower = noise_levels[section], noise_levels[section + 1]
        spread = upper * upper - lower * lower
        steps.append((upper, spread, math.sqrt(spread)))
        factor = step_factor * lower * lower
        steps.append((lower, factor, math.sqrt(2.0 * factor)))
    return steps


STEPS = sub_steps()


def shrink(level):
    return 1.0 / math.sqrt(1.0 + level * level)


def vmem_call(kernel, outs, *args, scratch=(), scalars=0, hbm_in=0, hbm_out=False, flops=0):
    args = list(args)
    for i in range(scalars, len(args)):
        place = pltpu.HBM if i < scalars + hbm_in else pltpu.VMEM
        args[i] = pltpu.with_memory_space_constraint(args[i], place)
    smem = pl.BlockSpec(memory_space=pltpu.SMEM)
    vmem, hbm = pl.BlockSpec(memory_space=pltpu.VMEM), pl.BlockSpec(memory_space=pltpu.HBM)
    out_type = jax.ShapeDtypeStruct if hbm_out else pltpu.VMEM
    return pl.pallas_call(
        kernel,
        out_shape=[out_type(shape, dtype) for shape, dtype in outs],
        in_specs=[smem] * scalars + [hbm] * hbm_in + [vmem] * (len(args) - scalars - hbm_in),
        out_specs=[hbm if hbm_out else vmem] * len(outs),
        scratch_shapes=list(scratch),
        cost_estimate=pl.CostEstimate(flops=flops, bytes_accessed=0, transcendentals=0),
        compiler_params=pltpu.CompilerParams(vmem_limit_bytes=48 * 2**20),
    )(*args)


def dot(a, b, ca=1, cb=0):
    return lax.dot_general(a, b, (((ca,), (cb,)), ((), ())), preferred_element_type=F32)


def pieces(x, count):
    out = []
    for _ in range(count):
        part = x.astype(BF16)
        out.append(part)
        x = x - part.astype(F32)
    return out


def iota(shape, dim):
    return lax.broadcasted_iota(jnp.int32, shape, dim).astype(F32)


def silu_norm(values, gain):
    power = jnp.mean(values * values, axis=1, keepdims=True)
    half = values * (0.5 * lax.rsqrt(power + 1e-06)) * gain
    return half + half * jnp.tanh(half)


def is_even(axis):
    return lax.rem(lax.axis_index(axis), 2) == 0


def stage_kernel(*refs, n_args, slots):
    live, sources, staged = refs[0], refs[1 : 1 + n_args], refs[1 + n_args : 1 + 2 * n_args]
    msg, entry_msg, sems = refs[1 + 2 * n_args :]
    copies = [
        pltpu.make_async_copy(source, target, sems.at[i])
        for i, (source, target) in enumerate(zip(sources, staged))
    ]
    for copy in copies:
        copy.start()
    prior, _, cell, owner, slot, weight, station = staged[:7]
    _, latb, lond = prior.shape
    copies[0].wait()
    for r in range(latb):
        msg[r] = (prior[:, r, :] * shrink(STEPS[0][0])).astype(BF16)
    for copy in copies[2:7]:
        copy.wait()
    count = cell.shape[1]
    cells = cell[...]
    lon = cells % lond
    row = (cells // lond) % latb
    variable = cells // (lond * latb)
    rv = row * prior.shape[0] + variable
    key = owner[...] * slots + slot[...]
    alive = lax.broadcasted_iota(jnp.int32, (1, count), 1) < live[0]
    weights = jnp.where(alive, weight[...], 0.0)
    mine = lax.axis_index("band") * slots + lax.broadcasted_iota(jnp.int32, (1, count), 1)
    entry_msg[0:1] = key.astype(F32)
    entry_msg[1:2] = rv.astype(F32)
    entry_msg[2:3] = lon.astype(F32)
    entry_msg[3:4] = weights
    entry_msg[4:5] = station[...]
    entry_msg[5:6] = mine.astype(F32)
    entry_msg[6:8] = jnp.zeros((2, count), F32)
    columns = jnp.transpose(entry_msg[...])
    rv_col, lon_col = columns[:, 1:2], columns[:, 2:3]
    one_hot = jnp.where(rv_col == iota((count, latb * prior.shape[0]), 1), 1.0, 0.0).astype(BF16)
    current = jnp.concatenate([prior[:, r, :] for r in range(latb)], axis=0)
    picked = sum(dot(one_hot, part) for part in pieces(current, 2))
    at = jnp.sum(jnp.where(lon_col == iota((count, lond), 1), picked, 0.0), axis=1, keepdims=True)
    eye = iota((count, count), 0) == iota((count, count), 1)
    entry_msg[6:7] = weights * jnp.sum(jnp.where(eye, at, 0.0), axis=0, keepdims=True)
    copies[1].wait()
    for copy in copies[7:]:
        copy.wait()


def edges_into(edge_ref, state, rows, level):
    lane = lax.broadcasted_iota(jnp.int32, (1, LANES), 1)
    width = state.shape[2]
    edge = jnp.zeros(edge_ref.shape, F32)
    for r in range(rows):
        slab = state[r]
        edge = jnp.where(lane == r, slab[:, 0:1], edge)
        edge = jnp.where(lane == HALF + r, slab[:, width - 1 : width], edge)
    edge_ref[...] = (edge * shrink(level)).astype(BF16)


def extend_kernel(*refs, latb):
    prior, halo_a, halo_b = refs[:3]
    state, edge = refs[-2:]
    grow = 1.0 / shrink(STEPS[0][0])
    for r in range(latb):
        state[HALO + r] = prior[:, r, :]

    @pl.when(is_even("band"))
    def _():
        for r in range(latb):
            state[r] = halo_b[r].astype(F32) * grow
            state[HALO + latb + r] = halo_a[r].astype(F32) * grow

    @pl.when(jnp.logical_not(is_even("band")))
    def _():
        for r in range(latb):
            state[r] = halo_a[r].astype(F32) * grow
            state[HALO + latb + r] = halo_b[r].astype(F32) * grow

    edges_into(edge, state, 2 * HALO + latb, STEPS[0][0])


def noise_kernel(noise, after, noise_a, noise_b):
    latb = noise.shape[2]
    up = [(k, r) for k in range(HALO - 1) for r in range(1 + k, latb)]
    down = [(k, r) for k in range(HALO - 1) for r in range(0, latb - 1 - k)]

    @pl.when(is_even("band"))
    def _():
        for i in range(len(up)):
            noise_a[i] = noise[up[i][0], :, up[i][1], :].astype(BF16)
            noise_b[i] = noise[down[i][0], :, down[i][1], :].astype(BF16)

    @pl.when(jnp.logical_not(is_even("band")))
    def _():
        for i in range(len(up)):
            noise_a[i] = noise[down[i][0], :, down[i][1], :].astype(BF16)
            noise_b[i] = noise[up[i][0], :, up[i][1], :].astype(BF16)


def wide(column):
    return jnp.broadcast_to(column, (column.shape[0], LANES))


def one_hot(position, shape, dim):
    return jnp.where(position == iota(shape, dim), 1.0, 0.0).astype(BF16)


def own_kernel(msg, cols, pick, spread, *, variables, latb, lond):
    count = msg.shape[1]
    high = latb * variables
    col = jnp.transpose(msg[...])
    cols[0] = wide(col[:, 0:1])
    cols[1] = wide(col[:, 3:4])
    cols[2] = wide(col[:, 2:3])
    cols[3] = wide(col[:, 1:2] * lond + col[:, 2:3])
    cols[4] = wide(col[:, 5:6])
    pick[...] = one_hot(col[:, 1:2], (count, high), 1)
    spread[...] = one_hot(msg[1:2], (high, count), 0)


def tables_kernel(*refs, n_msgs, variables, latb):
    own_cols, msgs = refs[0], refs[1 : 1 + n_msgs]
    keys, near, seen, spread = refs[1 + n_msgs :]
    count = msgs[0].shape[1]
    even = is_even("band")
    low = jnp.where(even, msgs[2][...], msgs[1][...])
    up = jnp.where(even, msgs[1][...], msgs[2][...])
    for i in range(n_msgs):
        keys[:, i * count : (i + 1) * count] = msgs[i][...]
    for j, msg in enumerate((low, up)):
        col = jnp.transpose(msg)
        for i, source in enumerate((0, 3, 2)):
            near[i, j * count : (j + 1) * count] = wide(col[:, source : source + 1])
        spread[j] = one_hot(msg[1:2], (latb * variables, count), 0)
    for j in range(3):
        block = slice((j - 1) * count, j * count)
        key = near[0, block] if j else own_cols[0]
        acc = jnp.zeros((count, LANES), F32)
        for i in range(n_msgs):
            for part in range(count // LANES):
                at = slice(part * LANES, (part + 1) * LANES)
                acc = acc + jnp.where(key == msgs[i][5:6, at], msgs[i][4:5, at], 0.0)
        seen[j * count : (j + 1) * count] = wide(jnp.sum(acc, axis=1, keepdims=True))


def network_kernel(*refs, step, rows, latb, gather):
    state, edge_a, edge_b, noise, lift, conv, head, gain_1, gain_2 = refs[:9]
    if gather:
        pick, cols, target, at_entries, firsts, lifteds, sums, parts = refs[9:]
    else:
        target, firsts, lifteds, sums = refs[9:]
    level, drift, kick = STEPS[step]
    scale = shrink(level)
    out_halo = (rows - latb) // 2
    width = state.shape[2]
    channels = lift.shape[1]
    band = lax.axis_index("band")
    north = band == 0
    south = band == lax.axis_size("band") - 1

    lane = lax.broadcasted_iota(jnp.int32, (1, LANES), 1)
    even = is_even("wt")
    from_a, from_b = edge_a[...].astype(F32), edge_b[...].astype(F32)
    right = jnp.where(even, from_a, from_b)
    left = jnp.where(even, from_b, from_a)
    edge = pltpu.roll(jnp.where(lane < HALF, right, left), HALF, 1).astype(BF16)
    edge = silu_norm(dot(edge, lift[...], 0, 0), gain_1[...])

    sub = lax.broadcasted_iota(jnp.int32, (width, 1), 0)
    def first_row(r):
        lifted = dot((state[r] * scale).astype(BF16), lift[...], 0, 0)
        if 1 <= r <= rows:
            lifteds[(r - 1) * width : r * width] = lifted
        first = silu_norm(lifted, gain_1[...])
        before, after = edge[r : r + 1], edge[HALF + r : HALF + r + 1]
        outside = None
        if r < out_halo + 1:
            outside = north
        elif r >= out_halo + 1 + latb:
            outside = south
        if outside is not None:
            first = jnp.where(outside, 0.0, first)
            before = jnp.where(outside, 0.0, before)
            after = jnp.where(outside, 0.0, after)
        here = slice(r * width, (r + 1) * width)
        firsts[here, 0:channels] = jnp.where(sub == 0, before, pltpu.roll(first, 1, 0)).astype(BF16)
        firsts[here, channels : 2 * channels] = first.astype(BF16)
        firsts[here, 2 * channels : 3 * channels] = jnp.where(
            sub == width - 1, after, pltpu.roll(first, width - 1, 0)
        ).astype(BF16)

    def mix(start, stop):
        total = lifteds[start * width : stop * width]
        for p in range(3):
            total = total + dot(
                firsts[(start + p) * width : (stop + p) * width],
                conv[3 * channels * p : 3 * channels * (p + 1)],
            )
        sums[start * width : stop * width] = total

    def finish(start, stop):
        for i in range(start, stop):
            second = silu_norm(sums[i * width : (i + 1) * width], gain_2[...]).astype(BF16)
            moved = state[i + 1] + (drift / level) * dot(head[...], second, 1, 1)
            if out_halo <= i < out_halo + latb:
                moved = moved + kick * noise[step, :, i - out_halo, :]
            target[i] = moved

    bounds = [0]
    while bounds[-1] < rows:
        bounds.append(min(rows, bounds[-1] + CHUNK))
    made = 0
    for j, (start, stop) in enumerate(zip(bounds, bounds[1:])):
        for r in range(made, stop + 2):
            first_row(r)
        made = stop + 2
        mix(start, stop)
        if j + 2 < len(bounds):
            for r in range(made, bounds[j + 2] + 2):
                first_row(r)
            made = bounds[j + 2] + 2
        if j:
            finish(bounds[j - 1], start)
    finish(bounds[-2], rows)
    if gather:
        variables = state.shape[1]
        for r in range(latb):
            for j, part in enumerate(pieces(target[out_halo + r], 2)):
                parts[r * variables : (r + 1) * variables, j * width : (j + 1) * width] = part
        picked = dot(pick[...], parts[...])
        picked = picked[:, 0:width] + picked[:, width:]
        count = pick.shape[0]
        lon = jnp.concatenate([cols[2]] * (width // LANES), axis=1)
        at = jnp.sum(jnp.where(lon == iota((count, width), 1), picked, 0.0), axis=1, keepdims=True)
        at_entries[...] = jnp.broadcast_to(at, (count, LANES))


def matching(key, keys, values):
    count = values[0].shape[1]
    acc = jnp.zeros(key.shape, F32)
    for i, row in enumerate(values):
        for part in range(count // LANES):
            at = slice(part * LANES, (part + 1) * LANES)
            known = keys[0:1, i * count + part * LANES : i * count + (part + 1) * LANES]
            acc = acc + jnp.where(key == known, row[:, at], 0.0)
    return jnp.sum(acc, axis=1, keepdims=True)


def update_kernel(*refs, step, n_msgs, rows, latb, value_row):
    target, keys, cols, spread, near, seen, near_spread = refs[:7]
    values = [ref[value_row : value_row + 1] for ref in refs[7 : 7 + n_msgs]]
    rest = refs[7 + n_msgs :]
    last = step == len(STEPS) - 1
    count = values[0].shape[1]
    variables, width = target.shape[1], target.shape[2]
    out_halo = (rows - latb) // 2
    strength = obs_precision * STEPS[step][1]

    def columns_of(j):
        if j == 0:
            return cols[0], cols[1], cols[2]
        block = slice((j - 1) * count, j * count)
        return near[0, block], near[1, block], near[2, block]

    def column(j):
        key, weight, _ = columns_of(j)
        found = matching(key, keys, values)
        return strength * weight * (seen[j * count : (j + 1) * count] - found)

    def spread_rows(j, column_j, rows_from, rows_to):
        lon = jnp.concatenate([columns_of(j)[2]] * (width // LANES), axis=1)
        tall = jnp.concatenate([column_j] * (width // LANES), axis=1)
        value = jnp.where(lon == iota((count, width), 1), tall, 0.0)
        parts = jnp.concatenate(pieces(value, 2), axis=1)
        here = slice(rows_from * variables, rows_to * variables)
        both = dot(near_spread[j - 1, here] if j else spread[here], parts)
        return both[:, 0:width] + both[:, width:]

    mine = column(0)
    own = spread_rows(0, mine, 0, latb)
    if last:
        state_out, innov_out, state, innov, sems = rest
        for r in range(latb):
            state[:, r, :] = target[out_halo + r] + own[r * variables : (r + 1) * variables]
        state_copy = pltpu.make_async_copy(state, state_out, sems.at[0])
        state_copy.start()
        found = matching(cols[4], keys, values)
        eye = iota((count, count), 0) == iota((count, count), 1)
        innov[...] = keys[4:5, 0:count] - jnp.sum(jnp.where(eye, found, 0.0), axis=0, keepdims=True)
        innov_copy = pltpu.make_async_copy(innov, innov_out, sems.at[1])
        innov_copy.start()
        state_copy.wait()
        innov_copy.wait()
        return
    at_entries, halo_a, halo_b, state, edge, value = rest
    row_cell = keys[1:2, 0:count] * width + keys[2:3, 0:count]
    cell = jnp.concatenate([cols[3]] * (count // LANES), axis=1)
    tall = jnp.concatenate([mine] * (count // LANES), axis=1)
    before = jnp.concatenate([at_entries[...]] * (count // LANES), axis=1)
    eye = iota((count, count), 0) == iota((count, count), 1)
    total = jnp.where(cell == row_cell, tall, 0.0) + jnp.where(eye, before, 0.0)
    value[...] = jnp.broadcast_to(
        keys[3:4, 0:count] * jnp.sum(total, axis=0, keepdims=True), value.shape
    )
    for r in range(latb):
        state[out_halo + r] = target[out_halo + r] + own[r * variables : (r + 1) * variables]
    if out_halo:
        low = spread_rows(1, column(1), latb - out_halo, latb)
        up = spread_rows(2, column(2), 0, out_halo)
        base = sum(HALO - 1 - k for k in range(step))
        even = is_even("band")
        kick = STEPS[step][2]
        for r in range(out_halo):
            here = slice(r * variables, (r + 1) * variables)
            from_a, from_b = halo_a[base + r].astype(F32), halo_b[base + r].astype(F32)
            state[r] = target[r] + low[here] + kick * jnp.where(even, from_b, from_a)
            state[out_halo + latb + r] = (
                target[out_halo + latb + r] + up[here] + kick * jnp.where(even, from_a, from_b)
            )
    edges_into(edge, state, rows, STEPS[step + 1][0])


def swaps(count):
    first = [(i, i ^ 1) for i in range(count)]
    other = [(i, (i - 1) % count if i % 2 == 0 else (i + 1) % count) for i in range(count)]
    return first, other


def from_neighbours(block, axis):
    return [lax.ppermute(block, axis, route) for route in swaps(lax.axis_size(axis))]


def from_bands(block):
    count = lax.axis_size("band")
    found = [block] + from_neighbours(block, "band")
    reach = min(2 * REACH + 1, count)
    far = sorted({d % count for d in range(-reach, reach + 1)} - {0, 1, count - 1})
    for distance in far:
        route = [(i, (i + distance) % count) for i in range(count)]
        found.append(lax.ppermute(block, "band", route))
    return found


def per_device(
    prior_state, langevin_noise, station_values, entry_cell, entry_owner, entry_slot,
    entry_weight, live_counts, lift_weight, conv_weight, head_weight, first_gain, second_gain,
):
    variables, latb, lond = prior_state.shape
    count = entry_cell.shape[0]
    slots = station_values.shape[0]
    channels = lift_weight.shape[1]
    taps = conv_weight.reshape(-1, channels)
    gain_1, gain_2 = first_gain.reshape(1, -1), second_gain.reshape(1, -1)

    def row(a):
        return a.reshape(1, -1)

    taken = [
        prior_state, langevin_noise, row(entry_cell), row(entry_owner), row(entry_slot),
        row(entry_weight), row(station_values), taps, lift_weight, head_weight.T, gain_1, gain_2,
    ]
    *staged, msg, entry_msg = vmem_call(
        functools.partial(stage_kernel, n_args=len(taken), slots=slots),
        [(a.shape, a.dtype) for a in taken]
        + [((latb, variables, lond), BF16), ((8, count), F32)],
        live_counts, *taken,
        scalars=1,
        hbm_in=len(taken),
        scratch=[pltpu.SemaphoreType.DMA((len(taken),))],
    )
    prior_state, langevin_noise = staged[:2]
    taps, lift_weight, head_weight, gain_1, gain_2 = staged[7:]
    route_a, route_b = swaps(lax.axis_size("band"))
    route_b = [pair for pair in route_b if abs(pair[0] - pair[1]) == 1]
    halos = [lax.ppermute(msg, "band", route) for route in (route_a, route_b)]
    msgs = from_bands(entry_msg)
    n_msgs = len(msgs)
    high = latb * variables
    cols, pick, spread = vmem_call(
        functools.partial(own_kernel, variables=variables, latb=latb, lond=lond),
        [((5, count, LANES), F32), ((count, high), BF16), ((high, count), BF16)],
        entry_msg,
    )
    state, edge = vmem_call(
        functools.partial(extend_kernel, latb=latb),
        [((2 * HALO + latb, variables, lond), F32), ((variables, LANES), BF16)],
        prior_state, *halos, *msgs,
    )
    edges = from_neighbours(edge, "wt")
    slabs = ((sum(HALO - 1 - k for k in range(HALO - 1)), variables, lond), BF16)
    noise_a, noise_b = vmem_call(noise_kernel, [slabs, slabs], langevin_noise, edge)
    noise_halos = [lax.ppermute(noise_a, "band", route_a), lax.ppermute(noise_b, "band", route_b)]
    keys, near, seen, near_spread = vmem_call(
        functools.partial(tables_kernel, n_msgs=n_msgs, variables=variables, latb=latb),
        [
            ((8, n_msgs * count), F32),
            ((3, 2 * count, LANES), F32),
            ((3 * count, LANES), F32),
            ((2, high, count), BF16),
        ],
        cols, *msgs,
    )
    tables = (keys, cols, spread, near, seen, near_spread)
    values, value_row = msgs, 6
    for step in range(len(STEPS)):
        last = step == len(STEPS) - 1
        rows = latb + 2 * (HALO - 1 - step)
        network_out = [((rows, variables, lond), F32)]
        network_in = [
            state, *edges, langevin_noise,
            lift_weight, taps, head_weight, gain_1, gain_2,
        ]
        scratch = [
            pltpu.VMEM(((rows + 2) * lond, 3 * channels), BF16),
            pltpu.VMEM((rows * lond, channels), F32),
            pltpu.VMEM((rows * lond, channels), F32),
        ]
        if not last:
            network_out.append(((count, LANES), F32))
            network_in += [pick, cols]
            scratch.append(pltpu.VMEM((high, 2 * lond), BF16))
        found = vmem_call(
            functools.partial(network_kernel, step=step, rows=rows, latb=latb, gather=not last),
            network_out,
            *network_in,
            scratch=scratch,
            flops=4 * rows * lond * taps.size,
        )
        update = functools.partial(
            update_kernel, step=step, n_msgs=n_msgs, rows=rows, latb=latb, value_row=value_row
        )
        if last:
            outs = [((variables, latb, lond), F32), ((1, count), F32)]
            state, innov = vmem_call(
                update, outs, found[0], *tables, *values, hbm_out=True,
                scratch=[pltpu.VMEM(*out) for out in outs] + [pltpu.SemaphoreType.DMA((2,))],
            )
            return state, innov.reshape(-1)
        state, edge, value = vmem_call(
            update,
            [((rows, variables, lond), F32), ((variables, LANES), BF16), ((8, count), F32)],
            found[0], *tables, *values, found[1], *noise_halos,
        )
        values, value_row = from_bands(value), 0
        edges = from_neighbours(edge, "wt")


def solution(mesh):
    split = P(("groups", "band", "wt"))
    in_specs = (
        P("groups", "band", "wt"),
        P(None, "groups", "band", "wt"),
        split, split, split, split, split, split,
        P(), P(), P(), P(), P(),
    )
    out_specs = (P("groups", "band", "wt"), split)
    return jax.shard_map(
        per_device, mesh=mesh, in_specs=in_specs, out_specs=out_specs, check_vma=False
    )
```

```python
import functools
import math

import jax
import jax.numpy as jnp
from jax import lax
from jax.experimental import pallas as pl
from jax.experimental.pallas import tpu as pltpu
from jax.sharding import PartitionSpec as P

F32 = jnp.float32
BF16 = jnp.bfloat16
REACH = 2
HALO = 4
LANES = 128
HALF = 64
CHUNK = 4
PIECES = 3

noise_levels = (1.0, 0.6, 0.3)
obs_precision = 4.0
step_factor = 0.1


def sub_steps():
    steps = []
    for section in range(2):
        upper, lower = noise_levels[section], noise_levels[section + 1]
        spread = upper * upper - lower * lower
        steps.append((upper, spread, math.sqrt(spread)))
        factor = step_factor * lower * lower
        steps.append((lower, factor, math.sqrt(2.0 * factor)))
    return steps


STEPS = sub_steps()


def shrink(level):
    return 1.0 / math.sqrt(1.0 + level * level)


def vmem_call(kernel, outs, *args, scratch=(), scalars=0, hbm_in=0, hbm_out=False, flops=0):
    args = list(args)
    for i in range(scalars, len(args)):
        place = pltpu.HBM if i < scalars + hbm_in else pltpu.VMEM
        args[i] = pltpu.with_memory_space_constraint(args[i], place)
    smem = pl.BlockSpec(memory_space=pltpu.SMEM)
    vmem, hbm = pl.BlockSpec(memory_space=pltpu.VMEM), pl.BlockSpec(memory_space=pltpu.HBM)
    out_type = jax.ShapeDtypeStruct if hbm_out else pltpu.VMEM
    return pl.pallas_call(
        kernel,
        out_shape=[out_type(shape, dtype) for shape, dtype in outs],
        in_specs=[smem] * scalars + [hbm] * hbm_in + [vmem] * (len(args) - scalars - hbm_in),
        out_specs=[hbm if hbm_out else vmem] * len(outs),
        scratch_shapes=list(scratch),
        cost_estimate=pl.CostEstimate(flops=flops, bytes_accessed=0, transcendentals=0),
        compiler_params=pltpu.CompilerParams(vmem_limit_bytes=48 * 2**20),
    )(*args)


def dot(a, b, ca=1, cb=0):
    return lax.dot_general(a, b, (((ca,), (cb,)), ((), ())), preferred_element_type=F32)


def pieces(x, count):
    out = []
    for _ in range(count):
        part = x.astype(BF16)
        out.append(part)
        x = x - part.astype(F32)
    return out


def iota(shape, dim):
    return lax.broadcasted_iota(jnp.int32, shape, dim).astype(F32)


def silu_norm(values, gain):
    power = jnp.mean(values * values, axis=1, keepdims=True)
    half = values * (0.5 * lax.rsqrt(power + 1e-06)) * gain
    return half + half * jnp.tanh(half)


def is_even(axis):
    return lax.rem(lax.axis_index(axis), 2) == 0


def start_all(pairs, sems):
    copies = [
        pltpu.make_async_copy(source, target, sems.at[i])
        for i, (source, target) in enumerate(pairs)
    ]
    for copy in copies:
        copy.start()
    return copies


def rows_of(source, target):
    return [(source.at[:, r, :], target.at[r]) for r in range(target.shape[0])]


def later_kernel(noise_in, *refs):
    half = (len(refs) - 3) // 2
    noise, noise_a, noise_b, sems = refs[half], *refs[-3:]
    pairs = []
    for k in range(noise.shape[0]):
        pairs += rows_of(noise_in.at[k], noise.at[k])
    pairs += list(zip(refs[:half], refs[half + 1 : -3]))
    copies = start_all(pairs, sems)
    for copy in copies:
        copy.wait()
    latb = noise.shape[1]
    up = [(k, r) for k in range(HALO - 1) for r in range(1 + k, latb)]
    down = [(k, r) for k in range(HALO - 1) for r in range(0, latb - 1 - k)]

    @pl.when(is_even("band"))
    def _():
        for i in range(len(up)):
            noise_a[i] = noise[up[i]].astype(BF16)
            noise_b[i] = noise[down[i]].astype(BF16)

    @pl.when(jnp.logical_not(is_even("band")))
    def _():
        for i in range(len(up)):
            noise_a[i] = noise[down[i]].astype(BF16)
            noise_b[i] = noise[up[i]].astype(BF16)


def stage_kernel(*refs, slots):
    live, prior_in, entries_in = refs[0], refs[1], refs[2:7]
    prior, msg, copy_msg, entry_msg, *entries, sems = refs[7:]
    latb, _, lond = prior.shape
    copies = start_all(rows_of(prior_in, prior) + list(zip(entries_in, entries)), sems)
    for r in range(latb):
        copies[r].wait()
        slab = (prior[r] * shrink(STEPS[0][0])).astype(BF16)
        msg[r] = slab
        copy_msg[r] = slab
    for copy in copies[latb:]:
        copy.wait()
    cell, owner, slot, weight, station = entries
    count = cell.shape[1]
    cells = cell[...]
    lon = cells % lond
    row = (cells // lond) % latb
    variable = cells // (lond * latb)
    rv = row * prior.shape[1] + variable
    key = owner[...] * slots + slot[...]
    alive = lax.broadcasted_iota(jnp.int32, (1, count), 1) < live[0]
    weights = jnp.where(alive, weight[...], 0.0)
    mine = lax.axis_index("band") * slots + lax.broadcasted_iota(jnp.int32, (1, count), 1)
    entry_msg[0:1] = key.astype(F32)
    entry_msg[1:2] = rv.astype(F32)
    entry_msg[2:3] = lon.astype(F32)
    entry_msg[3:4] = weights
    entry_msg[4:5] = station[...]
    entry_msg[5:6] = mine.astype(F32)
    entry_msg[6:8] = jnp.zeros((2, count), F32)
    columns = jnp.transpose(entry_msg[...])
    rv_col, lon_col = columns[:, 1:2], columns[:, 2:3]
    one_hot = jnp.where(rv_col == iota((count, latb * prior.shape[1]), 1), 1.0, 0.0).astype(BF16)
    current = jnp.concatenate([prior[r] for r in range(latb)], axis=0)
    picked = sum(dot(one_hot, part) for part in pieces(current, 2))
    at = jnp.sum(jnp.where(lon_col == iota((count, lond), 1), picked, 0.0), axis=1, keepdims=True)
    eye = iota((count, count), 0) == iota((count, count), 1)
    entry_msg[6:7] = weights * jnp.sum(jnp.where(eye, at, 0.0), axis=0, keepdims=True)
    high = jnp.concatenate([part.astype(F32) for part in pieces(entry_msg[...], PIECES)], axis=0)
    msg[latb, 0 : 8 * PIECES] = high.astype(BF16)
    copy_msg[latb, 0 : 8 * PIECES] = high.astype(BF16)


def edges_into(edge_ref, state, rows, level):
    lane = lax.broadcasted_iota(jnp.int32, (1, LANES), 1)
    width = state.shape[2]
    edge = jnp.zeros(edge_ref.shape, F32)
    for r in range(rows):
        slab = state[r]
        edge = jnp.where(lane == r, slab[:, 0:1], edge)
        edge = jnp.where(lane == HALF + r, slab[:, width - 1 : width], edge)
    edge_ref[...] = (edge * shrink(level)).astype(BF16)


def extend_kernel(prior, halo_a, halo_b, far, *refs, latb):
    state, edge, msg_a, msg_b = refs[-4:]
    grow = 1.0 / shrink(STEPS[0][0])
    band = lax.axis_index("band")
    even = is_even("band")
    for r in range(latb):
        from_a, from_b = halo_a[r].astype(F32) * grow, halo_b[r].astype(F32) * grow
        state[r] = jnp.where(even, from_b, from_a)
        state[HALO + r] = prior[r]
        state[HALO + latb + r] = jnp.where(even, from_a, from_b)
    edges_into(edge, state, 2 * HALO + latb, STEPS[0][0])
    outer = jnp.logical_or(band == 0, band == lax.axis_size("band") - 1)
    for halo, msg in ((halo_a, msg_a), (halo_b, msg_b)):
        parts = halo[latb, 0 : 8 * PIECES].astype(F32)
        whole = sum(parts[8 * i : 8 * i + 8] for i in range(PIECES))
        msg[...] = jnp.where(outer, far[...], whole) if halo is halo_b else whole


def pass_kernel(value, *refs):
    refs[-1][...] = value[...]


def wide(column):
    return jnp.broadcast_to(column, (column.shape[0], LANES))


def one_hot(position, shape, dim):
    return jnp.where(position == iota(shape, dim), 1.0, 0.0).astype(BF16)


def own_kernel(msg, cols, pick, spread, *, variables, latb, lond):
    count = msg.shape[1]
    high = latb * variables
    col = jnp.transpose(msg[...])
    cols[0] = wide(col[:, 0:1])
    cols[1] = wide(col[:, 3:4])
    cols[2] = wide(col[:, 2:3])
    cols[3] = wide(col[:, 1:2] * lond + col[:, 2:3])
    cols[4] = wide(col[:, 5:6])
    pick[...] = one_hot(col[:, 1:2], (count, high), 1)
    spread[...] = one_hot(msg[1:2], (high, count), 0)


def tables_kernel(*refs, n_msgs, variables, latb):
    own_cols, msgs = refs[0], refs[1 : 1 + n_msgs]
    keys, near, seen, spread = refs[-4:]
    count = msgs[0].shape[1]
    even = is_even("band")
    low = jnp.where(even, msgs[2][...], msgs[1][...])
    up = jnp.where(even, msgs[1][...], msgs[2][...])
    for i in range(n_msgs):
        keys[:, i * count : (i + 1) * count] = msgs[i][...]
    for j, msg in enumerate((low, up)):
        col = jnp.transpose(msg)
        for i, source in enumerate((0, 3, 2)):
            near[i, j * count : (j + 1) * count] = wide(col[:, source : source + 1])
        spread[j] = one_hot(msg[1:2], (latb * variables, count), 0)
    for j in range(3):
        block = slice((j - 1) * count, j * count)
        key = near[0, block] if j else own_cols[0]
        acc = jnp.zeros((count, LANES), F32)
        for i in range(n_msgs):
            for part in range(count // LANES):
                at = slice(part * LANES, (part + 1) * LANES)
                acc = acc + jnp.where(key == msgs[i][5:6, at], msgs[i][4:5, at], 0.0)
        seen[j * count : (j + 1) * count] = wide(jnp.sum(acc, axis=1, keepdims=True))


def network_kernel(*refs, step, rows, latb, gather):
    state, edge_a, edge_b, noise, lift, conv, head, gain_1, gain_2 = refs[:9]
    if gather:
        pick, cols, target, at_entries, firsts, lifteds, sums, parts = refs[9:]
    else:
        target, firsts, lifteds, sums = refs[9:]
    level, drift, kick = STEPS[step]
    scale = shrink(level)
    out_halo = (rows - latb) // 2
    width = state.shape[2]
    channels = lift.shape[1]
    band = lax.axis_index("band")
    north = band == 0
    south = band == lax.axis_size("band") - 1

    lane = lax.broadcasted_iota(jnp.int32, (1, LANES), 1)
    even = is_even("wt")
    from_a, from_b = edge_a[...].astype(F32), edge_b[...].astype(F32)
    right = jnp.where(even, from_a, from_b)
    left = jnp.where(even, from_b, from_a)
    edge = pltpu.roll(jnp.where(lane < HALF, right, left), HALF, 1).astype(BF16)
    edge = silu_norm(dot(edge, lift[...], 0, 0), gain_1[...])

    sub = lax.broadcasted_iota(jnp.int32, (width, 1), 0)
    def first_row(r):
        lifted = dot((state[r] * scale).astype(BF16), lift[...], 0, 0)
        if 1 <= r <= rows:
            lifteds[(r - 1) * width : r * width] = lifted
        first = silu_norm(lifted, gain_1[...])
        before, after = edge[r : r + 1], edge[HALF + r : HALF + r + 1]
        outside = None
        if r < out_halo + 1:
            outside = north
        elif r >= out_halo + 1 + latb:
            outside = south
        if outside is not None:
            first = jnp.where(outside, 0.0, first)
            before = jnp.where(outside, 0.0, before)
            after = jnp.where(outside, 0.0, after)
        here = slice(r * width, (r + 1) * width)
        firsts[here, 0:channels] = jnp.where(sub == 0, before, pltpu.roll(first, 1, 0)).astype(BF16)
        firsts[here, channels : 2 * channels] = first.astype(BF16)
        firsts[here, 2 * channels : 3 * channels] = jnp.where(
            sub == width - 1, after, pltpu.roll(first, width - 1, 0)
        ).astype(BF16)

    def mix(start, stop):
        total = lifteds[start * width : stop * width]
        for p in range(3):
            total = total + dot(
                firsts[(start + p) * width : (stop + p) * width],
                conv[3 * channels * p : 3 * channels * (p + 1)],
            )
        sums[start * width : stop * width] = total

    def finish(start, stop):
        for i in range(start, stop):
            second = silu_norm(sums[i * width : (i + 1) * width], gain_2[...]).astype(BF16)
            moved = state[i + 1] + (drift / level) * dot(head[...], second, 1, 1)
            if out_halo <= i < out_halo + latb:
                moved = moved + kick * noise[step, i - out_halo]
            target[i] = moved

    bounds = [0]
    while bounds[-1] < rows:
        bounds.append(min(rows, bounds[-1] + CHUNK))
    made = 0
    for j, (start, stop) in enumerate(zip(bounds, bounds[1:])):
        for r in range(made, stop + 2):
            first_row(r)
        made = stop + 2
        mix(start, stop)
        if j + 2 < len(bounds):
            for r in range(made, bounds[j + 2] + 2):
                first_row(r)
            made = bounds[j + 2] + 2
        if j:
            finish(bounds[j - 1], start)
    finish(bounds[-2], rows)
    if gather:
        variables = state.shape[1]
        for r in range(latb):
            for j, part in enumerate(pieces(target[out_halo + r], 2)):
                parts[r * variables : (r + 1) * variables, j * width : (j + 1) * width] = part
        picked = dot(pick[...], parts[...])
        picked = picked[:, 0:width] + picked[:, width:]
        count = pick.shape[0]
        lon = jnp.concatenate([cols[2]] * (width // LANES), axis=1)
        at = jnp.sum(jnp.where(lon == iota((count, width), 1), picked, 0.0), axis=1, keepdims=True)
        at_entries[...] = jnp.broadcast_to(at, (count, LANES))


def matching(key, keys, values):
    count = values[0].shape[1]
    acc = jnp.zeros(key.shape, F32)
    for i, row in enumerate(values):
        for part in range(count // LANES):
            at = slice(part * LANES, (part + 1) * LANES)
            known = keys[0:1, i * count + part * LANES : i * count + (part + 1) * LANES]
            acc = acc + jnp.where(key == known, row[:, at], 0.0)
    return jnp.sum(acc, axis=1, keepdims=True)


def update_kernel(*refs, step, n_msgs, rows, latb, value_row):
    target, keys, cols, spread, near, seen, near_spread = refs[:7]
    values = [ref[value_row : value_row + 1] for ref in refs[7 : 7 + n_msgs]]
    rest = refs[7 + n_msgs :]
    last = step == len(STEPS) - 1
    count = values[0].shape[1]
    variables, width = target.shape[1], target.shape[2]
    out_halo = (rows - latb) // 2
    strength = obs_precision * STEPS[step][1]

    def columns_of(j):
        if j == 0:
            return cols[0], cols[1], cols[2]
        block = slice((j - 1) * count, j * count)
        return near[0, block], near[1, block], near[2, block]

    def column(j):
        key, weight, _ = columns_of(j)
        found = matching(key, keys, values)
        return strength * weight * (seen[j * count : (j + 1) * count] - found)

    def spread_rows(j, column_j, rows_from, rows_to):
        lon = jnp.concatenate([columns_of(j)[2]] * (width // LANES), axis=1)
        tall = jnp.concatenate([column_j] * (width // LANES), axis=1)
        value = jnp.where(lon == iota((count, width), 1), tall, 0.0)
        parts = jnp.concatenate(pieces(value, 2), axis=1)
        here = slice(rows_from * variables, rows_to * variables)
        both = dot(near_spread[j - 1, here] if j else spread[here], parts)
        return both[:, 0:width] + both[:, width:]

    mine = column(0)
    own = spread_rows(0, mine, 0, latb)
    if last:
        state_out, innov_out, state, innov, sems = rest
        for r in range(latb):
            state[r] = target[out_halo + r] + own[r * variables : (r + 1) * variables]
        copies = [
            pltpu.make_async_copy(state.at[r], state_out.at[:, r, :], sems.at[r])
            for r in range(latb)
        ]
        for copy in copies:
            copy.start()
        found = matching(cols[4], keys, values)
        eye = iota((count, count), 0) == iota((count, count), 1)
        innov[...] = keys[4:5, 0:count] - jnp.sum(jnp.where(eye, found, 0.0), axis=0, keepdims=True)
        copies.append(pltpu.make_async_copy(innov, innov_out, sems.at[latb]))
        copies[-1].start()
        for copy in copies:
            copy.wait()
        return
    at_entries, halo_a, halo_b, state, edge, value = rest
    row_cell = keys[1:2, 0:count] * width + keys[2:3, 0:count]
    cell = jnp.concatenate([cols[3]] * (count // LANES), axis=1)
    tall = jnp.concatenate([mine] * (count // LANES), axis=1)
    before = jnp.concatenate([at_entries[...]] * (count // LANES), axis=1)
    eye = iota((count, count), 0) == iota((count, count), 1)
    total = jnp.where(cell == row_cell, tall, 0.0) + jnp.where(eye, before, 0.0)
    value[...] = jnp.broadcast_to(
        keys[3:4, 0:count] * jnp.sum(total, axis=0, keepdims=True), value.shape
    )
    for r in range(latb):
        state[out_halo + r] = target[out_halo + r] + own[r * variables : (r + 1) * variables]
    if out_halo:
        low = spread_rows(1, column(1), latb - out_halo, latb)
        up = spread_rows(2, column(2), 0, out_halo)
        base = sum(HALO - 1 - k for k in range(step))
        even = is_even("band")
        kick = STEPS[step][2]
        for r in range(out_halo):
            here = slice(r * variables, (r + 1) * variables)
            from_a, from_b = halo_a[base + r].astype(F32), halo_b[base + r].astype(F32)
            state[r] = target[r] + low[here] + kick * jnp.where(even, from_b, from_a)
            state[out_halo + latb + r] = (
                target[out_halo + latb + r] + up[here] + kick * jnp.where(even, from_a, from_b)
            )
    edges_into(edge, state, rows, STEPS[step + 1][0])


def swaps(count):
    first = [(i, i ^ 1) for i in range(count)]
    other = [(i, (i - 1) % count if i % 2 == 0 else (i + 1) % count) for i in range(count)]
    return first, other


def from_neighbours(block, axis):
    return [lax.ppermute(block, axis, route) for route in swaps(lax.axis_size(axis))]


def from_far(block):
    count = lax.axis_size("band")
    reach = min(2 * REACH + 1, count)
    found = []
    for distance in sorted({d % count for d in range(-reach, reach + 1)} - {0, 1, count - 1}):
        route = [(i, (i + distance) % count) for i in range(count)]
        found.append(lax.ppermute(block, "band", route))
    return found


def from_bands(block):
    return [block] + from_neighbours(block, "band") + from_far(block)


def per_device(
    prior_state, langevin_noise, station_values, entry_cell, entry_owner, entry_slot,
    entry_weight, live_counts, lift_weight, conv_weight, head_weight, first_gain, second_gain,
):
    variables, latb, lond = prior_state.shape
    count = entry_cell.shape[0]
    slots = station_values.shape[0]
    channels = lift_weight.shape[1]
    taps = conv_weight.reshape(-1, channels)
    gain_1, gain_2 = first_gain.reshape(1, -1), second_gain.reshape(1, -1)

    def row(a):
        return a.reshape(1, -1)

    entries = [
        row(entry_cell), row(entry_owner), row(entry_slot), row(entry_weight), row(station_values),
    ]
    message = ((latb + 1, variables, lond), BF16)
    prior_state, msg, copy_msg, entry_msg = vmem_call(
        functools.partial(stage_kernel, slots=slots),
        [((latb, variables, lond), F32), message, message, ((8, count), F32)],
        live_counts, prior_state, *entries,
        scalars=1,
        hbm_in=1 + len(entries),
        scratch=[pltpu.VMEM(a.shape, a.dtype) for a in entries]
        + [pltpu.SemaphoreType.DMA((latb + len(entries),))],
    )
    weights = [taps, lift_weight, head_weight.T, gain_1, gain_2]
    slabs = ((sum(HALO - 1 - k for k in range(HALO - 1)), variables, lond), BF16)
    langevin_noise, taps, lift_weight, head_weight, gain_1, gain_2, noise_a, noise_b = vmem_call(
        later_kernel,
        [((len(STEPS), latb, variables, lond), F32)]
        + [(a.shape, a.dtype) for a in weights]
        + [slabs, slabs],
        langevin_noise, *weights,
        hbm_in=1 + len(weights),
        scratch=[pltpu.SemaphoreType.DMA((len(STEPS) * latb + len(weights),))],
    )
    route_a, route_b = swaps(lax.axis_size("band"))
    near_b = [pair for pair in route_b if abs(pair[0] - pair[1]) == 1]
    far_b = [pair for pair in route_b if abs(pair[0] - pair[1]) != 1]
    halos = [lax.ppermute(msg, "band", route_a), lax.ppermute(copy_msg, "band", near_b)]
    around = lax.ppermute(entry_msg, "band", far_b)
    others = from_far(entry_msg)
    high = latb * variables
    cols, pick, spread = vmem_call(
        functools.partial(own_kernel, variables=variables, latb=latb, lond=lond),
        [((5, count, LANES), F32), ((count, high), BF16), ((high, count), BF16)],
        entry_msg,
    )
    state, edge, msg_a, msg_b = vmem_call(
        functools.partial(extend_kernel, latb=latb),
        [
            ((2 * HALO + latb, variables, lond), F32),
            ((variables, LANES), BF16),
            ((8, count), F32),
            ((8, count), F32),
        ],
        prior_state, *halos, around, noise_a, cols,
    )
    msgs = [entry_msg, msg_a, msg_b, *others]
    n_msgs = len(msgs)
    edges = from_neighbours(edge, "wt")
    (after_a,) = vmem_call(pass_kernel, [slabs], noise_a, *edges)
    noise_halos = [lax.ppermute(after_a, "band", route_a), lax.ppermute(noise_b, "band", near_b)]
    keys, near, seen, near_spread = vmem_call(
        functools.partial(tables_kernel, n_msgs=n_msgs, variables=variables, latb=latb),
        [
            ((8, n_msgs * count), F32),
            ((3, 2 * count, LANES), F32),
            ((3 * count, LANES), F32),
            ((2, high, count), BF16),
        ],
        cols, *msgs, *noise_halos,
    )
    tables = (keys, cols, spread, near, seen, near_spread)
    values, value_row = msgs, 6
    for step in range(len(STEPS)):
        last = step == len(STEPS) - 1
        rows = latb + 2 * (HALO - 1 - step)
        network_out = [((rows, variables, lond), F32)]
        network_in = [
            state, *edges, langevin_noise,
            lift_weight, taps, head_weight, gain_1, gain_2,
        ]
        scratch = [
            pltpu.VMEM(((rows + 2) * lond, 3 * channels), BF16),
            pltpu.VMEM((rows * lond, channels), F32),
            pltpu.VMEM((rows * lond, channels), F32),
        ]
        if not last:
            network_out.append(((count, LANES), F32))
            network_in += [pick, cols]
            scratch.append(pltpu.VMEM((high, 2 * lond), BF16))
        found = vmem_call(
            functools.partial(network_kernel, step=step, rows=rows, latb=latb, gather=not last),
            network_out,
            *network_in,
            scratch=scratch,
            flops=4 * rows * lond * taps.size,
        )
        update = functools.partial(
            update_kernel, step=step, n_msgs=n_msgs, rows=rows, latb=latb, value_row=value_row
        )
        if last:
            outs = [((variables, latb, lond), F32), ((1, count), F32)]
            state, innov = vmem_call(
                update, outs, found[0], *tables, *values, hbm_out=True,
                scratch=[
                    pltpu.VMEM((latb, variables, lond), F32),
                    pltpu.VMEM((1, count), F32),
                    pltpu.SemaphoreType.DMA((latb + 1,)),
                ],
            )
            return state, innov.reshape(-1)
        state, edge, value = vmem_call(
            update,
            [((rows, variables, lond), F32), ((variables, LANES), BF16), ((8, count), F32)],
            found[0], *tables, *values, found[1], *noise_halos,
        )
        values, value_row = from_bands(value), 0
        edges = from_neighbours(edge, "wt")


def solution(mesh):
    split = P(("groups", "band", "wt"))
    in_specs = (
        P("groups", "band", "wt"),
        P(None, "groups", "band", "wt"),
        split, split, split, split, split, split,
        P(), P(), P(), P(), P(),
    )
    out_specs = (P("groups", "band", "wt"), split)
    return jax.shard_map(
        per_device, mesh=mesh, in_specs=in_specs, out_specs=out_specs, check_vma=False
    )
```

```python
import functools
import math

import jax
import jax.numpy as jnp
from jax import lax
from jax.experimental import pallas as pl
from jax.experimental.pallas import tpu as pltpu
from jax.sharding import PartitionSpec as P

F32 = jnp.float32
BF16 = jnp.bfloat16
REACH = 2
LANES = 128
PIECES = 3

noise_levels = (1.0, 0.6, 0.3)
obs_precision = 4.0
step_factor = 0.1


def sub_steps():
    steps = []
    for section in range(2):
        upper, lower = noise_levels[section], noise_levels[section + 1]
        spread = upper * upper - lower * lower
        steps.append((upper, spread, math.sqrt(spread)))
        factor = step_factor * lower * lower
        steps.append((lower, factor, math.sqrt(2.0 * factor)))
    return steps


STEPS = sub_steps()


def shrink(level):
    return 1.0 / math.sqrt(1.0 + level * level)


def vmem_call(kernel, outs, *args, scratch=(), scalars=0, hbm_in=0, hbm_out=False, flops=0):
    args = list(args)
    for i in range(scalars, len(args)):
        place = pltpu.HBM if i < scalars + hbm_in else pltpu.VMEM
        args[i] = pltpu.with_memory_space_constraint(args[i], place)
    smem = pl.BlockSpec(memory_space=pltpu.SMEM)
    vmem, hbm = pl.BlockSpec(memory_space=pltpu.VMEM), pl.BlockSpec(memory_space=pltpu.HBM)
    out_type = jax.ShapeDtypeStruct if hbm_out else pltpu.VMEM
    return pl.pallas_call(
        kernel,
        out_shape=[out_type(shape, dtype) for shape, dtype in outs],
        in_specs=[smem] * scalars + [hbm] * hbm_in + [vmem] * (len(args) - scalars - hbm_in),
        out_specs=[hbm if hbm_out else vmem] * len(outs),
        scratch_shapes=list(scratch),
        cost_estimate=pl.CostEstimate(flops=flops, bytes_accessed=0, transcendentals=0),
        compiler_params=pltpu.CompilerParams(vmem_limit_bytes=48 * 2**20),
    )(*args)


def dot(a, b, ca=1, cb=0):
    return lax.dot_general(a, b, (((ca,), (cb,)), ((), ())), preferred_element_type=F32)


def pieces(x, count):
    out = []
    for _ in range(count):
        part = x.astype(BF16)
        out.append(part)
        x = x - part.astype(F32)
    return out


def iota(shape, dim):
    return lax.broadcasted_iota(jnp.int32, shape, dim).astype(F32)


def silu_norm(values, gain):
    power = jnp.mean(values * values, axis=1, keepdims=True)
    half = values * (0.5 * lax.rsqrt(power + 1e-06)) * gain
    return half + half * jnp.tanh(half)


def row_order(latb):
    return [*range(1, latb - 1), 0, latb - 1]


def is_even(axis):
    return lax.rem(lax.axis_index(axis), 2) == 0


def start_all(pairs, sems):
    copies = [
        pltpu.make_async_copy(source, target, sems.at[i])
        for i, (source, target) in enumerate(pairs)
    ]
    for copy in copies:
        copy.start()
    return copies


def rows_of(source, target):
    return [(source.at[:, r, :], target.at[r]) for r in range(target.shape[0])]


def later_kernel(noise_in, *refs):
    half = (len(refs) - 2) // 2
    noise, sems = refs[half], refs[-1]
    pairs = []
    for k in range(noise.shape[0]):
        pairs += rows_of(noise_in.at[k], noise.at[k])
    pairs += list(zip(refs[:half], refs[half + 1 : -1]))
    for copy in start_all(pairs, sems):
        copy.wait()


def stage_kernel(*refs, slots):
    live, prior_in, entries_in = refs[0], refs[1], refs[2:7]
    prior, edge, entry_msg, *entries, sems = refs[7:]
    latb, _, lond = prior.shape
    copies = start_all(rows_of(prior_in, prior) + list(zip(entries_in, entries)), sems)
    for copy in copies[:latb]:
        copy.wait()
    edges_into(edge, prior, latb, STEPS[0][0])
    for copy in copies[latb:]:
        copy.wait()
    cell, owner, slot, weight, station = entries
    count = cell.shape[1]
    cells = cell[...]
    lon = cells % lond
    row = (cells // lond) % latb
    row = jnp.where(row == 0, latb - 2, jnp.where(row == latb - 1, row, row - 1))
    variable = cells // (lond * latb)
    rv = row * prior.shape[1] + variable
    key = owner[...] * slots + slot[...]
    alive = lax.broadcasted_iota(jnp.int32, (1, count), 1) < live[0]
    weights = jnp.where(alive, weight[...], 0.0)
    mine = lax.axis_index("band") * slots + lax.broadcasted_iota(jnp.int32, (1, count), 1)
    entry_msg[0:1] = key.astype(F32)
    entry_msg[1:2] = rv.astype(F32)
    entry_msg[2:3] = lon.astype(F32)
    entry_msg[3:4] = weights
    entry_msg[4:5] = station[...]
    entry_msg[5:6] = mine.astype(F32)
    entry_msg[6:8] = jnp.zeros((2, count), F32)
    columns = jnp.transpose(entry_msg[...])
    rv_col, lon_col = columns[:, 1:2], columns[:, 2:3]
    one_hot = jnp.where(rv_col == iota((count, latb * prior.shape[1]), 1), 1.0, 0.0).astype(BF16)
    current = jnp.concatenate([prior[r] for r in row_order(latb)], axis=0)
    picked = sum(dot(one_hot, part) for part in pieces(current, 2))
    at = jnp.sum(jnp.where(lon_col == iota((count, lond), 1), picked, 0.0), axis=1, keepdims=True)
    eye = iota((count, count), 0) == iota((count, count), 1)
    entry_msg[6:7] = weights * jnp.sum(jnp.where(eye, at, 0.0), axis=0, keepdims=True)


def edges_into(edge_ref, state, rows, level):
    lane = lax.broadcasted_iota(jnp.int32, (1, LANES), 1)
    variables, width = state.shape[1:]
    edge = jnp.zeros((variables, LANES), F32)
    for r in range(rows):
        slab = state[r]
        edge = jnp.where(lane == r, slab[:, 0:1], edge)
        edge = jnp.where(lane == rows + r, slab[:, width - 1 : width], edge)
    edge = (edge * shrink(level)).astype(BF16).astype(F32)
    edge_ref[...] = jnp.transpose(jnp.concatenate([edge] * (LANES // variables), axis=0))[0 : 2 * rows]


def from_sides(axis, from_a, from_b):
    even = is_even(axis)
    return jnp.where(even, from_b, from_a), jnp.where(even, from_a, from_b)


def message_kernel(state, edge_a, edge_b, value, msg_a, msg_b, *, level, used):
    latb, variables, width = state.shape
    even = is_even("band")
    left, right = from_sides("wt", edge_a[...], edge_b[...])
    parts = [part.astype(F32) for part in pieces(value[0:used], PIECES)]
    padding = jnp.zeros((msg_a.shape[0] - variables - PIECES * used - 1, width), F32)
    below, above = [
        jnp.concatenate(
            [
                state[r] * shrink(level),
                *parts,
                jnp.concatenate([left[latb + r : latb + r + 1], right[r : r + 1]], axis=1),
                padding,
            ],
            axis=0,
        )
        for r in (0, latb - 1)
    ]
    msg_a[...] = jnp.where(even, above, below).astype(BF16)
    msg_b[...] = jnp.where(even, below, above).astype(BF16)


def unpacked(msg, variables, used):
    packed = msg[variables:].astype(F32)
    return sum(packed[used * i : used * (i + 1)] for i in range(PIECES))


def wide(column):
    return jnp.broadcast_to(column, (column.shape[0], LANES))


def one_hot(position, shape, dim):
    return jnp.where(position == iota(shape, dim), 1.0, 0.0).astype(BF16)


def own_kernel(msg, cols, pick, spread, *, variables, latb, lond):
    count = msg.shape[1]
    high = latb * variables
    col = jnp.transpose(msg[...])
    cols[0] = wide(col[:, 0:1])
    cols[1] = wide(col[:, 3:4])
    cols[2] = wide(col[:, 2:3])
    cols[3] = wide(col[:, 1:2] * lond + col[:, 2:3])
    cols[4] = wide(col[:, 5:6])
    pick[...] = one_hot(col[:, 1:2], (count, high), 1)
    spread[...] = one_hot(msg[1:2], (high, count), 0)


def tables_kernel(cols, own, msg_a, msg_b, *refs, variables):
    far, keys, seen = refs[:-2], refs[-2], refs[-1]
    count = own.shape[1]
    msgs = [own[...], *(unpacked(msg, variables, 8) for msg in (msg_a, msg_b))]
    msgs += [ref[...] for ref in far]
    for i, msg in enumerate(msgs):
        keys[:, i * count : (i + 1) * count] = msg
    acc = jnp.zeros((count, LANES), F32)
    for msg in msgs:
        for part in range(count // LANES):
            at = slice(part * LANES, (part + 1) * LANES)
            acc = acc + jnp.where(cols[0] == msg[5:6, at], msg[4:5, at], 0.0)
    seen[...] = wide(jnp.sum(acc, axis=1, keepdims=True))


def first_row(scaled, before, after, lift, gain):
    lifted = dot(scaled, lift[...], 0, 0)
    first = silu_norm(lifted, gain[...])
    width = first.shape[0]
    sub = lax.broadcasted_iota(jnp.int32, (width, 1), 0)
    shifted = [
        jnp.where(sub == 0, before, pltpu.roll(first, 1, 0)),
        first,
        jnp.where(sub == width - 1, after, pltpu.roll(first, width - 1, 0)),
    ]
    return lifted, [x.astype(BF16) for x in shifted]


def picked_from(rows, pick, lon, parts):
    variables, width = rows[0].shape
    for r, row in enumerate(rows):
        for j, part in enumerate(pieces(row, 2)):
            parts[r * variables : (r + 1) * variables, j * width : (j + 1) * width] = part
    picked = dot(pick, parts[...])
    picked = picked[:, 0:width] + picked[:, width:]
    lons = jnp.concatenate([lon] * (width // LANES), axis=1)
    spots = jnp.where(lons == iota((lon.shape[0], width), 1), picked, 0.0)
    return wide(jnp.sum(spots, axis=1, keepdims=True))


def inner_kernel(
    state, edge_a, edge_b, noise, lift, conv, head, gain_1, gain_2, pick, cols,
    middle, sums, at_entries, firsts, total, parts, *, step,
):
    level, drift, kick = STEPS[step]
    latb, _, width = state.shape
    channels = lift.shape[1]
    variables = state.shape[1]
    left, right = from_sides("wt", edge_a[...], edge_b[...])
    edge = jnp.concatenate([left, right], axis=0)[:, 0:variables].astype(BF16)
    edge = silu_norm(dot(edge, lift[...]), gain_1[...])
    for r in range(latb):
        lifted, shifted = first_row(
            (state[r] * shrink(level)).astype(BF16),
            edge[latb + r : latb + r + 1], edge[2 * latb + r : 2 * latb + r + 1], lift, gain_1,
        )
        here = slice(r * width, (r + 1) * width)
        total[here] = lifted
        for q in range(3):
            firsts[here, q * channels : (q + 1) * channels] = shifted[q]
    deep = 3 * channels
    inside = (latb - 1) * width
    total[...] += dot(firsts[...], conv[deep : 2 * deep])
    total[width:] += dot(firsts[0:inside], conv[0:deep])
    total[0:inside] += dot(firsts[width:], conv[2 * deep :])
    sums[0] = total[0:width]
    sums[1] = total[inside:]
    for r in range(1, latb - 1):
        second = silu_norm(total[r * width : (r + 1) * width], gain_2[...]).astype(BF16)
        score = dot(head[...], second, 1, 1)
        middle[r - 1] = state[r] + (drift / level) * score + kick * noise[step, r]
    done = (latb - 2) * variables
    at_entries[...] = picked_from(
        [middle[r] for r in range(latb - 2)], pick[:, 0:done], cols[2], parts
    )


def outer_kernel(*refs, step, gather, used):
    state, msg_a, msg_b, middle, sums, noise, lift, conv, head, gain_1, gain_2 = refs[:11]
    if gather:
        pick, cols, before, target, at_entries, parts = refs[11:]
    else:
        (target,) = refs[11:]
    level, drift, kick = STEPS[step]
    latb, variables, width = state.shape
    channels = lift.shape[1]
    deep = 3 * channels
    band = lax.axis_index("band")
    beyond = (band == 0, band == lax.axis_size("band") - 1)
    near = from_sides("band", msg_a[...].astype(F32), msg_b[...].astype(F32))
    spot = variables + PIECES * used
    corner = [side[spot : spot + 1, at : at + LANES] for side in near for at in (0, LANES)]
    corner = jnp.concatenate([*corner, jnp.zeros((12, LANES), F32)], axis=0)
    edge = silu_norm(dot(corner[:, 0:variables].astype(BF16), lift[...]), gain_1[...])
    for r in range(1, latb - 1):
        target[r] = middle[r - 1]
    for i, (r, p) in enumerate(((0, 0), (latb - 1, 2))):
        _, shifted = first_row(
            near[i][0:variables].astype(BF16),
            edge[2 * i : 2 * i + 1], edge[2 * i + 1 : 2 * i + 2], lift, gain_1,
        )
        first = jnp.where(beyond[i], 0.0, jnp.concatenate(shifted, axis=1).astype(F32)).astype(BF16)
        mixed = sums[i] + dot(first, conv[p * deep : (p + 1) * deep])
        second = silu_norm(mixed, gain_2[...]).astype(BF16)
        score = dot(head[...], second, 1, 1)
        target[r] = state[r] + (drift / level) * score + kick * noise[step, r]
    if gather:
        done = (latb - 2) * variables
        at_entries[...] = before[...] + picked_from(
            [target[0], target[latb - 1]], pick[:, done:], cols[2], parts
        )


def matching(key, keys, values):
    count = values[0].shape[1]
    acc = jnp.zeros(key.shape, F32)
    for i, row in enumerate(values):
        for part in range(count // LANES):
            at = slice(part * LANES, (part + 1) * LANES)
            known = keys[0:1, i * count + part * LANES : i * count + (part + 1) * LANES]
            acc = acc + jnp.where(key == known, row[:, at], 0.0)
    return jnp.sum(acc, axis=1, keepdims=True)


def update_kernel(*refs, step, n_far, value_row, used):
    target, keys, cols, spread, seen, own, msg_a, msg_b = refs[:8]
    far, rest = refs[8 : 8 + n_far], refs[8 + n_far :]
    here = slice(value_row, value_row + 1)
    count = own.shape[1]
    latb, variables, width = target.shape
    values = [own[here], *(unpacked(msg, variables, used)[here] for msg in (msg_a, msg_b))]
    values += [ref[here] for ref in far]
    found = matching(cols[0], keys, values)
    mine = obs_precision * STEPS[step][1] * cols[1] * (seen[...] - found)
    lon = jnp.concatenate([cols[2]] * (width // LANES), axis=1)
    tall = jnp.concatenate([mine] * (width // LANES), axis=1)
    spots = jnp.where(lon == iota((count, width), 1), tall, 0.0)
    both = dot(spread[...], jnp.concatenate(pieces(spots, 2), axis=1))
    added = both[:, 0:width] + both[:, width:]
    place = {r: slice(i * variables, (i + 1) * variables) for i, r in enumerate(row_order(latb))}
    eye = iota((count, count), 0) == iota((count, count), 1)
    if step == len(STEPS) - 1:
        state_out, innov_out, state, innov, sems = rest
        for r in range(latb):
            state[r] = target[r] + added[place[r]]
        copies = [
            pltpu.make_async_copy(state.at[r], state_out.at[:, r, :], sems.at[r])
            for r in range(latb)
        ]
        for copy in copies:
            copy.start()
        found = matching(cols[4], keys, values)
        innov[...] = keys[4:5, 0:count] - jnp.sum(jnp.where(eye, found, 0.0), axis=0, keepdims=True)
        copies.append(pltpu.make_async_copy(innov, innov_out, sems.at[latb]))
        copies[-1].start()
        for copy in copies:
            copy.wait()
        return
    at_entries, state, edge, value = rest
    for r in range(latb):
        state[r] = target[r] + added[place[r]]
    edges_into(edge, state, latb, STEPS[step + 1][0])
    row_cell = keys[1:2, 0:count] * width + keys[2:3, 0:count]
    cell = jnp.concatenate([cols[3]] * (count // LANES), axis=1)
    tall = jnp.concatenate([mine] * (count // LANES), axis=1)
    before = jnp.concatenate([at_entries[...]] * (count // LANES), axis=1)
    total = jnp.where(cell == row_cell, tall, 0.0) + jnp.where(eye, before, 0.0)
    value[...] = jnp.broadcast_to(
        keys[3:4, 0:count] * jnp.sum(total, axis=0, keepdims=True), value.shape
    )


def swaps(count):
    first = [(i, i ^ 1) for i in range(count)]
    other = [(i, (i - 1) % count if i % 2 == 0 else (i + 1) % count) for i in range(count)]
    return first, other


def from_neighbours(block, axis):
    return [lax.ppermute(block, axis, route) for route in swaps(lax.axis_size(axis))]


def from_far(block):
    count = lax.axis_size("band")
    reach = min(2 * REACH, count)
    found = []
    for distance in sorted({d % count for d in range(-reach, reach + 1)} - {0, 1, count - 1}):
        route = [(i, (i + distance) % count) for i in range(count)]
        found.append(lax.ppermute(block, "band", route))
    return found


def per_device(
    prior_state, langevin_noise, station_values, entry_cell, entry_owner, entry_slot,
    entry_weight, live_counts, lift_weight, conv_weight, head_weight, first_gain, second_gain,
):
    variables, latb, lond = prior_state.shape
    count = entry_cell.shape[0]
    slots = station_values.shape[0]
    channels = lift_weight.shape[1]
    taps = conv_weight.reshape(-1, channels)
    gain_1, gain_2 = first_gain.reshape(1, -1), second_gain.reshape(1, -1)

    def row(a):
        return a.reshape(1, -1)

    entries = [
        row(entry_cell), row(entry_owner), row(entry_slot), row(entry_weight), row(station_values),
    ]
    state, edge, value = vmem_call(
        functools.partial(stage_kernel, slots=slots),
        [((latb, variables, lond), F32), ((2 * latb, LANES), F32), ((8, count), F32)],
        live_counts, prior_state, *entries,
        scalars=1,
        hbm_in=1 + len(entries),
        scratch=[pltpu.VMEM(a.shape, a.dtype) for a in entries]
        + [pltpu.SemaphoreType.DMA((latb + len(entries),))],
    )
    weights = [taps, lift_weight, head_weight.T, gain_1, gain_2]
    noise, taps, *weights = vmem_call(
        later_kernel,
        [((len(STEPS), latb, variables, lond), F32)] + [(a.shape, a.dtype) for a in weights],
        langevin_noise, *weights,
        hbm_in=1 + len(weights),
        scratch=[pltpu.SemaphoreType.DMA((len(STEPS) * latb + len(weights),))],
    )
    weights = [weights[0], taps, *weights[1:]]
    high = latb * variables
    cols, pick, spread = vmem_call(
        functools.partial(own_kernel, variables=variables, latb=latb, lond=lond),
        [((5, count, LANES), F32), ((count, high), BF16), ((high, count), BF16)],
        value,
    )
    route_a, route_b = swaps(lax.axis_size("band"))
    whole = ((latb, variables, lond), F32)
    value_row, used = 6, 8
    for step in range(len(STEPS)):
        last = step == len(STEPS) - 1
        far = from_far(value)
        edges = from_neighbours(edge, "wt")
        msg_a, msg_b = vmem_call(
            functools.partial(message_kernel, level=STEPS[step][0], used=used),
            [((variables + (32 if used == 8 else 16), lond), BF16)] * 2,
            state, *edges, value,
        )
        msg_a, msg_b = lax.ppermute(msg_a, "band", route_a), lax.ppermute(msg_b, "band", route_b)
        middle, sums, before = vmem_call(
            functools.partial(inner_kernel, step=step),
            [
                ((latb - 2, variables, lond), F32),
                ((2, lond, channels), F32),
                ((count, LANES), F32),
            ],
            state, *edges, noise, *weights, pick, cols,
            scratch=[
                pltpu.VMEM((latb * lond, 3 * channels), BF16),
                pltpu.VMEM((latb * lond, channels), F32),
                pltpu.VMEM(((latb - 2) * variables, 2 * lond), BF16),
            ],
            flops=4 * latb * lond * taps.size,
        )
        if step == 0:
            keys, seen = vmem_call(
                functools.partial(tables_kernel, variables=variables),
                [((8, (3 + len(far)) * count), F32), ((count, LANES), F32)],
                cols, value, msg_a, msg_b, *far,
            )
        outer_in = [state, msg_a, msg_b, middle, sums, noise, *weights]
        outer = functools.partial(outer_kernel, step=step, gather=not last, used=used)
        update = functools.partial(
            update_kernel, step=step, n_far=len(far), value_row=value_row, used=used
        )
        given = [keys, cols, spread, seen, value, msg_a, msg_b, *far]
        if last:
            (target,) = vmem_call(outer, [whole], *outer_in)
            state, innov = vmem_call(
                update, [((variables, latb, lond), F32), ((1, count), F32)], target, *given,
                hbm_out=True,
                scratch=[
                    pltpu.VMEM(*whole),
                    pltpu.VMEM((1, count), F32),
                    pltpu.SemaphoreType.DMA((latb + 1,)),
                ],
            )
            return state, innov.reshape(-1)
        target, at_entries = vmem_call(
            outer, [whole, ((count, LANES), F32)], *outer_in, pick, cols, before,
            scratch=[pltpu.VMEM((2 * variables, 2 * lond), BF16)],
        )
        state, edge, value = vmem_call(
            update, [whole, ((2 * latb, LANES), F32), ((8, count), F32)],
            target, *given, at_entries,
        )
        value_row, used = 0, 1


def solution(mesh):
    split = P(("groups", "band", "wt"))
    in_specs = (
        P("groups", "band", "wt"),
        P(None, "groups", "band", "wt"),
        split, split, split, split, split, split,
        P(), P(), P(), P(), P(),
    )
    out_specs = (P("groups", "band", "wt"), split)
    return jax.shard_map(
        per_device, mesh=mesh, in_specs=in_specs, out_specs=out_specs, check_vma=False
    )
```

```python
import functools
import math

import jax
import jax.numpy as jnp
from jax import lax
from jax.experimental import pallas as pl
from jax.experimental.pallas import tpu as pltpu
from jax.sharding import PartitionSpec as P

F32 = jnp.float32
BF16 = jnp.bfloat16
REACH = 2
LANES = 128
PIECES = 3

noise_levels = (1.0, 0.6, 0.3)
obs_precision = 4.0
step_factor = 0.1


def sub_steps():
    steps = []
    for section in range(2):
        upper, lower = noise_levels[section], noise_levels[section + 1]
        spread = upper * upper - lower * lower
        steps.append((upper, spread, math.sqrt(spread)))
        factor = step_factor * lower * lower
        steps.append((lower, factor, math.sqrt(2.0 * factor)))
    return steps


STEPS = sub_steps()


def shrink(level):
    return 1.0 / math.sqrt(1.0 + level * level)


def vmem_call(kernel, outs, *args, scratch=(), scalars=0, hbm_in=0, hbm_out=False, flops=0):
    args = list(args)
    for i in range(scalars, len(args)):
        place = pltpu.HBM if i < scalars + hbm_in else pltpu.VMEM
        args[i] = pltpu.with_memory_space_constraint(args[i], place)
    smem = pl.BlockSpec(memory_space=pltpu.SMEM)
    vmem, hbm = pl.BlockSpec(memory_space=pltpu.VMEM), pl.BlockSpec(memory_space=pltpu.HBM)
    out_type = jax.ShapeDtypeStruct if hbm_out else pltpu.VMEM
    return pl.pallas_call(
        kernel,
        out_shape=[out_type(shape, dtype) for shape, dtype in outs],
        in_specs=[smem] * scalars + [hbm] * hbm_in + [vmem] * (len(args) - scalars - hbm_in),
        out_specs=[hbm if hbm_out else vmem] * len(outs),
        scratch_shapes=list(scratch),
        cost_estimate=pl.CostEstimate(flops=flops, bytes_accessed=0, transcendentals=0),
        compiler_params=pltpu.CompilerParams(vmem_limit_bytes=48 * 2**20),
    )(*args)


def dot(a, b, ca=1, cb=0):
    return lax.dot_general(a, b, (((ca,), (cb,)), ((), ())), preferred_element_type=F32)


def pieces(x, count):
    out = []
    for _ in range(count):
        part = x.astype(BF16)
        out.append(part)
        x = x - part.astype(F32)
    return out


def iota(shape, dim):
    return lax.broadcasted_iota(jnp.int32, shape, dim).astype(F32)


def silu_norm(values, gain):
    power = jnp.mean(values * values, axis=1, keepdims=True)
    half = values * (0.5 * lax.rsqrt(power + 1e-06)) * gain
    return half + half * jnp.tanh(half)


def row_order(latb):
    return [*range(1, latb - 1), 0, latb - 1]


def is_even(axis):
    return lax.rem(lax.axis_index(axis), 2) == 0


def start_all(pairs, sems):
    copies = [
        pltpu.make_async_copy(source, target, sems.at[i])
        for i, (source, target) in enumerate(pairs)
    ]
    for copy in copies:
        copy.start()
    return copies


def rows_of(source, target):
    return [(source.at[:, r, :], target.at[r]) for r in range(target.shape[0])]


def later_kernel(noise_in, *refs):
    half = (len(refs) - 2) // 2
    noise, sems = refs[half], refs[-1]
    pairs = []
    for k in range(noise.shape[0]):
        pairs += rows_of(noise_in.at[k], noise.at[k])
    pairs += list(zip(refs[:half], refs[half + 1 : -1]))
    for copy in start_all(pairs, sems):
        copy.wait()


def stage_kernel(*refs, slots):
    live, prior_in, entries_in = refs[0], refs[1], refs[2:7]
    prior, edge, entry_msg, *entries, sems = refs[7:]
    latb, _, lond = prior.shape
    copies = start_all(rows_of(prior_in, prior) + list(zip(entries_in, entries)), sems)
    for copy in copies[:latb]:
        copy.wait()
    edges_into(edge, prior, latb, STEPS[0][0])
    for copy in copies[latb:]:
        copy.wait()
    cell, owner, slot, weight, station = entries
    count = cell.shape[1]
    cells = cell[...]
    lon = cells % lond
    row = (cells // lond) % latb
    row = jnp.where(row == 0, latb - 2, jnp.where(row == latb - 1, row, row - 1))
    variable = cells // (lond * latb)
    rv = row * prior.shape[1] + variable
    key = owner[...] * slots + slot[...]
    alive = lax.broadcasted_iota(jnp.int32, (1, count), 1) < live[0]
    weights = jnp.where(alive, weight[...], 0.0)
    mine = lax.axis_index("band") * slots + lax.broadcasted_iota(jnp.int32, (1, count), 1)
    entry_msg[0:1] = key.astype(F32)
    entry_msg[1:2] = rv.astype(F32)
    entry_msg[2:3] = lon.astype(F32)
    entry_msg[3:4] = weights
    entry_msg[4:5] = station[...]
    entry_msg[5:6] = mine.astype(F32)
    entry_msg[6:8] = jnp.zeros((2, count), F32)
    columns = jnp.transpose(entry_msg[...])
    rv_col, lon_col = columns[:, 1:2], columns[:, 2:3]
    one_hot = jnp.where(rv_col == iota((count, latb * prior.shape[1]), 1), 1.0, 0.0).astype(BF16)
    current = jnp.concatenate([prior[r] for r in row_order(latb)], axis=0)
    picked = sum(dot(one_hot, part) for part in pieces(current, 2))
    at = jnp.sum(jnp.where(lon_col == iota((count, lond), 1), picked, 0.0), axis=1, keepdims=True)
    eye = iota((count, count), 0) == iota((count, count), 1)
    entry_msg[6:7] = weights * jnp.sum(jnp.where(eye, at, 0.0), axis=0, keepdims=True)


def edges_into(edge_ref, state, rows, level):
    lane = lax.broadcasted_iota(jnp.int32, (1, LANES), 1)
    variables, width = state.shape[1:]
    edge = jnp.zeros((variables, LANES), F32)
    for r in range(rows):
        slab = state[r]
        edge = jnp.where(lane == r, slab[:, 0:1], edge)
        edge = jnp.where(lane == rows + r, slab[:, width - 1 : width], edge)
    edge = (edge * shrink(level)).astype(BF16).astype(F32)
    edge_ref[...] = jnp.transpose(jnp.concatenate([edge] * (LANES // variables), axis=0))[0 : 2 * rows]


def from_sides(axis, from_a, from_b):
    even = is_even(axis)
    return jnp.where(even, from_b, from_a), jnp.where(even, from_a, from_b)


def message_kernel(state, edge_a, edge_b, value, msg_a, msg_b, *, level, used):
    latb, variables, width = state.shape
    even = is_even("band")
    left, right = from_sides("wt", edge_a[...], edge_b[...])
    parts = [part.astype(F32) for part in pieces(value[0:used], PIECES)]
    padding = jnp.zeros((msg_a.shape[0] - variables - PIECES * used - 1, width), F32)
    below, above = [
        jnp.concatenate(
            [
                state[r] * shrink(level),
                *parts,
                jnp.concatenate([left[latb + r : latb + r + 1], right[r : r + 1]], axis=1),
                padding,
            ],
            axis=0,
        )
        for r in (0, latb - 1)
    ]
    msg_a[...] = jnp.where(even, above, below).astype(BF16)
    msg_b[...] = jnp.where(even, below, above).astype(BF16)


def unpacked(msg, variables, used):
    packed = msg[variables:].astype(F32)
    return sum(packed[used * i : used * (i + 1)] for i in range(PIECES))


def wide(column):
    return jnp.broadcast_to(column, (column.shape[0], LANES))


def one_hot(position, shape, dim):
    return jnp.where(position == iota(shape, dim), 1.0, 0.0).astype(BF16)


def own_kernel(msg, cols, pick, spread, *, variables, latb, lond):
    count = msg.shape[1]
    high = latb * variables
    col = jnp.transpose(msg[...])
    cols[0] = wide(col[:, 0:1])
    cols[1] = wide(col[:, 3:4])
    cols[2] = wide(col[:, 2:3])
    cols[3] = wide(col[:, 1:2] * lond + col[:, 2:3])
    cols[4] = wide(col[:, 5:6])
    pick[...] = one_hot(col[:, 1:2], (count, high), 1)
    spread[...] = one_hot(msg[1:2], (high, count), 0)


def tables_kernel(cols, own, msg_a, msg_b, *refs, variables):
    far, keys, seen = refs[:-2], refs[-2], refs[-1]
    count = own.shape[1]
    msgs = [own[...], *(unpacked(msg, variables, 8) for msg in (msg_a, msg_b))]
    msgs += [ref[...] for ref in far]
    for i, msg in enumerate(msgs):
        keys[:, i * count : (i + 1) * count] = msg
    acc = jnp.zeros((count, LANES), F32)
    for msg in msgs:
        for part in range(count // LANES):
            at = slice(part * LANES, (part + 1) * LANES)
            acc = acc + jnp.where(cols[0] == msg[5:6, at], msg[4:5, at], 0.0)
    seen[...] = wide(jnp.sum(acc, axis=1, keepdims=True))


def first_row(scaled, before, after, lift, gain):
    lifted = dot(scaled, lift[...], 0, 0)
    first = silu_norm(lifted, gain[...])
    width = first.shape[0]
    sub = lax.broadcasted_iota(jnp.int32, (width, 1), 0)
    shifted = [
        jnp.where(sub == 0, before, pltpu.roll(first, 1, 0)),
        first,
        jnp.where(sub == width - 1, after, pltpu.roll(first, width - 1, 0)),
    ]
    return lifted, [x.astype(BF16) for x in shifted]


def inner_kernel(
    state, edge_a, edge_b, noise, lift, conv, head, gain_1, gain_2,
    middle, sums, firsts, total, *, step,
):
    level, drift, kick = STEPS[step]
    latb, _, width = state.shape
    channels = lift.shape[1]
    variables = state.shape[1]
    left, right = from_sides("wt", edge_a[...], edge_b[...])
    edge = jnp.concatenate([left, right], axis=0)[:, 0:variables].astype(BF16)
    edge = silu_norm(dot(edge, lift[...]), gain_1[...])
    for r in range(latb):
        lifted, shifted = first_row(
            (state[r] * shrink(level)).astype(BF16),
            edge[latb + r : latb + r + 1], edge[2 * latb + r : 2 * latb + r + 1], lift, gain_1,
        )
        here = slice(r * width, (r + 1) * width)
        total[here] = lifted
        for q in range(3):
            firsts[here, q * channels : (q + 1) * channels] = shifted[q]
    deep = 3 * channels
    inside = (latb - 1) * width
    total[...] += dot(firsts[...], conv[deep : 2 * deep])
    total[width:] += dot(firsts[0:inside], conv[0:deep])
    total[0:inside] += dot(firsts[width:], conv[2 * deep :])
    sums[0] = total[0:width]
    sums[1] = total[inside:]
    for r in range(1, latb - 1):
        second = silu_norm(total[r * width : (r + 1) * width], gain_2[...]).astype(BF16)
        score = dot(head[...], second, 1, 1)
        middle[r - 1] = state[r] + (drift / level) * score + kick * noise[step, r]


def value_kernel(state, keys, cols, pick, value, parts):
    latb, variables, width = state.shape
    count = pick.shape[0]
    for i, r in enumerate(row_order(latb)):
        for j, part in enumerate(pieces(state[r], 2)):
            parts[i * variables : (i + 1) * variables, j * width : (j + 1) * width] = part
    picked = dot(pick[...], parts[...])
    picked = picked[:, 0:width] + picked[:, width:]
    lon = jnp.concatenate([cols[2]] * (width // LANES), axis=1)
    spots = jnp.where(lon == iota((count, width), 1), picked, 0.0)
    at = jnp.sum(spots, axis=1, keepdims=True)
    eye = iota((count, count), 0) == iota((count, count), 1)
    row = keys[3:4, 0:count] * jnp.sum(jnp.where(eye, at, 0.0), axis=0, keepdims=True)
    value[...] = jnp.broadcast_to(row, value.shape)


def matching(key, keys, values):
    count = values[0].shape[1]
    acc = jnp.zeros(key.shape, F32)
    for i, row in enumerate(values):
        for part in range(count // LANES):
            at = slice(part * LANES, (part + 1) * LANES)
            known = keys[0:1, i * count + part * LANES : i * count + (part + 1) * LANES]
            acc = acc + jnp.where(key == known, row[:, at], 0.0)
    return jnp.sum(acc, axis=1, keepdims=True)


def update_kernel(*refs, step, n_far, value_row, used):
    state, middle, sums, noise, lift, conv, head, gain_1, gain_2 = refs[:9]
    keys, cols, spread, seen, own, msg_a, msg_b = refs[9:16]
    far, rest = refs[16 : 16 + n_far], refs[16 + n_far :]
    level, drift, kick = STEPS[step]
    latb, variables, width = state.shape
    deep = 3 * lift.shape[1]
    count = own.shape[1]

    near = from_sides("band", msg_a[...].astype(F32), msg_b[...].astype(F32))
    spot = variables + PIECES * used
    corner = [side[spot : spot + 1, at : at + LANES] for side in near for at in (0, LANES)]
    corner = jnp.concatenate([*corner, jnp.zeros((12, LANES), F32)], axis=0)
    edge = silu_norm(dot(corner[:, 0:variables].astype(BF16), lift[...]), gain_1[...])

    here = slice(value_row, value_row + 1)
    values = [own[here], *(unpacked(msg, variables, used)[here] for msg in (msg_a, msg_b))]
    values += [ref[here] for ref in far]
    found = matching(cols[0], keys, values)
    mine = obs_precision * drift * cols[1] * (seen[...] - found)
    lon = jnp.concatenate([cols[2]] * (width // LANES), axis=1)
    tall = jnp.concatenate([mine] * (width // LANES), axis=1)
    spots = jnp.where(lon == iota((count, width), 1), tall, 0.0)
    both = dot(spread[...], jnp.concatenate(pieces(spots, 2), axis=1))
    added = both[:, 0:width] + both[:, width:]
    place = {r: slice(i * variables, (i + 1) * variables) for i, r in enumerate(row_order(latb))}
    moved = {r: middle[r - 1] + added[place[r]] for r in range(1, latb - 1)}

    band = lax.axis_index("band")
    beyond = (band == 0, band == lax.axis_size("band") - 1)
    for i, (r, p) in enumerate(((0, 0), (latb - 1, 2))):
        _, shifted = first_row(
            near[i][0:variables].astype(BF16),
            edge[2 * i : 2 * i + 1], edge[2 * i + 1 : 2 * i + 2], lift, gain_1,
        )
        first = jnp.where(beyond[i], 0.0, jnp.concatenate(shifted, axis=1).astype(F32)).astype(BF16)
        mixed = sums[i] + dot(first, conv[p * deep : (p + 1) * deep])
        second = silu_norm(mixed, gain_2[...]).astype(BF16)
        score = dot(head[...], second, 1, 1)
        moved[r] = state[r] + (drift / level) * score + kick * noise[step, r] + added[place[r]]

    if step < len(STEPS) - 1:
        after, border = rest
        for r in range(latb):
            after[r] = moved[r]
        edges_into(border, after, latb, STEPS[step + 1][0])
        return
    state_out, innov_out, after, innov, sems = rest
    found = matching(cols[4], keys, values)
    eye = iota((count, count), 0) == iota((count, count), 1)
    innov[...] = keys[4:5, 0:count] - jnp.sum(jnp.where(eye, found, 0.0), axis=0, keepdims=True)
    copies = [pltpu.make_async_copy(innov, innov_out, sems.at[latb])]
    copies[0].start()
    for r in row_order(latb):
        after[r] = moved[r]
        copies.append(pltpu.make_async_copy(after.at[r], state_out.at[:, r, :], sems.at[r]))
        copies[-1].start()
    for copy in copies:
        copy.wait()


def swaps(count):
    first = [(i, i ^ 1) for i in range(count)]
    other = [(i, (i - 1) % count if i % 2 == 0 else (i + 1) % count) for i in range(count)]
    return first, other


def from_neighbours(block, axis):
    return [lax.ppermute(block, axis, route) for route in swaps(lax.axis_size(axis))]


def from_far(block):
    count = lax.axis_size("band")
    reach = min(2 * REACH, count)
    found = []
    for distance in sorted({d % count for d in range(-reach, reach + 1)} - {0, 1, count - 1}):
        route = [(i, (i + distance) % count) for i in range(count)]
        found.append(lax.ppermute(block, "band", route))
    return found


def per_device(
    prior_state, langevin_noise, station_values, entry_cell, entry_owner, entry_slot,
    entry_weight, live_counts, lift_weight, conv_weight, head_weight, first_gain, second_gain,
):
    variables, latb, lond = prior_state.shape
    count = entry_cell.shape[0]
    slots = station_values.shape[0]
    channels = lift_weight.shape[1]
    taps = conv_weight.reshape(-1, channels)
    gain_1, gain_2 = first_gain.reshape(1, -1), second_gain.reshape(1, -1)

    def row(a):
        return a.reshape(1, -1)

    entries = [
        row(entry_cell), row(entry_owner), row(entry_slot), row(entry_weight), row(station_values),
    ]
    state, edge, value = vmem_call(
        functools.partial(stage_kernel, slots=slots),
        [((latb, variables, lond), F32), ((2 * latb, LANES), F32), ((8, count), F32)],
        live_counts, prior_state, *entries,
        scalars=1,
        hbm_in=1 + len(entries),
        scratch=[pltpu.VMEM(a.shape, a.dtype) for a in entries]
        + [pltpu.SemaphoreType.DMA((latb + len(entries),))],
    )
    weights = [taps, lift_weight, head_weight.T, gain_1, gain_2]
    noise, taps, *weights = vmem_call(
        later_kernel,
        [((len(STEPS), latb, variables, lond), F32)] + [(a.shape, a.dtype) for a in weights],
        langevin_noise, *weights,
        hbm_in=1 + len(weights),
        scratch=[pltpu.SemaphoreType.DMA((len(STEPS) * latb + len(weights),))],
    )
    weights = [weights[0], taps, *weights[1:]]
    high = latb * variables
    cols, pick, spread = vmem_call(
        functools.partial(own_kernel, variables=variables, latb=latb, lond=lond),
        [((5, count, LANES), F32), ((count, high), BF16), ((high, count), BF16)],
        value,
    )
    route_a, route_b = swaps(lax.axis_size("band"))
    whole = ((latb, variables, lond), F32)
    value_row, used = 6, 8
    for step in range(len(STEPS)):
        last = step == len(STEPS) - 1
        far = from_far(value)
        edges = from_neighbours(edge, "wt")
        msg_a, msg_b = vmem_call(
            functools.partial(message_kernel, level=STEPS[step][0], used=used),
            [((variables + (32 if used == 8 else 16), lond), BF16)] * 2,
            state, *edges, value,
        )
        msg_a, msg_b = lax.ppermute(msg_a, "band", route_a), lax.ppermute(msg_b, "band", route_b)
        middle, sums = vmem_call(
            functools.partial(inner_kernel, step=step),
            [((latb - 2, variables, lond), F32), ((2, lond, channels), F32)],
            state, *edges, noise, *weights,
            scratch=[
                pltpu.VMEM((latb * lond, 3 * channels), BF16),
                pltpu.VMEM((latb * lond, channels), F32),
            ],
            flops=4 * latb * lond * taps.size,
        )
        if step == 0:
            keys, seen = vmem_call(
                functools.partial(tables_kernel, variables=variables),
                [((8, (3 + len(far)) * count), F32), ((count, LANES), F32)],
                cols, value, msg_a, msg_b, *far,
            )
        update = functools.partial(
            update_kernel, step=step, n_far=len(far), value_row=value_row, used=used
        )
        given = [state, middle, sums, noise, *weights]
        given += [keys, cols, spread, seen, value, msg_a, msg_b, *far]
        if last:
            state, innov = vmem_call(
                update, [((variables, latb, lond), F32), ((1, count), F32)], *given,
                hbm_out=True,
                scratch=[
                    pltpu.VMEM(*whole),
                    pltpu.VMEM((1, count), F32),
                    pltpu.SemaphoreType.DMA((latb + 1,)),
                ],
            )
            return state, innov.reshape(-1)
        state, edge = vmem_call(update, [whole, ((2 * latb, LANES), F32)], *given)
        (value,) = vmem_call(
            value_kernel, [((8, count), F32)], state, keys, cols, pick,
            scratch=[pltpu.VMEM((high, 2 * lond), BF16)],
        )
        value_row, used = 0, 1


def solution(mesh):
    split = P(("groups", "band", "wt"))
    in_specs = (
        P("groups", "band", "wt"),
        P(None, "groups", "band", "wt"),
        split, split, split, split, split, split,
        P(), P(), P(), P(), P(),
    )
    out_specs = (P("groups", "band", "wt"), split)
    return jax.shard_map(
        per_device, mesh=mesh, in_specs=in_specs, out_specs=out_specs, check_vma=False
    )
```

```python
import functools
import math

import jax
import jax.numpy as jnp
from jax import lax
from jax.experimental import pallas as pl
from jax.experimental.pallas import tpu as pltpu
from jax.sharding import PartitionSpec as P

F32 = jnp.float32
BF16 = jnp.bfloat16
REACH = 2
LANES = 128
PIECES = 3

noise_levels = (1.0, 0.6, 0.3)
obs_precision = 4.0
step_factor = 0.1


def sub_steps():
    steps = []
    for section in range(2):
        upper, lower = noise_levels[section], noise_levels[section + 1]
        spread = upper * upper - lower * lower
        steps.append((upper, spread, math.sqrt(spread)))
        factor = step_factor * lower * lower
        steps.append((lower, factor, math.sqrt(2.0 * factor)))
    return steps


STEPS = sub_steps()


def shrink(level):
    return 1.0 / math.sqrt(1.0 + level * level)


def vmem_call(kernel, outs, *args, scratch=(), scalars=0, hbm_in=0, hbm_out=False, flops=0):
    args = list(args)
    for i in range(scalars, len(args)):
        place = pltpu.HBM if i < scalars + hbm_in else pltpu.VMEM
        args[i] = pltpu.with_memory_space_constraint(args[i], place)
    smem = pl.BlockSpec(memory_space=pltpu.SMEM)
    vmem, hbm = pl.BlockSpec(memory_space=pltpu.VMEM), pl.BlockSpec(memory_space=pltpu.HBM)
    out_type = jax.ShapeDtypeStruct if hbm_out else pltpu.VMEM
    return pl.pallas_call(
        kernel,
        out_shape=[out_type(shape, dtype) for shape, dtype in outs],
        in_specs=[smem] * scalars + [hbm] * hbm_in + [vmem] * (len(args) - scalars - hbm_in),
        out_specs=[hbm if hbm_out else vmem] * len(outs),
        scratch_shapes=list(scratch),
        cost_estimate=pl.CostEstimate(flops=flops, bytes_accessed=0, transcendentals=0),
        compiler_params=pltpu.CompilerParams(vmem_limit_bytes=48 * 2**20),
    )(*args)


def dot(a, b, ca=1, cb=0):
    return lax.dot_general(a, b, (((ca,), (cb,)), ((), ())), preferred_element_type=F32)


def pieces(x, count):
    out = []
    for _ in range(count):
        part = x.astype(BF16)
        out.append(part)
        x = x - part.astype(F32)
    return out


def iota(shape, dim):
    return lax.broadcasted_iota(jnp.int32, shape, dim).astype(F32)


def silu_norm(values, gain):
    power = jnp.mean(values * values, axis=1, keepdims=True)
    half = values * (0.5 * lax.rsqrt(power + 1e-06)) * gain
    return half + half * jnp.tanh(half)


def row_order(latb):
    return [*range(1, latb - 1), 0, latb - 1]


def is_even(axis):
    return lax.rem(lax.axis_index(axis), 2) == 0


def start_all(pairs, sems):
    copies = [
        pltpu.make_async_copy(source, target, sems.at[i])
        for i, (source, target) in enumerate(pairs)
    ]
    for copy in copies:
        copy.start()
    return copies


def rows_of(source, target):
    return [(source.at[:, r, :], target.at[r]) for r in range(target.shape[0])]


def later_kernel(noise_in, *refs):
    half = (len(refs) - 2) // 2
    noise, sems = refs[half], refs[-1]
    pairs = []
    for k in range(noise.shape[0]):
        pairs += rows_of(noise_in.at[k], noise.at[k])
    pairs += list(zip(refs[:half], refs[half + 1 : -1]))
    for copy in start_all(pairs, sems):
        copy.wait()


def stage_kernel(*refs, slots):
    live, prior_in, entries_in = refs[0], refs[1], refs[2:7]
    prior, edge, entry_msg, *entries, sems = refs[7:]
    latb, _, lond = prior.shape
    copies = start_all(rows_of(prior_in, prior) + list(zip(entries_in, entries)), sems)
    for copy in copies[:latb]:
        copy.wait()
    edges_into(edge, prior, latb, STEPS[0][0])
    for copy in copies[latb:]:
        copy.wait()
    cell, owner, slot, weight, station = entries
    count = cell.shape[1]
    cells = cell[...]
    lon = cells % lond
    row = (cells // lond) % latb
    row = jnp.where(row == 0, latb - 2, jnp.where(row == latb - 1, row, row - 1))
    variable = cells // (lond * latb)
    rv = row * prior.shape[1] + variable
    key = owner[...] * slots + slot[...]
    alive = lax.broadcasted_iota(jnp.int32, (1, count), 1) < live[0]
    weights = jnp.where(alive, weight[...], 0.0)
    mine = lax.axis_index("band") * slots + lax.broadcasted_iota(jnp.int32, (1, count), 1)
    entry_msg[0:1] = key.astype(F32)
    entry_msg[1:2] = rv.astype(F32)
    entry_msg[2:3] = lon.astype(F32)
    entry_msg[3:4] = weights
    entry_msg[4:5] = station[...]
    entry_msg[5:6] = mine.astype(F32)
    entry_msg[6:8] = jnp.zeros((2, count), F32)
    columns = jnp.transpose(entry_msg[...])
    rv_col, lon_col = columns[:, 1:2], columns[:, 2:3]
    one_hot = jnp.where(rv_col == iota((count, latb * prior.shape[1]), 1), 1.0, 0.0).astype(BF16)
    current = jnp.concatenate([prior[r] for r in row_order(latb)], axis=0)
    picked = sum(dot(one_hot, part) for part in pieces(current, 2))
    at = jnp.sum(jnp.where(lon_col == iota((count, lond), 1), picked, 0.0), axis=1, keepdims=True)
    eye = iota((count, count), 0) == iota((count, count), 1)
    entry_msg[6:7] = weights * jnp.sum(jnp.where(eye, at, 0.0), axis=0, keepdims=True)


def edges_into(edge_ref, state, rows, level):
    lane = lax.broadcasted_iota(jnp.int32, (1, LANES), 1)
    variables, width = state.shape[1:]
    edge = jnp.zeros((variables, LANES), F32)
    for r in range(rows):
        slab = state[r]
        edge = jnp.where(lane == r, slab[:, 0:1], edge)
        edge = jnp.where(lane == rows + r, slab[:, width - 1 : width], edge)
    edge = (edge * shrink(level)).astype(BF16).astype(F32)
    edge_ref[...] = jnp.transpose(jnp.concatenate([edge] * (LANES // variables), axis=0))[0 : 2 * rows]


def from_sides(axis, from_a, from_b):
    even = is_even(axis)
    return jnp.where(even, from_b, from_a), jnp.where(even, from_a, from_b)


def message_kernel(state, edge_a, edge_b, value, *refs, level, used, first):
    msg = refs[-1]
    latb, variables, width = state.shape
    even = is_even("band")
    left, right = from_sides("wt", edge_a[...], edge_b[...])
    parts = [part.astype(F32) for part in pieces(value[0:used], PIECES)]
    padding = jnp.zeros((msg.shape[0] - variables - PIECES * used - 1, width), F32)
    below, above = [
        jnp.concatenate(
            [
                state[r] * shrink(level),
                *parts,
                jnp.concatenate([left[latb + r : latb + r + 1], right[r : r + 1]], axis=1),
                padding,
            ],
            axis=0,
        )
        for r in (0, latb - 1)
    ]
    upward = even if first else jnp.logical_not(even)
    msg[...] = jnp.where(upward, above, below).astype(BF16)


def unpacked(msg, variables, used):
    packed = msg[variables:].astype(F32)
    return sum(packed[used * i : used * (i + 1)] for i in range(PIECES))


def wide(column):
    return jnp.broadcast_to(column, (column.shape[0], LANES))


def one_hot(position, shape, dim):
    return jnp.where(position == iota(shape, dim), 1.0, 0.0).astype(BF16)


def own_kernel(msg, cols, pick, spread, *, variables, latb, lond):
    count = msg.shape[1]
    high = latb * variables
    col = jnp.transpose(msg[...])
    cols[0] = wide(col[:, 0:1])
    cols[1] = wide(col[:, 3:4])
    cols[2] = wide(col[:, 2:3])
    cols[3] = wide(col[:, 1:2] * lond + col[:, 2:3])
    cols[4] = wide(col[:, 5:6])
    pick[...] = one_hot(col[:, 1:2], (count, high), 1)
    spread[...] = one_hot(msg[1:2], (high, count), 0)


def tables_kernel(cols, own, msg_a, msg_b, *refs, variables):
    far, keys, seen = refs[:-2], refs[-2], refs[-1]
    count = own.shape[1]
    msgs = [own[...], *(unpacked(msg, variables, 8) for msg in (msg_a, msg_b))]
    msgs += [ref[...] for ref in far]
    for i, msg in enumerate(msgs):
        keys[:, i * count : (i + 1) * count] = msg
    acc = jnp.zeros((count, LANES), F32)
    for msg in msgs:
        for part in range(count // LANES):
            at = slice(part * LANES, (part + 1) * LANES)
            acc = acc + jnp.where(cols[0] == msg[5:6, at], msg[4:5, at], 0.0)
    seen[...] = wide(jnp.sum(acc, axis=1, keepdims=True))


def first_row(scaled, before, after, lift, gain):
    lifted = dot(scaled, lift[...], 0, 0)
    first = silu_norm(lifted, gain[...])
    width = first.shape[0]
    sub = lax.broadcasted_iota(jnp.int32, (width, 1), 0)
    shifted = [
        jnp.where(sub == 0, before, pltpu.roll(first, 1, 0)),
        first,
        jnp.where(sub == width - 1, after, pltpu.roll(first, width - 1, 0)),
    ]
    return lifted, [x.astype(BF16) for x in shifted]


def inner_kernel(
    state, edge_a, edge_b, noise, lift, conv, head, gain_1, gain_2,
    middle, sums, firsts, total, *, step,
):
    level, drift, kick = STEPS[step]
    latb, _, width = state.shape
    channels = lift.shape[1]
    variables = state.shape[1]
    left, right = from_sides("wt", edge_a[...], edge_b[...])
    edge = jnp.concatenate([left, right], axis=0)[:, 0:variables].astype(BF16)
    edge = silu_norm(dot(edge, lift[...]), gain_1[...])
    for r in range(latb):
        lifted, shifted = first_row(
            (state[r] * shrink(level)).astype(BF16),
            edge[latb + r : latb + r + 1], edge[2 * latb + r : 2 * latb + r + 1], lift, gain_1,
        )
        here = slice(r * width, (r + 1) * width)
        total[here] = lifted
        for q in range(3):
            firsts[here, q * channels : (q + 1) * channels] = shifted[q]
    deep = 3 * channels
    inside = (latb - 1) * width
    total[...] += dot(firsts[...], conv[deep : 2 * deep])
    total[width:] += dot(firsts[0:inside], conv[0:deep])
    total[0:inside] += dot(firsts[width:], conv[2 * deep :])
    sums[0] = total[0:width]
    sums[1] = total[inside:]
    for r in range(1, latb - 1):
        second = silu_norm(total[r * width : (r + 1) * width], gain_2[...]).astype(BF16)
        score = dot(head[...], second, 1, 1)
        middle[r - 1] = state[r] + (drift / level) * score + kick * noise[step, r]


def value_kernel(state, keys, cols, pick, value, parts):
    latb, variables, width = state.shape
    count = pick.shape[0]
    for i, r in enumerate(row_order(latb)):
        for j, part in enumerate(pieces(state[r], 2)):
            parts[i * variables : (i + 1) * variables, j * width : (j + 1) * width] = part
    picked = dot(pick[...], parts[...])
    picked = picked[:, 0:width] + picked[:, width:]
    lon = jnp.concatenate([cols[2]] * (width // LANES), axis=1)
    spots = jnp.where(lon == iota((count, width), 1), picked, 0.0)
    at = jnp.sum(spots, axis=1, keepdims=True)
    eye = iota((count, count), 0) == iota((count, count), 1)
    row = keys[3:4, 0:count] * jnp.sum(jnp.where(eye, at, 0.0), axis=0, keepdims=True)
    value[...] = jnp.broadcast_to(row, value.shape)


def matching(key, keys, values):
    count = values[0].shape[1]
    acc = jnp.zeros(key.shape, F32)
    for i, row in enumerate(values):
        for part in range(count // LANES):
            at = slice(part * LANES, (part + 1) * LANES)
            known = keys[0:1, i * count + part * LANES : i * count + (part + 1) * LANES]
            acc = acc + jnp.where(key == known, row[:, at], 0.0)
    return jnp.sum(acc, axis=1, keepdims=True)


def update_kernel(*refs, step, n_far, value_row, used):
    state, middle, sums, noise, lift, conv, head, gain_1, gain_2 = refs[:9]
    keys, cols, spread, seen, own, msg_a, msg_b = refs[9:16]
    far, rest = refs[16 : 16 + n_far], refs[16 + n_far :]
    level, drift, kick = STEPS[step]
    latb, variables, width = state.shape
    deep = 3 * lift.shape[1]
    count = own.shape[1]

    near = from_sides("band", msg_a[...].astype(F32), msg_b[...].astype(F32))
    spot = variables + PIECES * used
    corner = [side[spot : spot + 1, at : at + LANES] for side in near for at in (0, LANES)]
    corner = jnp.concatenate([*corner, jnp.zeros((12, LANES), F32)], axis=0)
    edge = silu_norm(dot(corner[:, 0:variables].astype(BF16), lift[...]), gain_1[...])

    here = slice(value_row, value_row + 1)
    values = [own[here], *(unpacked(msg, variables, used)[here] for msg in (msg_a, msg_b))]
    values += [ref[here] for ref in far]
    found = matching(cols[0], keys, values)
    mine = obs_precision * drift * cols[1] * (seen[...] - found)
    lon = jnp.concatenate([cols[2]] * (width // LANES), axis=1)
    tall = jnp.concatenate([mine] * (width // LANES), axis=1)
    spots = jnp.where(lon == iota((count, width), 1), tall, 0.0)
    both = dot(spread[...], jnp.concatenate(pieces(spots, 2), axis=1))
    added = both[:, 0:width] + both[:, width:]
    place = {r: slice(i * variables, (i + 1) * variables) for i, r in enumerate(row_order(latb))}
    moved = {r: middle[r - 1] + added[place[r]] for r in range(1, latb - 1)}

    band = lax.axis_index("band")
    beyond = (band == 0, band == lax.axis_size("band") - 1)
    for i, (r, p) in enumerate(((0, 0), (latb - 1, 2))):
        _, shifted = first_row(
            near[i][0:variables].astype(BF16),
            edge[2 * i : 2 * i + 1], edge[2 * i + 1 : 2 * i + 2], lift, gain_1,
        )
        first = jnp.where(beyond[i], 0.0, jnp.concatenate(shifted, axis=1).astype(F32)).astype(BF16)
        mixed = sums[i] + dot(first, conv[p * deep : (p + 1) * deep])
        second = silu_norm(mixed, gain_2[...]).astype(BF16)
        score = dot(head[...], second, 1, 1)
        moved[r] = state[r] + (drift / level) * score + kick * noise[step, r] + added[place[r]]

    if step < len(STEPS) - 1:
        after, border = rest
        for r in range(latb):
            after[r] = moved[r]
        edges_into(border, after, latb, STEPS[step + 1][0])
        return
    state_out, innov_out, after, innov, sems = rest
    found = matching(cols[4], keys, values)
    eye = iota((count, count), 0) == iota((count, count), 1)
    innov[...] = keys[4:5, 0:count] - jnp.sum(jnp.where(eye, found, 0.0), axis=0, keepdims=True)
    copies = [pltpu.make_async_copy(innov, innov_out, sems.at[latb])]
    copies[0].start()
    for r in row_order(latb):
        after[r] = moved[r]
        copies.append(pltpu.make_async_copy(after.at[r], state_out.at[:, r, :], sems.at[r]))
        copies[-1].start()
    for copy in copies:
        copy.wait()


def swaps(count):
    first = [(i, i ^ 1) for i in range(count)]
    other = [(i, (i - 1) % count if i % 2 == 0 else (i + 1) % count) for i in range(count)]
    return first, other


def from_neighbours(block, axis):
    return [lax.ppermute(block, axis, route) for route in swaps(lax.axis_size(axis))]


def from_far(block):
    count = lax.axis_size("band")
    reach = min(2 * REACH, count)
    found = []
    for distance in sorted({d % count for d in range(-reach, reach + 1)} - {0, 1, count - 1}):
        route = [(i, (i + distance) % count) for i in range(count)]
        found.append(lax.ppermute(block, "band", route))
    return found


def per_device(
    prior_state, langevin_noise, station_values, entry_cell, entry_owner, entry_slot,
    entry_weight, live_counts, lift_weight, conv_weight, head_weight, first_gain, second_gain,
):
    variables, latb, lond = prior_state.shape
    count = entry_cell.shape[0]
    slots = station_values.shape[0]
    channels = lift_weight.shape[1]
    taps = conv_weight.reshape(-1, channels)
    gain_1, gain_2 = first_gain.reshape(1, -1), second_gain.reshape(1, -1)

    def row(a):
        return a.reshape(1, -1)

    entries = [
        row(entry_cell), row(entry_owner), row(entry_slot), row(entry_weight), row(station_values),
    ]
    state, edge, value = vmem_call(
        functools.partial(stage_kernel, slots=slots),
        [((latb, variables, lond), F32), ((2 * latb, LANES), F32), ((8, count), F32)],
        live_counts, prior_state, *entries,
        scalars=1,
        hbm_in=1 + len(entries),
        scratch=[pltpu.VMEM(a.shape, a.dtype) for a in entries]
        + [pltpu.SemaphoreType.DMA((latb + len(entries),))],
    )
    weights = [taps, lift_weight, head_weight.T, gain_1, gain_2]
    noise, taps, *weights = vmem_call(
        later_kernel,
        [((len(STEPS), latb, variables, lond), F32)] + [(a.shape, a.dtype) for a in weights],
        langevin_noise, *weights,
        hbm_in=1 + len(weights),
        scratch=[pltpu.SemaphoreType.DMA((len(STEPS) * latb + len(weights),))],
    )
    weights = [weights[0], taps, *weights[1:]]
    high = latb * variables
    cols, pick, spread = vmem_call(
        functools.partial(own_kernel, variables=variables, latb=latb, lond=lond),
        [((5, count, LANES), F32), ((count, high), BF16), ((high, count), BF16)],
        value,
    )
    route_a, route_b = swaps(lax.axis_size("band"))
    whole = ((latb, variables, lond), F32)
    value_row, used = 6, 8
    for step in range(len(STEPS)):
        last = step == len(STEPS) - 1
        far = from_far(value)
        edges = from_neighbours(edge, "wt")
        message = [((variables + (32 if used == 8 else 16), lond), BF16)]
        make = functools.partial(message_kernel, level=STEPS[step][0], used=used)
        given = [state, *edges, value]
        (msg_b,) = vmem_call(functools.partial(make, first=False), message, *given)
        (msg_a,) = vmem_call(functools.partial(make, first=True), message, *given, msg_b)
        msg_a, msg_b = lax.ppermute(msg_a, "band", route_a), lax.ppermute(msg_b, "band", route_b)
        middle, sums = vmem_call(
            functools.partial(inner_kernel, step=step),
            [((latb - 2, variables, lond), F32), ((2, lond, channels), F32)],
            state, *edges, noise, *weights,
            scratch=[
                pltpu.VMEM((latb * lond, 3 * channels), BF16),
                pltpu.VMEM((latb * lond, channels), F32),
            ],
            flops=4 * latb * lond * taps.size,
        )
        if step == 0:
            keys, seen = vmem_call(
                functools.partial(tables_kernel, variables=variables),
                [((8, (3 + len(far)) * count), F32), ((count, LANES), F32)],
                cols, value, msg_a, msg_b, *far,
            )
        update = functools.partial(
            update_kernel, step=step, n_far=len(far), value_row=value_row, used=used
        )
        given = [state, middle, sums, noise, *weights]
        given += [keys, cols, spread, seen, value, msg_a, msg_b, *far]
        if last:
            state, innov = vmem_call(
                update, [((variables, latb, lond), F32), ((1, count), F32)], *given,
                hbm_out=True,
                scratch=[
                    pltpu.VMEM(*whole),
                    pltpu.VMEM((1, count), F32),
                    pltpu.SemaphoreType.DMA((latb + 1,)),
                ],
            )
            return state, innov.reshape(-1)
        state, edge = vmem_call(update, [whole, ((2 * latb, LANES), F32)], *given)
        (value,) = vmem_call(
            value_kernel, [((8, count), F32)], state, keys, cols, pick,
            scratch=[pltpu.VMEM((high, 2 * lond), BF16)],
        )
        value_row, used = 0, 1


def solution(mesh):
    split = P(("groups", "band", "wt"))
    in_specs = (
        P("groups", "band", "wt"),
        P(None, "groups", "band", "wt"),
        split, split, split, split, split, split,
        P(), P(), P(), P(), P(),
    )
    out_specs = (P("groups", "band", "wt"), split)
    return jax.shard_map(
        per_device, mesh=mesh, in_specs=in_specs, out_specs=out_specs, check_vma=False
    )
```

```python
import functools
import math

import jax
import jax.numpy as jnp
from jax import lax
from jax.experimental import pallas as pl
from jax.experimental.pallas import tpu as pltpu
from jax.sharding import PartitionSpec as P

F32 = jnp.float32
BF16 = jnp.bfloat16
REACH = 2
LANES = 128
PIECES = 3

noise_levels = (1.0, 0.6, 0.3)
obs_precision = 4.0
step_factor = 0.1


def sub_steps():
    steps = []
    for section in range(2):
        upper, lower = noise_levels[section], noise_levels[section + 1]
        spread = upper * upper - lower * lower
        steps.append((upper, spread, math.sqrt(spread)))
        factor = step_factor * lower * lower
        steps.append((lower, factor, math.sqrt(2.0 * factor)))
    return steps


STEPS = sub_steps()


def shrink(level):
    return 1.0 / math.sqrt(1.0 + level * level)


def vmem_call(kernel, outs, *args, scratch=(), scalars=0, hbm_in=0, hbm_out=False, flops=0):
    args = list(args)
    for i in range(scalars, len(args)):
        place = pltpu.HBM if i < scalars + hbm_in else pltpu.VMEM
        args[i] = pltpu.with_memory_space_constraint(args[i], place)
    smem = pl.BlockSpec(memory_space=pltpu.SMEM)
    vmem, hbm = pl.BlockSpec(memory_space=pltpu.VMEM), pl.BlockSpec(memory_space=pltpu.HBM)
    out_type = jax.ShapeDtypeStruct if hbm_out else pltpu.VMEM
    return pl.pallas_call(
        kernel,
        out_shape=[out_type(shape, dtype) for shape, dtype in outs],
        in_specs=[smem] * scalars + [hbm] * hbm_in + [vmem] * (len(args) - scalars - hbm_in),
        out_specs=[hbm if hbm_out else vmem] * len(outs),
        scratch_shapes=list(scratch),
        cost_estimate=pl.CostEstimate(flops=flops, bytes_accessed=0, transcendentals=0),
        compiler_params=pltpu.CompilerParams(vmem_limit_bytes=48 * 2**20),
    )(*args)


def dot(a, b, ca=1, cb=0):
    return lax.dot_general(a, b, (((ca,), (cb,)), ((), ())), preferred_element_type=F32)


def pieces(x, count):
    out = []
    for _ in range(count):
        part = x.astype(BF16)
        out.append(part)
        x = x - part.astype(F32)
    return out


def iota(shape, dim):
    return lax.broadcasted_iota(jnp.int32, shape, dim).astype(F32)


def silu_norm(values, gain):
    power = jnp.mean(values * values, axis=1, keepdims=True)
    half = values * (0.5 * lax.rsqrt(power + 1e-06)) * gain
    return half + half * jnp.tanh(half)


def row_order(latb):
    return [*range(1, latb - 1), 0, latb - 1]


def is_even(axis):
    return lax.rem(lax.axis_index(axis), 2) == 0


def start_all(pairs, sems):
    copies = [
        pltpu.make_async_copy(source, target, sems.at[i])
        for i, (source, target) in enumerate(pairs)
    ]
    for copy in copies:
        copy.start()
    return copies


def rows_of(source, target):
    return [(source.at[:, r, :], target.at[r]) for r in range(target.shape[0])]


def later_kernel(noise_in, *refs):
    half = (len(refs) - 3) // 2
    noise, sems = refs[half + 1], refs[-1]
    pairs = []
    for k in range(noise.shape[0]):
        pairs += rows_of(noise_in.at[k], noise.at[k])
    pairs += list(zip(refs[:half], refs[half + 2 : -1]))
    for copy in start_all(pairs, sems):
        copy.wait()


def stage_kernel(*refs, slots):
    live, prior_in, entries_in = refs[0], refs[1], refs[2:7]
    prior, edge, entry_msg, *entries, sems = refs[7:]
    latb, _, lond = prior.shape
    copies = start_all(rows_of(prior_in, prior) + list(zip(entries_in, entries)), sems)
    for copy in copies[:latb]:
        copy.wait()
    edges_into(edge, prior, latb, STEPS[0][0])
    for copy in copies[latb:]:
        copy.wait()
    cell, owner, slot, weight, station = entries
    count = cell.shape[1]
    cells = cell[...]
    lon = cells % lond
    row = (cells // lond) % latb
    row = jnp.where(row == 0, latb - 2, jnp.where(row == latb - 1, row, row - 1))
    variable = cells // (lond * latb)
    rv = row * prior.shape[1] + variable
    key = owner[...] * slots + slot[...]
    alive = lax.broadcasted_iota(jnp.int32, (1, count), 1) < live[0]
    weights = jnp.where(alive, weight[...], 0.0)
    mine = lax.axis_index("band") * slots + lax.broadcasted_iota(jnp.int32, (1, count), 1)
    entry_msg[0:1] = key.astype(F32)
    entry_msg[1:2] = rv.astype(F32)
    entry_msg[2:3] = lon.astype(F32)
    entry_msg[3:4] = weights
    entry_msg[4:5] = station[...]
    entry_msg[5:6] = mine.astype(F32)
    entry_msg[6:8] = jnp.zeros((2, count), F32)
    columns = jnp.transpose(entry_msg[...])
    rv_col, lon_col = columns[:, 1:2], columns[:, 2:3]
    one_hot = jnp.where(rv_col == iota((count, latb * prior.shape[1]), 1), 1.0, 0.0).astype(BF16)
    current = jnp.concatenate([prior[r] for r in row_order(latb)], axis=0)
    picked = sum(dot(one_hot, part) for part in pieces(current, 2))
    at = jnp.sum(jnp.where(lon_col == iota((count, lond), 1), picked, 0.0), axis=1, keepdims=True)
    eye = iota((count, count), 0) == iota((count, count), 1)
    entry_msg[6:7] = weights * jnp.sum(jnp.where(eye, at, 0.0), axis=0, keepdims=True)


def edges_into(edge_ref, state, rows, level):
    lane = lax.broadcasted_iota(jnp.int32, (1, LANES), 1)
    variables, width = state.shape[1:]
    edge = jnp.zeros((variables, LANES), F32)
    for r in range(rows):
        slab = state[r]
        edge = jnp.where(lane == r, slab[:, 0:1], edge)
        edge = jnp.where(lane == rows + r, slab[:, width - 1 : width], edge)
    edge = (edge * shrink(level)).astype(BF16).astype(F32)
    edge_ref[...] = jnp.transpose(jnp.concatenate([edge] * (LANES // variables), axis=0))[0 : 2 * rows]


def from_sides(axis, from_a, from_b):
    even = is_even(axis)
    return jnp.where(even, from_b, from_a), jnp.where(even, from_a, from_b)


def message_kernel(state, edge_a, edge_b, value, *refs, level, used, first):
    msg = refs[-1]
    latb, variables, width = state.shape
    even = is_even("band")
    left, right = from_sides("wt", edge_a[...], edge_b[...])
    parts = [part.astype(F32) for part in pieces(value[0:used], PIECES)]
    padding = jnp.zeros((msg.shape[0] - variables - PIECES * used - 1, width), F32)
    below, above = [
        jnp.concatenate(
            [
                state[r] * shrink(level),
                *parts,
                jnp.concatenate([left[latb + r : latb + r + 1], right[r : r + 1]], axis=1),
                padding,
            ],
            axis=0,
        )
        for r in (0, latb - 1)
    ]
    upward = even if first else jnp.logical_not(even)
    msg[...] = jnp.where(upward, above, below).astype(BF16)


def unpacked(msg, variables, used):
    packed = msg[variables:].astype(F32)
    return sum(packed[used * i : used * (i + 1)] for i in range(PIECES))


def wide(column):
    return jnp.broadcast_to(column, (column.shape[0], LANES))


def one_hot(position, shape, dim):
    return jnp.where(position == iota(shape, dim), 1.0, 0.0).astype(BF16)


def own_kernel(msg, after, cols, pick, spread, *, variables, latb, lond):
    count = msg.shape[1]
    high = latb * variables
    col = jnp.transpose(msg[...])
    cols[0] = wide(col[:, 0:1])
    cols[1] = wide(col[:, 3:4])
    cols[2] = wide(col[:, 2:3])
    cols[3] = wide(col[:, 1:2] * lond + col[:, 2:3])
    cols[4] = wide(col[:, 5:6])
    pick[...] = one_hot(col[:, 1:2], (count, high), 1)
    spread[...] = one_hot(msg[1:2], (high, count), 0)


def tables_kernel(cols, own, msg_a, msg_b, *refs, variables):
    far, keys, seen = refs[:-2], refs[-2], refs[-1]
    count = own.shape[1]
    msgs = [own[...], *(unpacked(msg, variables, 8) for msg in (msg_a, msg_b))]
    msgs += [ref[...] for ref in far]
    for i, msg in enumerate(msgs):
        keys[:, i * count : (i + 1) * count] = msg
    acc = jnp.zeros((count, LANES), F32)
    for msg in msgs:
        for part in range(count // LANES):
            at = slice(part * LANES, (part + 1) * LANES)
            acc = acc + jnp.where(cols[0] == msg[5:6, at], msg[4:5, at], 0.0)
    seen[...] = wide(jnp.sum(acc, axis=1, keepdims=True))


def first_row(scaled, before, after, lift, gain):
    lifted = dot(scaled, lift[...], 0, 0)
    first = silu_norm(lifted, gain[...])
    width = first.shape[0]
    sub = lax.broadcasted_iota(jnp.int32, (width, 1), 0)
    shifted = [
        jnp.where(sub == 0, before, pltpu.roll(first, 1, 0)),
        first,
        jnp.where(sub == width - 1, after, pltpu.roll(first, width - 1, 0)),
    ]
    return lifted, [x.astype(BF16) for x in shifted]


def inner_kernel(
    state, edge_a, edge_b, noise, lift, conv, head, gain_1, gain_2,
    middle, sums, firsts, total, *, step,
):
    level, drift, kick = STEPS[step]
    latb, _, width = state.shape
    channels = lift.shape[1]
    variables = state.shape[1]
    left, right = from_sides("wt", edge_a[...], edge_b[...])
    edge = jnp.concatenate([left, right], axis=0)[:, 0:variables].astype(BF16)
    edge = silu_norm(dot(edge, lift[...]), gain_1[...])
    for r in range(latb):
        lifted, shifted = first_row(
            (state[r] * shrink(level)).astype(BF16),
            edge[latb + r : latb + r + 1], edge[2 * latb + r : 2 * latb + r + 1], lift, gain_1,
        )
        here = slice(r * width, (r + 1) * width)
        total[here] = lifted
        for q in range(3):
            firsts[here, q * channels : (q + 1) * channels] = shifted[q]
    deep = 3 * channels
    inside = (latb - 1) * width
    total[...] += dot(firsts[...], conv[deep : 2 * deep])
    total[width:] += dot(firsts[0:inside], conv[0:deep])
    total[0:inside] += dot(firsts[width:], conv[2 * deep :])
    sums[0] = total[0:width]
    sums[1] = total[inside:]
    for r in range(1, latb - 1):
        second = silu_norm(total[r * width : (r + 1) * width], gain_2[...]).astype(BF16)
        score = dot(head[...], second, 1, 1)
        middle[r - 1] = state[r] + (drift / level) * score + kick * noise[step, r]


def value_kernel(state, keys, cols, pick, value, parts):
    latb, variables, width = state.shape
    count = pick.shape[0]
    for i, r in enumerate(row_order(latb)):
        for j, part in enumerate(pieces(state[r], 2)):
            parts[i * variables : (i + 1) * variables, j * width : (j + 1) * width] = part
    picked = dot(pick[...], parts[...])
    picked = picked[:, 0:width] + picked[:, width:]
    lon = jnp.concatenate([cols[2]] * (width // LANES), axis=1)
    spots = jnp.where(lon == iota((count, width), 1), picked, 0.0)
    at = jnp.sum(spots, axis=1, keepdims=True)
    eye = iota((count, count), 0) == iota((count, count), 1)
    row = keys[3:4, 0:count] * jnp.sum(jnp.where(eye, at, 0.0), axis=0, keepdims=True)
    value[...] = jnp.broadcast_to(row, value.shape)


def matching(key, keys, values):
    count = values[0].shape[1]
    acc = jnp.zeros(key.shape, F32)
    for i, row in enumerate(values):
        for part in range(count // LANES):
            at = slice(part * LANES, (part + 1) * LANES)
            known = keys[0:1, i * count + part * LANES : i * count + (part + 1) * LANES]
            acc = acc + jnp.where(key == known, row[:, at], 0.0)
    return jnp.sum(acc, axis=1, keepdims=True)


def update_kernel(*refs, step, n_far, value_row, used):
    state, middle, sums, noise, lift, conv, head, gain_1, gain_2 = refs[:9]
    keys, cols, spread, seen, own, msg_a, msg_b = refs[9:16]
    far, rest = refs[16 : 16 + n_far], refs[16 + n_far :]
    level, drift, kick = STEPS[step]
    latb, variables, width = state.shape
    deep = 3 * lift.shape[1]
    count = own.shape[1]

    near = from_sides("band", msg_a[...].astype(F32), msg_b[...].astype(F32))
    spot = variables + PIECES * used
    corner = [side[spot : spot + 1, at : at + LANES] for side in near for at in (0, LANES)]
    corner = jnp.concatenate([*corner, jnp.zeros((12, LANES), F32)], axis=0)
    edge = silu_norm(dot(corner[:, 0:variables].astype(BF16), lift[...]), gain_1[...])

    here = slice(value_row, value_row + 1)
    values = [own[here], *(unpacked(msg, variables, used)[here] for msg in (msg_a, msg_b))]
    values += [ref[here] for ref in far]
    found = matching(cols[0], keys, values)
    mine = obs_precision * drift * cols[1] * (seen[...] - found)
    lon = jnp.concatenate([cols[2]] * (width // LANES), axis=1)
    tall = jnp.concatenate([mine] * (width // LANES), axis=1)
    spots = jnp.where(lon == iota((count, width), 1), tall, 0.0)
    both = dot(spread[...], jnp.concatenate(pieces(spots, 2), axis=1))
    added = both[:, 0:width] + both[:, width:]
    place = {r: slice(i * variables, (i + 1) * variables) for i, r in enumerate(row_order(latb))}
    moved = {r: middle[r - 1] + added[place[r]] for r in range(1, latb - 1)}

    band = lax.axis_index("band")
    beyond = (band == 0, band == lax.axis_size("band") - 1)
    for i, (r, p) in enumerate(((0, 0), (latb - 1, 2))):
        _, shifted = first_row(
            near[i][0:variables].astype(BF16),
            edge[2 * i : 2 * i + 1], edge[2 * i + 1 : 2 * i + 2], lift, gain_1,
        )
        first = jnp.where(beyond[i], 0.0, jnp.concatenate(shifted, axis=1).astype(F32)).astype(BF16)
        mixed = sums[i] + dot(first, conv[p * deep : (p + 1) * deep])
        second = silu_norm(mixed, gain_2[...]).astype(BF16)
        score = dot(head[...], second, 1, 1)
        moved[r] = state[r] + (drift / level) * score + kick * noise[step, r] + added[place[r]]

    if step < len(STEPS) - 1:
        after, border = rest
        for r in range(latb):
            after[r] = moved[r]
        edges_into(border, after, latb, STEPS[step + 1][0])
        return
    state_out, innov_out, after, innov, sems = rest
    found = matching(cols[4], keys, values)
    eye = iota((count, count), 0) == iota((count, count), 1)
    innov[...] = keys[4:5, 0:count] - jnp.sum(jnp.where(eye, found, 0.0), axis=0, keepdims=True)
    copies = [pltpu.make_async_copy(innov, innov_out, sems.at[latb])]
    copies[0].start()
    for r in row_order(latb):
        after[r] = moved[r]
        copies.append(pltpu.make_async_copy(after.at[r], state_out.at[:, r, :], sems.at[r]))
        copies[-1].start()
    for copy in copies:
        copy.wait()


def swaps(count):
    first = [(i, i ^ 1) for i in range(count)]
    other = [(i, (i - 1) % count if i % 2 == 0 else (i + 1) % count) for i in range(count)]
    return first, other


def from_neighbours(block, axis):
    return [lax.ppermute(block, axis, route) for route in swaps(lax.axis_size(axis))]


def from_far(block):
    count = lax.axis_size("band")
    reach = min(2 * REACH, count)
    found = []
    for distance in sorted({d % count for d in range(-reach, reach + 1)} - {0, 1, count - 1}):
        route = [(i, (i + distance) % count) for i in range(count)]
        found.append(lax.ppermute(block, "band", route))
    return found


def per_device(
    prior_state, langevin_noise, station_values, entry_cell, entry_owner, entry_slot,
    entry_weight, live_counts, lift_weight, conv_weight, head_weight, first_gain, second_gain,
):
    variables, latb, lond = prior_state.shape
    count = entry_cell.shape[0]
    slots = station_values.shape[0]
    channels = lift_weight.shape[1]
    taps = conv_weight.reshape(-1, channels)
    gain_1, gain_2 = first_gain.reshape(1, -1), second_gain.reshape(1, -1)

    def row(a):
        return a.reshape(1, -1)

    entries = [
        row(entry_cell), row(entry_owner), row(entry_slot), row(entry_weight), row(station_values),
    ]
    state, edge, value = vmem_call(
        functools.partial(stage_kernel, slots=slots),
        [((latb, variables, lond), F32), ((2 * latb, LANES), F32), ((8, count), F32)],
        live_counts, prior_state, *entries,
        scalars=1,
        hbm_in=1 + len(entries),
        scratch=[pltpu.VMEM(a.shape, a.dtype) for a in entries]
        + [pltpu.SemaphoreType.DMA((latb + len(entries),))],
    )
    high = latb * variables
    route_a, route_b = swaps(lax.axis_size("band"))
    whole = ((latb, variables, lond), F32)
    value_row, used = 6, 8
    for step in range(len(STEPS)):
        last = step == len(STEPS) - 1
        far = from_far(value)
        edges = from_neighbours(edge, "wt")
        message = [((variables + (32 if used == 8 else 16), lond), BF16)]
        make = functools.partial(message_kernel, level=STEPS[step][0], used=used)
        given = [state, *edges, value]
        (msg_b,) = vmem_call(functools.partial(make, first=False), message, *given)
        (msg_a,) = vmem_call(functools.partial(make, first=True), message, *given, msg_b)
        if step == 0:
            weights = [taps, lift_weight, head_weight.T, gain_1, gain_2]
            noise, taps, *weights = vmem_call(
                later_kernel,
                [((len(STEPS), latb, variables, lond), F32)] + [(a.shape, a.dtype) for a in weights],
                langevin_noise, *weights, msg_a,
                hbm_in=1 + len(weights),
                scratch=[pltpu.SemaphoreType.DMA((len(STEPS) * latb + len(weights),))],
            )
            weights = [weights[0], taps, *weights[1:]]
            cols, pick, spread = vmem_call(
                functools.partial(own_kernel, variables=variables, latb=latb, lond=lond),
                [((5, count, LANES), F32), ((count, high), BF16), ((high, count), BF16)],
                value, msg_a,
            )
        msg_a, msg_b = lax.ppermute(msg_a, "band", route_a), lax.ppermute(msg_b, "band", route_b)
        middle, sums = vmem_call(
            functools.partial(inner_kernel, step=step),
            [((latb - 2, variables, lond), F32), ((2, lond, channels), F32)],
            state, *edges, noise, *weights,
            scratch=[
                pltpu.VMEM((latb * lond, 3 * channels), BF16),
                pltpu.VMEM((latb * lond, channels), F32),
            ],
            flops=4 * latb * lond * taps.size,
        )
        if step == 0:
            keys, seen = vmem_call(
                functools.partial(tables_kernel, variables=variables),
                [((8, (3 + len(far)) * count), F32), ((count, LANES), F32)],
                cols, value, msg_a, msg_b, *far,
            )
        update = functools.partial(
            update_kernel, step=step, n_far=len(far), value_row=value_row, used=used
        )
        given = [state, middle, sums, noise, *weights]
        given += [keys, cols, spread, seen, value, msg_a, msg_b, *far]
        if last:
            state, innov = vmem_call(
                update, [((variables, latb, lond), F32), ((1, count), F32)], *given,
                hbm_out=True,
                scratch=[
                    pltpu.VMEM(*whole),
                    pltpu.VMEM((1, count), F32),
                    pltpu.SemaphoreType.DMA((latb + 1,)),
                ],
            )
            return state, innov.reshape(-1)
        state, edge = vmem_call(update, [whole, ((2 * latb, LANES), F32)], *given)
        (value,) = vmem_call(
            value_kernel, [((8, count), F32)], state, keys, cols, pick,
            scratch=[pltpu.VMEM((high, 2 * lond), BF16)],
        )
        value_row, used = 0, 1


def solution(mesh):
    split = P(("groups", "band", "wt"))
    in_specs = (
        P("groups", "band", "wt"),
        P(None, "groups", "band", "wt"),
        split, split, split, split, split, split,
        P(), P(), P(), P(), P(),
    )
    out_specs = (P("groups", "band", "wt"), split)
    return jax.shard_map(
        per_device, mesh=mesh, in_specs=in_specs, out_specs=out_specs, check_vma=False
    )
```

```python
import functools
import math

import jax
import jax.numpy as jnp
from jax import lax
from jax.experimental import pallas as pl
from jax.experimental.pallas import tpu as pltpu
from jax.sharding import PartitionSpec as P

F32 = jnp.float32
BF16 = jnp.bfloat16
REACH = 2
LANES = 128
PIECES = 3

noise_levels = (1.0, 0.6, 0.3)
obs_precision = 4.0
step_factor = 0.1


def sub_steps():
    steps = []
    for section in range(2):
        upper, lower = noise_levels[section], noise_levels[section + 1]
        spread = upper * upper - lower * lower
        steps.append((upper, spread, math.sqrt(spread)))
        factor = step_factor * lower * lower
        steps.append((lower, factor, math.sqrt(2.0 * factor)))
    return steps


STEPS = sub_steps()


def shrink(level):
    return 1.0 / math.sqrt(1.0 + level * level)


def vmem_call(kernel, outs, *args, scratch=(), scalars=0, hbm_in=0, hbm_out=False, flops=0):
    args = list(args)
    for i in range(scalars, len(args)):
        place = pltpu.HBM if i < scalars + hbm_in else pltpu.VMEM
        args[i] = pltpu.with_memory_space_constraint(args[i], place)
    smem = pl.BlockSpec(memory_space=pltpu.SMEM)
    vmem, hbm = pl.BlockSpec(memory_space=pltpu.VMEM), pl.BlockSpec(memory_space=pltpu.HBM)
    out_type = jax.ShapeDtypeStruct if hbm_out else pltpu.VMEM
    return pl.pallas_call(
        kernel,
        out_shape=[out_type(shape, dtype) for shape, dtype in outs],
        in_specs=[smem] * scalars + [hbm] * hbm_in + [vmem] * (len(args) - scalars - hbm_in),
        out_specs=[hbm if hbm_out else vmem] * len(outs),
        scratch_shapes=list(scratch),
        cost_estimate=pl.CostEstimate(flops=flops, bytes_accessed=0, transcendentals=0),
        compiler_params=pltpu.CompilerParams(vmem_limit_bytes=48 * 2**20),
    )(*args)


def dot(a, b, ca=1, cb=0):
    return lax.dot_general(a, b, (((ca,), (cb,)), ((), ())), preferred_element_type=F32)


def pieces(x, count):
    out = []
    for _ in range(count):
        part = x.astype(BF16)
        out.append(part)
        x = x - part.astype(F32)
    return out


def iota(shape, dim):
    return lax.broadcasted_iota(jnp.int32, shape, dim).astype(F32)


def silu_norm(values, gain):
    power = jnp.mean(values * values, axis=1, keepdims=True)
    half = values * (0.5 * lax.rsqrt(power + 1e-06)) * gain
    return half + half * jnp.tanh(half)


def row_order(latb):
    return [*range(1, latb - 1), 0, latb - 1]


def is_even(axis):
    return lax.rem(lax.axis_index(axis), 2) == 0


def start_all(pairs, sems):
    copies = [
        pltpu.make_async_copy(source, target, sems.at[i])
        for i, (source, target) in enumerate(pairs)
    ]
    for copy in copies:
        copy.start()
    return copies


def rows_of(source, target):
    return [(source.at[:, r, :], target.at[r]) for r in range(target.shape[0])]


def later_kernel(noise_in, *refs):
    half = (len(refs) - 3) // 2
    noise, sems = refs[half + 1], refs[-1]
    pairs = []
    for k in range(noise.shape[0]):
        pairs += rows_of(noise_in.at[k], noise.at[k])
    pairs += list(zip(refs[:half], refs[half + 2 : -1]))
    for copy in start_all(pairs, sems):
        copy.wait()


def stage_kernel(*refs, slots):
    live, prior_in, entries_in = refs[0], refs[1], refs[2:7]
    prior, edge, entry_msg, *entries, sems = refs[7:]
    latb, _, lond = prior.shape
    copies = start_all(rows_of(prior_in, prior) + list(zip(entries_in, entries)), sems)
    for copy in copies[:latb]:
        copy.wait()
    edges_into(edge, prior, latb, STEPS[0][0])
    for copy in copies[latb:]:
        copy.wait()
    cell, owner, slot, weight, station = entries
    count = cell.shape[1]
    cells = cell[...]
    lon = cells % lond
    row = (cells // lond) % latb
    row = jnp.where(row == 0, latb - 2, jnp.where(row == latb - 1, row, row - 1))
    variable = cells // (lond * latb)
    rv = row * prior.shape[1] + variable
    key = owner[...] * slots + slot[...]
    alive = lax.broadcasted_iota(jnp.int32, (1, count), 1) < live[0]
    weights = jnp.where(alive, weight[...], 0.0)
    mine = lax.axis_index("band") * slots + lax.broadcasted_iota(jnp.int32, (1, count), 1)
    entry_msg[0:1] = key.astype(F32)
    entry_msg[1:2] = rv.astype(F32)
    entry_msg[2:3] = lon.astype(F32)
    entry_msg[3:4] = weights
    entry_msg[4:5] = station[...]
    entry_msg[5:6] = mine.astype(F32)
    entry_msg[6:8] = jnp.zeros((2, count), F32)
    columns = jnp.transpose(entry_msg[...])
    rv_col, lon_col = columns[:, 1:2], columns[:, 2:3]
    one_hot = jnp.where(rv_col == iota((count, latb * prior.shape[1]), 1), 1.0, 0.0).astype(BF16)
    current = jnp.concatenate([prior[r] for r in row_order(latb)], axis=0)
    picked = sum(dot(one_hot, part) for part in pieces(current, 2))
    at = jnp.sum(jnp.where(lon_col == iota((count, lond), 1), picked, 0.0), axis=1, keepdims=True)
    eye = iota((count, count), 0) == iota((count, count), 1)
    entry_msg[6:7] = weights * jnp.sum(jnp.where(eye, at, 0.0), axis=0, keepdims=True)


def edges_into(edge_ref, state, rows, level):
    lane = lax.broadcasted_iota(jnp.int32, (1, LANES), 1)
    variables, width = state.shape[1:]
    edge = jnp.zeros((variables, LANES), F32)
    for r in range(rows):
        slab = state[r]
        edge = jnp.where(lane == r, slab[:, 0:1], edge)
        edge = jnp.where(lane == rows + r, slab[:, width - 1 : width], edge)
    edge = (edge * shrink(level)).astype(BF16).astype(F32)
    edge_ref[...] = jnp.transpose(jnp.concatenate([edge] * (LANES // variables), axis=0))[0 : 2 * rows]


def from_sides(axis, from_a, from_b):
    even = is_even(axis)
    return jnp.where(even, from_b, from_a), jnp.where(even, from_a, from_b)


def message_kernel(state, edge_a, edge_b, value, *refs, level, used, first):
    msg = refs[-1]
    latb, variables, width = state.shape
    even = is_even("band")
    left, right = from_sides("wt", edge_a[...], edge_b[...])
    parts = [part.astype(F32) for part in pieces(value[0:used], PIECES)]
    padding = jnp.zeros((msg.shape[0] - variables - PIECES * used - 1, width), F32)
    below, above = [
        jnp.concatenate(
            [
                state[r] * shrink(level),
                *parts,
                jnp.concatenate([left[latb + r : latb + r + 1], right[r : r + 1]], axis=1),
                padding,
            ],
            axis=0,
        )
        for r in (0, latb - 1)
    ]
    upward = even if first else jnp.logical_not(even)
    msg[...] = jnp.where(upward, above, below).astype(BF16)


def unpacked(msg, variables, used):
    packed = msg[variables:].astype(F32)
    return sum(packed[used * i : used * (i + 1)] for i in range(PIECES))


def wide(column):
    return jnp.broadcast_to(column, (column.shape[0], LANES))


def one_hot(position, shape, dim):
    return jnp.where(position == iota(shape, dim), 1.0, 0.0).astype(BF16)


def own_kernel(msg, after, cols, pick, spread, *, variables, latb, lond):
    count = msg.shape[1]
    high = latb * variables
    col = jnp.transpose(msg[...])
    cols[0] = wide(col[:, 0:1])
    cols[1] = wide(col[:, 3:4])
    cols[2] = wide(col[:, 2:3])
    cols[3] = wide(col[:, 1:2] * lond + col[:, 2:3])
    cols[4] = wide(col[:, 5:6])
    pick[...] = one_hot(col[:, 1:2], (count, high), 1)
    spread[...] = one_hot(msg[1:2], (high, count), 0)


def tables_kernel(cols, own, msg_a, msg_b, *refs, variables):
    far, keys, seen = refs[:-2], refs[-2], refs[-1]
    count = own.shape[1]
    msgs = [own[...], *(unpacked(msg, variables, 8) for msg in (msg_a, msg_b))]
    msgs += [ref[...] for ref in far]
    for i, msg in enumerate(msgs):
        keys[:, i * count : (i + 1) * count] = msg
    acc = jnp.zeros((count, LANES), F32)
    for msg in msgs:
        for part in range(count // LANES):
            at = slice(part * LANES, (part + 1) * LANES)
            acc = acc + jnp.where(cols[0] == msg[5:6, at], msg[4:5, at], 0.0)
    seen[...] = wide(jnp.sum(acc, axis=1, keepdims=True))


def first_row(scaled, before, after, lift, gain):
    lifted = dot(scaled, lift[...], 0, 0)
    first = silu_norm(lifted, gain[...])
    width = first.shape[0]
    sub = lax.broadcasted_iota(jnp.int32, (width, 1), 0)
    shifted = [
        jnp.where(sub == 0, before, pltpu.roll(first, 1, 0)),
        first,
        jnp.where(sub == width - 1, after, pltpu.roll(first, width - 1, 0)),
    ]
    return lifted, [x.astype(BF16) for x in shifted]


def inner_kernel(
    state, edge_a, edge_b, noise, lift, conv, head, gain_1, gain_2,
    middle, sums, firsts, total, *, step,
):
    level, drift, kick = STEPS[step]
    latb, _, width = state.shape
    channels = lift.shape[1]
    variables = state.shape[1]
    left, right = from_sides("wt", edge_a[...], edge_b[...])
    edge = jnp.concatenate([left, right], axis=0)[:, 0:variables].astype(BF16)
    edge = silu_norm(dot(edge, lift[...]), gain_1[...])
    for r in range(latb):
        lifted, shifted = first_row(
            (state[r] * shrink(level)).astype(BF16),
            edge[latb + r : latb + r + 1], edge[2 * latb + r : 2 * latb + r + 1], lift, gain_1,
        )
        here = slice(r * width, (r + 1) * width)
        total[here] = lifted
        for q in range(3):
            firsts[here, q * channels : (q + 1) * channels] = shifted[q]
    deep = 3 * channels
    inside = (latb - 1) * width
    total[...] += dot(firsts[...], conv[deep : 2 * deep])
    total[width:] += dot(firsts[0:inside], conv[0:deep])
    total[0:inside] += dot(firsts[width:], conv[2 * deep :])
    sums[0] = total[0:width]
    sums[1] = total[inside:]
    for r in range(1, latb - 1):
        second = silu_norm(total[r * width : (r + 1) * width], gain_2[...]).astype(BF16)
        score = dot(head[...], second, 1, 1)
        middle[r - 1] = state[r] + (drift / level) * score + kick * noise[step, r]


def value_kernel(state, keys, cols, pick, value, parts):
    latb, variables, width = state.shape
    count = pick.shape[0]
    for i, r in enumerate(row_order(latb)):
        for j, part in enumerate(pieces(state[r], 2)):
            parts[i * variables : (i + 1) * variables, j * width : (j + 1) * width] = part
    picked = dot(pick[...], parts[...])
    picked = picked[:, 0:width] + picked[:, width:]
    lon = jnp.concatenate([cols[2]] * (width // LANES), axis=1)
    spots = jnp.where(lon == iota((count, width), 1), picked, 0.0)
    at = jnp.sum(spots, axis=1, keepdims=True)
    eye = iota((count, count), 0) == iota((count, count), 1)
    row = keys[3:4, 0:count] * jnp.sum(jnp.where(eye, at, 0.0), axis=0, keepdims=True)
    value[...] = jnp.broadcast_to(row, value.shape)


def matching(key, keys, values):
    count = values[0].shape[1]
    acc = jnp.zeros(key.shape, F32)
    for i, row in enumerate(values):
        for part in range(count // LANES):
            at = slice(part * LANES, (part + 1) * LANES)
            known = keys[0:1, i * count + part * LANES : i * count + (part + 1) * LANES]
            acc = acc + jnp.where(key == known, row[:, at], 0.0)
    return jnp.sum(acc, axis=1, keepdims=True)


def update_kernel(*refs, step, n_far, value_row, used):
    state, middle, sums, noise, lift, conv, head, gain_1, gain_2 = refs[:9]
    keys, cols, spread, seen, own, msg_a, msg_b = refs[9:16]
    far, rest = refs[16 : 16 + n_far], refs[16 + n_far :]
    level, drift, kick = STEPS[step]
    latb, variables, width = state.shape
    deep = 3 * lift.shape[1]
    count = own.shape[1]

    near = from_sides("band", msg_a[...].astype(F32), msg_b[...].astype(F32))
    spot = variables + PIECES * used
    corner = [side[spot : spot + 1, at : at + LANES] for side in near for at in (0, LANES)]
    corner = jnp.concatenate([*corner, jnp.zeros((12, LANES), F32)], axis=0)
    edge = silu_norm(dot(corner[:, 0:variables].astype(BF16), lift[...]), gain_1[...])

    here = slice(value_row, value_row + 1)
    values = [own[here], *(unpacked(msg, variables, used)[here] for msg in (msg_a, msg_b))]
    values += [ref[here] for ref in far]
    found = matching(cols[0], keys, values)
    mine = obs_precision * drift * cols[1] * (seen[...] - found)
    lon = jnp.concatenate([cols[2]] * (width // LANES), axis=1)
    tall = jnp.concatenate([mine] * (width // LANES), axis=1)
    spots = jnp.where(lon == iota((count, width), 1), tall, 0.0)
    both = dot(spread[...], jnp.concatenate(pieces(spots, 2), axis=1))
    added = both[:, 0:width] + both[:, width:]
    place = {r: slice(i * variables, (i + 1) * variables) for i, r in enumerate(row_order(latb))}
    moved = {r: middle[r - 1] + added[place[r]] for r in range(1, latb - 1)}

    band = lax.axis_index("band")
    beyond = (band == 0, band == lax.axis_size("band") - 1)
    for i, (r, p) in enumerate(((0, 0), (latb - 1, 2))):
        _, shifted = first_row(
            near[i][0:variables].astype(BF16),
            edge[2 * i : 2 * i + 1], edge[2 * i + 1 : 2 * i + 2], lift, gain_1,
        )
        first = jnp.where(beyond[i], 0.0, jnp.concatenate(shifted, axis=1).astype(F32)).astype(BF16)
        mixed = sums[i] + dot(first, conv[p * deep : (p + 1) * deep])
        second = silu_norm(mixed, gain_2[...]).astype(BF16)
        score = dot(head[...], second, 1, 1)
        moved[r] = state[r] + (drift / level) * score + kick * noise[step, r] + added[place[r]]

    if step < len(STEPS) - 1:
        after, border = rest
        for r in range(latb):
            after[r] = moved[r]
        edges_into(border, after, latb, STEPS[step + 1][0])
        return
    state_out, innov_out, after, innov, sems = rest
    found = matching(cols[4], keys, values)
    eye = iota((count, count), 0) == iota((count, count), 1)
    innov[...] = keys[4:5, 0:count] - jnp.sum(jnp.where(eye, found, 0.0), axis=0, keepdims=True)
    copies = [pltpu.make_async_copy(innov, innov_out, sems.at[latb])]
    copies[0].start()
    for r in row_order(latb):
        after[r] = moved[r]
        copies.append(pltpu.make_async_copy(after.at[r], state_out.at[:, r, :], sems.at[r]))
        copies[-1].start()
    for copy in copies:
        copy.wait()


def swaps(count):
    first = [(i, i ^ 1) for i in range(count)]
    other = [(i, (i - 1) % count if i % 2 == 0 else (i + 1) % count) for i in range(count)]
    return first, other


def from_neighbours(block, axis):
    return [lax.ppermute(block, axis, route) for route in swaps(lax.axis_size(axis))]


def from_far(block):
    count = lax.axis_size("band")
    reach = min(2 * REACH, count)
    found = []
    for distance in sorted({d % count for d in range(-reach, reach + 1)} - {0, 1, count - 1}):
        route = [(i, (i + distance) % count) for i in range(count)]
        found.append(lax.ppermute(block, "band", route))
    return found


def per_device(
    prior_state, langevin_noise, station_values, entry_cell, entry_owner, entry_slot,
    entry_weight, live_counts, lift_weight, conv_weight, head_weight, first_gain, second_gain,
):
    variables, latb, lond = prior_state.shape
    count = entry_cell.shape[0]
    slots = station_values.shape[0]
    channels = lift_weight.shape[1]
    taps = conv_weight.reshape(-1, channels)
    gain_1, gain_2 = first_gain.reshape(1, -1), second_gain.reshape(1, -1)

    def row(a):
        return a.reshape(1, -1)

    entries = [
        row(entry_cell), row(entry_owner), row(entry_slot), row(entry_weight), row(station_values),
    ]
    state, edge, value = vmem_call(
        functools.partial(stage_kernel, slots=slots),
        [((latb, variables, lond), F32), ((2 * latb, LANES), F32), ((8, count), F32)],
        live_counts, prior_state, *entries,
        scalars=1,
        hbm_in=1 + len(entries),
        scratch=[pltpu.VMEM(a.shape, a.dtype) for a in entries]
        + [pltpu.SemaphoreType.DMA((latb + len(entries),))],
    )
    high = latb * variables
    route_a, route_b = swaps(lax.axis_size("band"))
    whole = ((latb, variables, lond), F32)
    value_row, used = 6, 8
    for step in range(len(STEPS)):
        last = step == len(STEPS) - 1
        far = from_far(value)
        edges = from_neighbours(edge, "wt")
        message = [((variables + (32 if used == 8 else 16), lond), BF16)]
        make = functools.partial(message_kernel, level=STEPS[step][0], used=used)
        given = [state, *edges, value]
        (msg_b,) = vmem_call(functools.partial(make, first=False), message, *given)
        (msg_a,) = vmem_call(functools.partial(make, first=True), message, *given, msg_b)
        if step == 0:
            weights = [taps, lift_weight, head_weight.T, gain_1, gain_2]
            noise, taps, *weights = vmem_call(
                later_kernel,
                [((len(STEPS), latb, variables, lond), F32)] + [(a.shape, a.dtype) for a in weights],
                langevin_noise, *weights, msg_a,
                hbm_in=1 + len(weights),
                scratch=[pltpu.SemaphoreType.DMA((len(STEPS) * latb + len(weights),))],
            )
            weights = [weights[0], taps, *weights[1:]]
            cols, pick, spread = vmem_call(
                functools.partial(own_kernel, variables=variables, latb=latb, lond=lond),
                [((5, count, LANES), F32), ((count, high), BF16), ((high, count), BF16)],
                value, msg_a,
            )
        msg_a, msg_b = lax.ppermute(msg_a, "band", route_a), lax.ppermute(msg_b, "band", route_b)
        middle, sums = vmem_call(
            functools.partial(inner_kernel, step=step),
            [((latb - 2, variables, lond), F32), ((2, lond, channels), F32)],
            state, *edges, noise, *weights,
            scratch=[
                pltpu.VMEM((latb * lond, 3 * channels), BF16),
                pltpu.VMEM((latb * lond, channels), F32),
            ],
            flops=4 * latb * lond * taps.size,
        )
        if step == 0:
            keys, seen = vmem_call(
                functools.partial(tables_kernel, variables=variables),
                [((8, (3 + len(far)) * count), F32), ((count, LANES), F32)],
                cols, value, msg_a, msg_b, *far,
            )
        update = functools.partial(
            update_kernel, step=step, n_far=len(far), value_row=value_row, used=used
        )
        given = [state, middle, sums, noise, *weights]
        given += [keys, cols, spread, seen, value, msg_a, msg_b, *far]
        if last:
            state, innov = vmem_call(
                update, [((variables, latb, lond), F32), ((1, count), F32)], *given,
                hbm_out=True,
                scratch=[
                    pltpu.VMEM(*whole),
                    pltpu.VMEM((1, count), F32),
                    pltpu.SemaphoreType.DMA((latb + 1,)),
                ],
            )
            return state, innov.reshape(-1)
        state, edge = vmem_call(update, [whole, ((2 * latb, LANES), F32)], *given)
        (value,) = vmem_call(
            value_kernel, [((1, count), F32)], state, keys, cols, pick,
            scratch=[pltpu.VMEM((high, 2 * lond), BF16)],
        )
        value_row, used = 0, 1


def solution(mesh):
    split = P(("groups", "band", "wt"))
    in_specs = (
        P("groups", "band", "wt"),
        P(None, "groups", "band", "wt"),
        split, split, split, split, split, split,
        P(), P(), P(), P(), P(),
    )
    out_specs = (P("groups", "band", "wt"), split)
    return jax.shard_map(
        per_device, mesh=mesh, in_specs=in_specs, out_specs=out_specs, check_vma=False
    )
```

```python
import functools
import math

import jax
import jax.numpy as jnp
from jax import lax
from jax.experimental import pallas as pl
from jax.experimental.pallas import tpu as pltpu
from jax.sharding import PartitionSpec as P

F32 = jnp.float32
BF16 = jnp.bfloat16
REACH = 2
LANES = 128
PIECES = 3

noise_levels = (1.0, 0.6, 0.3)
obs_precision = 4.0
step_factor = 0.1


def sub_steps():
    steps = []
    for section in range(2):
        upper, lower = noise_levels[section], noise_levels[section + 1]
        spread = upper * upper - lower * lower
        steps.append((upper, spread, math.sqrt(spread)))
        factor = step_factor * lower * lower
        steps.append((lower, factor, math.sqrt(2.0 * factor)))
    return steps


STEPS = sub_steps()


def shrink(level):
    return 1.0 / math.sqrt(1.0 + level * level)


def vmem_call(kernel, outs, *args, scratch=(), scalars=0, hbm_in=0, hbm_out=False, flops=0):
    args = list(args)
    for i in range(scalars, len(args)):
        place = pltpu.HBM if i < scalars + hbm_in else pltpu.VMEM
        args[i] = pltpu.with_memory_space_constraint(args[i], place)
    smem = pl.BlockSpec(memory_space=pltpu.SMEM)
    vmem, hbm = pl.BlockSpec(memory_space=pltpu.VMEM), pl.BlockSpec(memory_space=pltpu.HBM)
    out_type = jax.ShapeDtypeStruct if hbm_out else pltpu.VMEM
    return pl.pallas_call(
        kernel,
        out_shape=[out_type(shape, dtype) for shape, dtype in outs],
        in_specs=[smem] * scalars + [hbm] * hbm_in + [vmem] * (len(args) - scalars - hbm_in),
        out_specs=[hbm if hbm_out else vmem] * len(outs),
        scratch_shapes=list(scratch),
        cost_estimate=pl.CostEstimate(flops=flops, bytes_accessed=0, transcendentals=0),
        compiler_params=pltpu.CompilerParams(vmem_limit_bytes=48 * 2**20),
    )(*args)


def dot(a, b, ca=1, cb=0):
    return lax.dot_general(a, b, (((ca,), (cb,)), ((), ())), preferred_element_type=F32)


def pieces(x, count):
    out = []
    for _ in range(count):
        part = x.astype(BF16)
        out.append(part)
        x = x - part.astype(F32)
    return out


def iota(shape, dim):
    return lax.broadcasted_iota(jnp.int32, shape, dim).astype(F32)


def silu_norm(values, gain):
    power = jnp.mean(values * values, axis=1, keepdims=True)
    half = values * (0.5 * lax.rsqrt(power + 1e-06)) * gain
    return half + half * jnp.tanh(half)


def row_order(latb):
    return [*range(1, latb - 1), 0, latb - 1]


def is_even(axis):
    return lax.rem(lax.axis_index(axis), 2) == 0


def start_all(pairs, sems):
    copies = [
        pltpu.make_async_copy(source, target, sems.at[i])
        for i, (source, target) in enumerate(pairs)
    ]
    for copy in copies:
        copy.start()
    return copies


def rows_of(source, target):
    return [(source.at[:, r, :], target.at[r]) for r in range(target.shape[0])]


def later_kernel(noise_in, *refs):
    half = (len(refs) - 3) // 2
    noise, sems = refs[half + 1], refs[-1]
    pairs = []
    for k in range(noise.shape[0]):
        pairs += rows_of(noise_in.at[k], noise.at[k])
    pairs += list(zip(refs[:half], refs[half + 2 : -1]))
    for copy in start_all(pairs, sems):
        copy.wait()


def stage_kernel(*refs, slots):
    live, prior_in, entries_in = refs[0], refs[1], refs[2:7]
    prior, edge, entry_msg, *entries, sems = refs[7:]
    latb, _, lond = prior.shape
    copies = start_all(rows_of(prior_in, prior) + list(zip(entries_in, entries)), sems)
    for copy in copies[:latb]:
        copy.wait()
    edges_into(edge, prior, latb, STEPS[0][0])
    for copy in copies[latb:]:
        copy.wait()
    cell, owner, slot, weight, station = entries
    count = cell.shape[1]
    cells = cell[...]
    lon = cells % lond
    row = (cells // lond) % latb
    row = jnp.where(row == 0, latb - 2, jnp.where(row == latb - 1, row, row - 1))
    variable = cells // (lond * latb)
    rv = row * prior.shape[1] + variable
    key = owner[...] * slots + slot[...]
    alive = lax.broadcasted_iota(jnp.int32, (1, count), 1) < live[0]
    weights = jnp.where(alive, weight[...], 0.0)
    mine = lax.axis_index("band") * slots + lax.broadcasted_iota(jnp.int32, (1, count), 1)
    entry_msg[0:1] = key.astype(F32)
    entry_msg[1:2] = rv.astype(F32)
    entry_msg[2:3] = lon.astype(F32)
    entry_msg[3:4] = weights
    entry_msg[4:5] = station[...]
    entry_msg[5:6] = mine.astype(F32)
    entry_msg[6:8] = jnp.zeros((2, count), F32)
    columns = jnp.transpose(entry_msg[...])
    rv_col, lon_col = columns[:, 1:2], columns[:, 2:3]
    one_hot = jnp.where(rv_col == iota((count, latb * prior.shape[1]), 1), 1.0, 0.0).astype(BF16)
    current = jnp.concatenate([prior[r] for r in row_order(latb)], axis=0)
    picked = sum(dot(one_hot, part) for part in pieces(current, 2))
    at = jnp.sum(jnp.where(lon_col == iota((count, lond), 1), picked, 0.0), axis=1, keepdims=True)
    eye = iota((count, count), 0) == iota((count, count), 1)
    entry_msg[6:7] = weights * jnp.sum(jnp.where(eye, at, 0.0), axis=0, keepdims=True)


def edges_into(edge_ref, state, rows, level):
    lane = lax.broadcasted_iota(jnp.int32, (1, LANES), 1)
    variables, width = state.shape[1:]
    edge = jnp.zeros((variables, LANES), F32)
    for r in range(rows):
        slab = state[r]
        edge = jnp.where(lane == r, slab[:, 0:1], edge)
        edge = jnp.where(lane == rows + r, slab[:, width - 1 : width], edge)
    edge = (edge * shrink(level)).astype(BF16).astype(F32)
    edge_ref[...] = jnp.transpose(jnp.concatenate([edge] * (LANES // variables), axis=0))[0 : 2 * rows]


def from_sides(axis, from_a, from_b):
    even = is_even(axis)
    return jnp.where(even, from_b, from_a), jnp.where(even, from_a, from_b)


def message_kernel(state, edge_a, edge_b, value, *refs, level, used, first):
    msg = refs[-1]
    latb, variables, width = state.shape
    even = is_even("band")
    left, right = from_sides("wt", edge_a[...], edge_b[...])
    parts = [part.astype(F32) for part in pieces(value[0:used], PIECES)]
    padding = jnp.zeros((msg.shape[0] - variables - PIECES * used - 1, width), F32)
    below, above = [
        jnp.concatenate(
            [
                state[r] * shrink(level),
                *parts,
                jnp.concatenate([left[latb + r : latb + r + 1], right[r : r + 1]], axis=1),
                padding,
            ],
            axis=0,
        )
        for r in (0, latb - 1)
    ]
    upward = even if first else jnp.logical_not(even)
    msg[...] = jnp.where(upward, above, below).astype(BF16)


def unpacked(msg, variables, used):
    packed = msg[variables:].astype(F32)
    return sum(packed[used * i : used * (i + 1)] for i in range(PIECES))


def wide(column):
    return jnp.broadcast_to(column, (column.shape[0], LANES))


def one_hot(position, shape, dim):
    return jnp.where(position == iota(shape, dim), 1.0, 0.0).astype(BF16)


def own_kernel(msg, after, cols, pick, spread, *, variables, latb, lond):
    count = msg.shape[1]
    high = latb * variables
    col = jnp.transpose(msg[...])
    cols[0] = wide(col[:, 0:1])
    cols[1] = wide(col[:, 3:4])
    cols[2] = wide(col[:, 2:3])
    cols[3] = wide(col[:, 1:2] * lond + col[:, 2:3])
    cols[4] = wide(col[:, 5:6])
    pick[...] = one_hot(col[:, 1:2], (count, high), 1)
    spread[...] = one_hot(msg[1:2], (high, count), 0)


def tables_kernel(cols, own, msg_a, msg_b, *refs, variables):
    far, keys, seen = refs[:-2], refs[-2], refs[-1]
    count = own.shape[1]
    msgs = [own[...], *(unpacked(msg, variables, 8) for msg in (msg_a, msg_b))]
    msgs += [ref[...] for ref in far]
    for i, msg in enumerate(msgs):
        keys[:, i * count : (i + 1) * count] = msg
    acc = jnp.zeros((count, LANES), F32)
    for msg in msgs:
        for part in range(count // LANES):
            at = slice(part * LANES, (part + 1) * LANES)
            acc = acc + jnp.where(cols[0] == msg[5:6, at], msg[4:5, at], 0.0)
    seen[...] = wide(jnp.sum(acc, axis=1, keepdims=True))


def first_row(scaled, before, after, lift, gain):
    lifted = dot(scaled, lift[...], 0, 0)
    first = silu_norm(lifted, gain[...])
    width = first.shape[0]
    sub = lax.broadcasted_iota(jnp.int32, (width, 1), 0)
    shifted = [
        jnp.where(sub == 0, before, pltpu.roll(first, 1, 0)),
        first,
        jnp.where(sub == width - 1, after, pltpu.roll(first, width - 1, 0)),
    ]
    return lifted, [x.astype(BF16) for x in shifted]


def inner_kernel(
    state, edge_a, edge_b, noise, lift, conv, head, gain_1, gain_2,
    middle, sums, firsts, total, *, step,
):
    level, drift, kick = STEPS[step]
    latb, _, width = state.shape
    channels = lift.shape[1]
    variables = state.shape[1]
    left, right = from_sides("wt", edge_a[...], edge_b[...])
    edge = jnp.concatenate([left, right], axis=0)[:, 0:variables].astype(BF16)
    edge = silu_norm(dot(edge, lift[...]), gain_1[...])
    for r in range(latb):
        lifted, shifted = first_row(
            (state[r] * shrink(level)).astype(BF16),
            edge[latb + r : latb + r + 1], edge[2 * latb + r : 2 * latb + r + 1], lift, gain_1,
        )
        here = slice(r * width, (r + 1) * width)
        total[here] = lifted
        for q in range(3):
            firsts[here, q * channels : (q + 1) * channels] = shifted[q]
    deep = 3 * channels
    inside = (latb - 1) * width
    total[...] += dot(firsts[...], conv[deep : 2 * deep])
    total[width:] += dot(firsts[0:inside], conv[0:deep])
    total[0:inside] += dot(firsts[width:], conv[2 * deep :])
    sums[0] = total[0:width]
    sums[1] = total[inside:]
    for r in range(1, latb - 1):
        second = silu_norm(total[r * width : (r + 1) * width], gain_2[...]).astype(BF16)
        score = dot(head[...], second, 1, 1)
        middle[r - 1] = state[r] + (drift / level) * score + kick * noise[step, r]


def value_kernel(state, keys, cols, pick, value, parts):
    latb, variables, width = state.shape
    count = pick.shape[0]
    for i, r in enumerate(row_order(latb)):
        for j, part in enumerate(pieces(state[r], 2)):
            parts[i * variables : (i + 1) * variables, j * width : (j + 1) * width] = part
    picked = dot(pick[...], parts[...])
    picked = picked[:, 0:width] + picked[:, width:]
    lon = jnp.concatenate([cols[2]] * (width // LANES), axis=1)
    spots = jnp.where(lon == iota((count, width), 1), picked, 0.0)
    at = jnp.sum(spots, axis=1, keepdims=True)
    eye = iota((count, count), 0) == iota((count, count), 1)
    row = keys[3:4, 0:count] * jnp.sum(jnp.where(eye, at, 0.0), axis=0, keepdims=True)
    value[...] = jnp.broadcast_to(row, value.shape)


def matching(key, keys, values):
    count = values[0].shape[1]
    acc = jnp.zeros(key.shape, F32)
    for i, row in enumerate(values):
        for part in range(count // LANES):
            at = slice(part * LANES, (part + 1) * LANES)
            known = keys[0:1, i * count + part * LANES : i * count + (part + 1) * LANES]
            acc = acc + jnp.where(key == known, row[:, at], 0.0)
    return jnp.sum(acc, axis=1, keepdims=True)


def update_kernel(*refs, step, n_far, value_row, used):
    state, middle, sums, noise, lift, conv, head, gain_1, gain_2 = refs[:9]
    keys, cols, spread, seen, own, msg_a, msg_b = refs[9:16]
    far, rest = refs[16 : 16 + n_far], refs[16 + n_far :]
    level, drift, kick = STEPS[step]
    latb, variables, width = state.shape
    deep = 3 * lift.shape[1]
    count = own.shape[1]

    near = from_sides("band", msg_a[...].astype(F32), msg_b[...].astype(F32))
    spot = variables + PIECES * used
    corner = [side[spot : spot + 1, at : at + LANES] for side in near for at in (0, LANES)]
    corner = jnp.concatenate([*corner, jnp.zeros((12, LANES), F32)], axis=0)
    edge = silu_norm(dot(corner[:, 0:variables].astype(BF16), lift[...]), gain_1[...])

    here = slice(value_row, value_row + 1)
    values = [own[here], *(unpacked(msg, variables, used)[here] for msg in (msg_a, msg_b))]
    values += [ref[here] for ref in far]
    found = matching(cols[0], keys, values)
    mine = obs_precision * drift * cols[1] * (seen[...] - found)
    lon = jnp.concatenate([cols[2]] * (width // LANES), axis=1)
    tall = jnp.concatenate([mine] * (width // LANES), axis=1)
    spots = jnp.where(lon == iota((count, width), 1), tall, 0.0)
    both = dot(spread[...], jnp.concatenate(pieces(spots, 2), axis=1))
    added = both[:, 0:width] + both[:, width:]
    place = {r: slice(i * variables, (i + 1) * variables) for i, r in enumerate(row_order(latb))}
    moved = {r: middle[r - 1] + added[place[r]] for r in range(1, latb - 1)}

    band = lax.axis_index("band")
    beyond = (band == 0, band == lax.axis_size("band") - 1)
    for i, (r, p) in enumerate(((0, 0), (latb - 1, 2))):
        _, shifted = first_row(
            near[i][0:variables].astype(BF16),
            edge[2 * i : 2 * i + 1], edge[2 * i + 1 : 2 * i + 2], lift, gain_1,
        )
        share = dot(jnp.concatenate(shifted, axis=1), conv[p * deep : (p + 1) * deep])
        mixed = sums[i] + jnp.where(beyond[i], 0.0, share)
        second = silu_norm(mixed, gain_2[...]).astype(BF16)
        score = dot(head[...], second, 1, 1)
        moved[r] = state[r] + (drift / level) * score + kick * noise[step, r] + added[place[r]]

    if step < len(STEPS) - 1:
        after, border = rest
        for r in range(latb):
            after[r] = moved[r]
        edges_into(border, after, latb, STEPS[step + 1][0])
        return
    state_out, innov_out, after, innov, sems = rest
    found = matching(cols[4], keys, values)
    eye = iota((count, count), 0) == iota((count, count), 1)
    innov[...] = keys[4:5, 0:count] - jnp.sum(jnp.where(eye, found, 0.0), axis=0, keepdims=True)
    copies = [pltpu.make_async_copy(innov, innov_out, sems.at[latb])]
    copies[0].start()
    for r in row_order(latb):
        after[r] = moved[r]
        copies.append(pltpu.make_async_copy(after.at[r], state_out.at[:, r, :], sems.at[r]))
        copies[-1].start()
    for copy in copies:
        copy.wait()


def swaps(count):
    first = [(i, i ^ 1) for i in range(count)]
    other = [(i, (i - 1) % count if i % 2 == 0 else (i + 1) % count) for i in range(count)]
    return first, other


def from_neighbours(block, axis):
    return [lax.ppermute(block, axis, route) for route in swaps(lax.axis_size(axis))]


def from_far(block):
    count = lax.axis_size("band")
    reach = min(2 * REACH, count)
    found = []
    for distance in sorted({d % count for d in range(-reach, reach + 1)} - {0, 1, count - 1}):
        route = [(i, (i + distance) % count) for i in range(count)]
        found.append(lax.ppermute(block, "band", route))
    return found


def per_device(
    prior_state, langevin_noise, station_values, entry_cell, entry_owner, entry_slot,
    entry_weight, live_counts, lift_weight, conv_weight, head_weight, first_gain, second_gain,
):
    variables, latb, lond = prior_state.shape
    count = entry_cell.shape[0]
    slots = station_values.shape[0]
    channels = lift_weight.shape[1]
    taps = conv_weight.reshape(-1, channels)
    gain_1, gain_2 = first_gain.reshape(1, -1), second_gain.reshape(1, -1)

    def row(a):
        return a.reshape(1, -1)

    entries = [
        row(entry_cell), row(entry_owner), row(entry_slot), row(entry_weight), row(station_values),
    ]
    state, edge, value = vmem_call(
        functools.partial(stage_kernel, slots=slots),
        [((latb, variables, lond), F32), ((2 * latb, LANES), F32), ((8, count), F32)],
        live_counts, prior_state, *entries,
        scalars=1,
        hbm_in=1 + len(entries),
        scratch=[pltpu.VMEM(a.shape, a.dtype) for a in entries]
        + [pltpu.SemaphoreType.DMA((latb + len(entries),))],
    )
    high = latb * variables
    route_a, route_b = swaps(lax.axis_size("band"))
    whole = ((latb, variables, lond), F32)
    value_row, used = 6, 8
    for step in range(len(STEPS)):
        last = step == len(STEPS) - 1
        far = from_far(value)
        edges = from_neighbours(edge, "wt")
        message = [((variables + (32 if used == 8 else 16), lond), BF16)]
        make = functools.partial(message_kernel, level=STEPS[step][0], used=used)
        given = [state, *edges, value]
        (msg_b,) = vmem_call(functools.partial(make, first=False), message, *given)
        (msg_a,) = vmem_call(functools.partial(make, first=True), message, *given, msg_b)
        if step == 0:
            weights = [taps, lift_weight, head_weight.T, gain_1, gain_2]
            noise, taps, *weights = vmem_call(
                later_kernel,
                [((len(STEPS), latb, variables, lond), F32)] + [(a.shape, a.dtype) for a in weights],
                langevin_noise, *weights, msg_a,
                hbm_in=1 + len(weights),
                scratch=[pltpu.SemaphoreType.DMA((len(STEPS) * latb + len(weights),))],
            )
            weights = [weights[0], taps, *weights[1:]]
            cols, pick, spread = vmem_call(
                functools.partial(own_kernel, variables=variables, latb=latb, lond=lond),
                [((5, count, LANES), F32), ((count, high), BF16), ((high, count), BF16)],
                value, msg_a,
            )
        msg_a, msg_b = lax.ppermute(msg_a, "band", route_a), lax.ppermute(msg_b, "band", route_b)
        middle, sums = vmem_call(
            functools.partial(inner_kernel, step=step),
            [((latb - 2, variables, lond), F32), ((2, lond, channels), F32)],
            state, *edges, noise, *weights,
            scratch=[
                pltpu.VMEM((latb * lond, 3 * channels), BF16),
                pltpu.VMEM((latb * lond, channels), F32),
            ],
            flops=4 * latb * lond * taps.size,
        )
        if step == 0:
            keys, seen = vmem_call(
                functools.partial(tables_kernel, variables=variables),
                [((8, (3 + len(far)) * count), F32), ((count, LANES), F32)],
                cols, value, msg_a, msg_b, *far,
            )
        update = functools.partial(
            update_kernel, step=step, n_far=len(far), value_row=value_row, used=used
        )
        given = [state, middle, sums, noise, *weights]
        given += [keys, cols, spread, seen, value, msg_a, msg_b, *far]
        if last:
            state, innov = vmem_call(
                update, [((variables, latb, lond), F32), ((1, count), F32)], *given,
                hbm_out=True,
                scratch=[
                    pltpu.VMEM(*whole),
                    pltpu.VMEM((1, count), F32),
                    pltpu.SemaphoreType.DMA((latb + 1,)),
                ],
            )
            return state, innov.reshape(-1)
        state, edge = vmem_call(update, [whole, ((2 * latb, LANES), F32)], *given)
        (value,) = vmem_call(
            value_kernel, [((8, count), F32)], state, keys, cols, pick,
            scratch=[pltpu.VMEM((high, 2 * lond), BF16)],
        )
        value_row, used = 0, 1


def solution(mesh):
    split = P(("groups", "band", "wt"))
    in_specs = (
        P("groups", "band", "wt"),
        P(None, "groups", "band", "wt"),
        split, split, split, split, split, split,
        P(), P(), P(), P(), P(),
    )
    out_specs = (P("groups", "band", "wt"), split)
    return jax.shard_map(
        per_device, mesh=mesh, in_specs=in_specs, out_specs=out_specs, check_vma=False
    )
```
